128 devices in a mesh: row: 8 (over y, x_hi), col: 16 (over x_lo, z, core).
Axes of the slice: x: 4 (x_hi: 2, x_lo: 2; x = x_hi * 2 + x_lo), y: 4, z: 4, core: 2. Of those that a mesh axis runs over, the one named last changes fastest.
Arguments:
- view_a: float32 [2048, 16384], P('col', 'row'), may hold values from -200 to 200
- view_b: float32 [2048, 16384], P('row', 'col'), may hold values from -200 to 200
Outputs:
- loss_value: float32 [], replicated
- grad_a: float32 [2048, 16384], P('col', 'row')
- grad_b: float32 [2048, 16384], P('row', 'col')
The draws below stay inside these ranges and needn't reach their ends.
All inputs are finite; a program needn't handle non-finite values.
Results may differ from the reference program's by a relative error of at most 0.0038.
Values may be sent and summed in bfloat16 or wider, within the bound.
No kernel may reach another device: no remote copies, remote signals or barrier semaphores. Data moves between devices by JAX's collectives and lax.ppermute only.
A program may use at most 192 MiB of HBM per device.

```python
import math
import jax
import jax.numpy as jnp
from jax import lax

FEAT = 16384
BATCH = 2048


def shared_parts(key):
    first, second, third = jax.random.split(key, 3)
    gauss = jnp.clip(jax.random.normal(first, (BATCH, FEAT), jnp.float32), -4.0, 4.0)
    common = gauss
    row_scale = jnp.exp(jax.random.uniform(second, (BATCH, 1), jnp.float32, math.log(0.3), math.log(3.0)))
    linked = jax.random.uniform(third, (1, FEAT), jnp.float32, 0.5, 0.9)
    return (common, row_scale, linked)


def draw_view_a(key, part):
    reach = 1.0
    common, row_scale, linked = shared_parts(key)
    key = jax.random.fold_in(key, 11)
    first, second = jax.random.split(key, 2)
    scale = jnp.exp(jax.random.uniform(first, (1, FEAT), jnp.float32, 0.0, math.log(10.0)))
    shift = jax.random.uniform(second, (1, FEAT), jnp.float32, -reach, reach) * scale
    return row_scale * scale * common + shift


def draw_view_b(key, part):
    reach = 1.0
    common, row_scale, linked = shared_parts(key)
    key = jax.random.fold_in(key, 12)
    first, second, third = jax.random.split(key, 3)
    gauss = jnp.clip(jax.random.normal(first, (BATCH, FEAT), jnp.float32), -4.0, 4.0)
    noise = gauss
    scale = jnp.exp(jax.random.uniform(second, (1, FEAT), jnp.float32, 0.0, math.log(10.0)))
    shift = jax.random.uniform(third, (1, FEAT), jnp.float32, -reach, reach) * scale
    mixed = linked * common + jnp.sqrt(1.0 - linked * linked) * noise
    return row_scale * scale * mixed + shift


def setup_inputs(seed: int = 0) -> dict:
    key_list = jax.random.split(jax.random.key(seed), 3)
    return {
        "view_a": draw_view_a(jax.random.fold_in(key_list[2], 71), 0),
        "view_b": draw_view_b(jax.random.fold_in(key_list[2], 71), 0),
    }


off_weight = 0.0051
eps_value = 1e-05

def normalize(view):
    mean = lax.optimization_barrier(jnp.mean(view, axis=0))
    square = lax.optimization_barrier(jnp.mean(view * view, axis=0))
    inv = lax.rsqrt(square - mean * mean + eps_value)
    return ((view - mean) * inv, inv)

def backward(upper, norm, inv):
    first = lax.optimization_barrier(jnp.mean(upper, axis=0))
    second = lax.optimization_barrier(jnp.mean(upper * norm, axis=0))
    return inv * (upper - first - norm * second)

def reference(view_a, view_b):
    norm_a, inv_a = normalize(view_a)
    norm_b, inv_b = normalize(view_b)
    half_a = norm_a.astype(jnp.bfloat16)
    half_b = norm_b.astype(jnp.bfloat16)
    wide_a = half_a.astype(jnp.float32)
    wide_b = half_b.astype(jnp.float32)
    blocks = 16
    width = FEAT // blocks
    columns = jnp.arange(FEAT).astype(jnp.int32)

    def step(carry, index):
        total, up_b = carry
        start = (index * width).astype(jnp.int32)
        block = lax.dynamic_slice_in_dim(half_a, start, width, 1)
        block_wide = lax.dynamic_slice_in_dim(wide_a, start, width, 1)
        corr = lax.dot_general(block, half_b, (((0,), (0,)), ((), ())), preferred_element_type=jnp.float32) / BATCH
        ids = start + jnp.arange(width).astype(jnp.int32)
        diag = ids[:, None] == columns[None, :]
        miss = 1.0 - corr
        total = total + jnp.sum(jnp.where(diag, miss * miss, off_weight * corr * corr))
        slope = jnp.where(diag, -2.0 * miss, 2.0 * off_weight * corr)
        piece_a = lax.dot_general(wide_b, slope, (((1,), (1,)), ((), ())), precision=lax.Precision.HIGHEST, preferred_element_type=jnp.float32)
        up_b = up_b + jnp.dot(block_wide, slope, precision=lax.Precision.HIGHEST, preferred_element_type=jnp.float32)
        return ((total, up_b), piece_a)
    start_carry = (jnp.zeros((), jnp.float32), jnp.zeros((BATCH, FEAT), jnp.float32))
    (total, up_b), pieces = lax.scan(step, start_carry, jnp.arange(blocks).astype(jnp.int32))
    up_a = jnp.transpose(pieces, (1, 0, 2)).reshape(BATCH, FEAT)
    grad_a = backward(up_a, norm_a, inv_a)
    grad_b = backward(up_b, norm_b, inv_b)
    return (total / FEAT, grad_a, grad_b)
```

```python
import functools

import jax
import jax.numpy as jnp
from jax import lax
from jax.experimental import pallas as pl
from jax.experimental.pallas import tpu as pltpu
from jax.sharding import Mesh, PartitionSpec as P

FEAT = 16384
BATCH = 2048

off_weight = 0.0051
eps_value = 1e-05

f32 = jnp.float32
bf16 = jnp.bfloat16

NAMES = ("y1", "y0", "xh", "xl", "z1", "z0", "k")
ROW = ("y1", "y0", "xh")
COL = ("xl", "z1", "z0", "k")
SWAP = [(0, 1), (1, 0)]
AHEAD = [(i, (i + 1) % 4) for i in range(4)]
BACK = [(i, (i + 3) % 4) for i in range(4)]


TURN_A = (((0, 1, 0), (1, 0, 0), (1, 0, 1)), ((0, 1, 0, 1), (1, 1, 1, 0), (0, 1, 0, 1)))
TURN_B = ((((0, 0, 1), (0, 1, 0), (1, 0, 0)), ((0, 1, 1, 1), (1, 0, 1, 1), (1, 0, 1, 0))),) * 2


def spread(x, axes, n):
    return lax.all_to_all(jnp.broadcast_to(x[None], (n,) + x.shape), axes, 0, 0)


def bits(n):
    return [(n >> s) & 1 for s in range(6, -1, -1)]


def number(p):
    return sum(v << s for v, s in zip(p, range(6, -1, -1)))


def turned(first, second, rows):
    matrix, shift = rows
    out = []
    for m, v in zip(matrix, shift):
        out.append((sum(a * b for a, b in zip(m, first)) + sum(a * b for a, b in zip(v, second))) % 2)
    return out


def crossing_tables():
    pairs_a, wanted_a = [], [[0, 0, 0]] * 128
    pairs_b, wanted_b = [[], []], [[0] * 8 for _ in range(128)]
    for target in range(128):
        y1, y0, xh, xl, z1, z0, k = bits(target)
        g = turned((y1, y0, xh), (xl, z1, z0, k), TURN_A)
        source = number((xl, z1, z0, k, g[0], g[1], g[2]))
        pairs_a.append((source, target))
        wanted_a[source] = [y0, xh, y1]
        for step in range(2):
            g = turned((xl, z1, z0), (y1, y0, xh, k), TURN_B[step])
            source = number((g[0], g[1], g[2], y1, y0, xh, k ^ step))
            pairs_b[step].append((source, target))
            wanted_b[source][4 * step : 4 * step + 4] = [xl, z1, z0, k]
    return pairs_a, wanted_a, pairs_b, wanted_b


def finish_stats(sums, count, view):
    mean = sums[0] / count
    inv = lax.rsqrt(sums[1] / count - mean * mean + eps_value)
    return ((view - mean) * inv, mean, inv)


def stats(view):
    return jnp.stack([jnp.sum(view, axis=0), jnp.sum(view * view, axis=0)])


def dot(x, y, dims):
    return lax.dot_general(x, y, (dims, ((), ())), preferred_element_type=f32)


def pick(x, index):
    return lax.dynamic_index_in_dim(x, index, 0, keepdims=False)


def both(which, mine, other, axis):
    return jnp.concatenate([jnp.where(which == 0, mine, other), jnp.where(which == 0, other, mine)], axis=axis)


def tie(*xs):
    return lax.optimization_barrier(xs)


def ring_near(own, ring):
    return [lax.ppermute(own, ring, AHEAD), lax.ppermute(own, ring, BACK)]


def trade(blocks, axis):
    return [lax.ppermute(x, axis, SWAP) for x in blocks]


OFFSETS = (0, 3, 1, 2)


def places(ids):
    return [((ids[0] + offset) & 3, ids[1] ^ flip) for flip in range(2) for offset in OFFSETS]


def gram_kernel(first, ids, *refs):
    if first:
        result, send, held, sems, out, out_sems = refs[8:]
    else:
        mine, give, *sends, held, sems = refs[8:]
    copies = []
    for i, ref in enumerate(refs[:8]):
        slot = held.at[i // 4, pl.ds(256 * (i % 4), 256), :]
        copies.append(pltpu.make_async_copy(ref, slot, sems.at[i]))
        copies[-1].start()
    copies[0].wait()
    own = held[0, 0:256, :].T
    leaving = []
    for flip in range(2):
        for index in range(4 * flip, 4 * flip + 4):
            if index:
                copies[index].wait()
        prod = dot(held[flip], own, ((1,), (0,))).astype(bf16)
        for index in range(4 * flip, 4 * flip + 4):
            p, k = places(ids)[index]
            high, low = p >> 1, p & 1
            for s in range(2):
                at = 256 * (index % 4) + 128 * s
                part = prod[at : at + 128]
                if first:
                    rows = pl.ds(pl.multiple_of(128 * k, 128), 128)
                    for half in range(2):
                        out[2 * (2 * s + high) + low, half, rows, :] = part[:, 128 * half : 128 * (half + 1)]
                    wanted = (high == ids[2]) & (low == ids[3]) & (s == ids[4])

                    @pl.when(wanted)
                    def _():
                        send[k] = held[flip, at : at + 128, :]

                else:

                    @pl.when(ids[10] == s)
                    def _():
                        mine[2 * p + k] = part

                    @pl.when(ids[10] != s)
                    def _():
                        give[2 * p + k] = part

                    for step in range(2):
                        place = [ids[2 + 4 * step + j] for j in range(4)]
                        wanted = (high == place[0]) & (low == place[1]) & (k == place[2]) & (s == place[3])

                        @pl.when(wanted)
                        def _():
                            if step == 0:
                                sends[0][...] = held[flip, at : at + 64, :]
                                sends[1][...] = held[flip, at + 64 : at + 128, :]
                            else:
                                sends[2][...] = held[flip, at : at + 128, :]

        if first:
            rows = pl.ds(pl.multiple_of(128 * (ids[1] ^ flip), 128), 128)
            away = pltpu.make_async_copy(out.at[:, :, rows, :], result.at[:, :, rows, :], out_sems.at[flip])
            away.start()
            leaving.append(away)
    for away in leaving:
        away.wait()


def call(kernel, out_shape, extra, name, space=pltpu.VMEM, scratch=(), flops=2 * 256 * 2048 * 1024, far=()):
    vmem = pl.BlockSpec(memory_space=pltpu.VMEM)
    return pl.pallas_call(
        kernel,
        out_shape=out_shape,
        in_specs=[pl.BlockSpec(memory_space=pltpu.SMEM)] + [vmem] * extra + [pl.BlockSpec(memory_space=space)] * 8,
        out_specs=[pl.BlockSpec(memory_space=pltpu.HBM) if i in far else vmem for i in range(len(out_shape))],
        scratch_shapes=list(scratch),
        compiler_params=pltpu.CompilerParams(vmem_limit_bytes=14 * 1024 * 1024),
        cost_estimate=pl.CostEstimate(flops=flops, bytes_accessed=flops >> 8, transcendentals=0),
        name=name,
    )


def gram_part(first, ids, blocks):
    if first:
        shapes = [(8, 2, 256, 128), (2, 128, 1024)]
    else:
        shapes = [(8, 128, 256), (8, 128, 256), (64, 1024), (64, 1024), (128, 1024)]
    out = [jax.ShapeDtypeStruct(shape, bf16) for shape in shapes]
    scratch = [pltpu.VMEM((2, 1024, 1024), bf16), pltpu.SemaphoreType.DMA((8,))]
    if first:
        scratch += [pltpu.VMEM((8, 2, 256, 128), bf16), pltpu.SemaphoreType.DMA((2,))]
    flops = 2 * 256 * 2048 * 1024 if first else 1 << 20
    kernel = functools.partial(gram_kernel, first)
    return call(kernel, out, 0, "gram_part", pl.ANY, scratch, flops, (0,) if first else ())(ids, *blocks)


def blend_kernel(mine, traded, received, out):
    piece = received[0].astype(f32)
    for i in range(1, 16):
        piece = piece + received[i].astype(f32)
    piece = piece.astype(bf16)
    for i in range(8):
        out[i, 0:128] = (mine[i].astype(f32) + traded[i].astype(f32)).astype(bf16)
        out[i, 128:256, 0:128] = piece[0:128]
        out[i, 128:256, 128:256] = piece[128:256]


def blend(mine, traded, received):
    vmem = pl.BlockSpec(memory_space=pltpu.VMEM)
    return pl.pallas_call(
        blend_kernel,
        out_shape=jax.ShapeDtypeStruct((8, 256, 256), bf16),
        in_specs=[vmem] * 3,
        out_specs=vmem,
        compiler_params=pltpu.CompilerParams(vmem_limit_bytes=14 * 1024 * 1024),
        cost_estimate=pl.CostEstimate(flops=1 << 20, bytes_accessed=4 << 20, transcendentals=0),
        name="blend",
    )(mine, traded, received)


def apply(part, blocks, ids):
    out = None
    for ref, (p, k) in zip(blocks, places(ids)):
        left = jnp.concatenate([part(p >> 1, p & 1, k, s) for s in range(2)], axis=1)
        prod = dot(left, ref[...], ((1,), (0,)))
        out = prod if out is None else out + prod
    return out * (2.0 * off_weight / BATCH)


def image_sum(x):
    return jnp.sum(x, axis=0, keepdims=True)


def split(x):
    high = x.astype(bf16).astype(f32)
    return [high, x - high]


def send_all(part, result, start, rows, sems, first_sem):
    copies = []
    for i in range(16):
        copies.append(pltpu.make_async_copy(part, result.at[i, start : start + rows], sems.at[first_sem + i]))
        copies[-1].start()
    return copies


def second_kernel(ids, mixed, traded, partner, *refs):
    blocks, up, result, out, sems = refs[:8], refs[8], refs[9], refs[10], refs[11]

    def part(high, low, k, s):
        index = 4 * high + 2 * low + k
        rows = jnp.where(ids[10] == s, mixed[index, 128:256, :], traded[index])
        return jnp.concatenate([rows[:, 0:128], rows[:, 128:256]], axis=0)

    piece = mixed[0, 0:128].astype(f32)
    for i in range(1, 8):
        piece = piece + mixed[i, 0:128].astype(f32)
    out[0:128] = piece.astype(bf16)
    leaving = send_all(out.at[0:128], result, 0, 128, sems, 0)
    value = apply(part, blocks, ids)
    up[...] = value
    norm = blocks[0][...].astype(f32)
    sums = [image_sum(value), partner[0:1], image_sum(norm), jnp.zeros((1, 1024), f32)]
    sums += split(image_sum(value * norm)) + split(partner[1:2])
    row = lax.broadcasted_iota(jnp.int32, (8, 1024), 0)
    rows = jnp.zeros((8, 1024), f32)
    for i in range(8):
        rows = jnp.where(row == i, sums[i], rows)
    rows = jnp.concatenate([rows[:, 256 * i : 256 * (i + 1)] for i in range(4)], axis=0).astype(bf16)
    out[128:160] = rows
    leaving += send_all(out.at[128:160], result, 128, 32, sems, 16)
    for away in leaving:
        away.wait()


def second_view(ids, mixed, traded, partner, blocks):
    out = [jax.ShapeDtypeStruct((256, 1024), f32), jax.ShapeDtypeStruct((16, 160, 256), bf16)]
    scratch = [pltpu.VMEM((160, 256), bf16), pltpu.SemaphoreType.DMA((32,))]
    return call(second_kernel, out, 3, "second_view", scratch=scratch, far=(1,))(ids, mixed, traded, partner, *blocks)


def first_kernel(ids, last, *refs):
    blocks, keep, give, result, out, sems = refs[:8], refs[8], refs[9], refs[10], refs[11], refs[12]

    def part(high, low, k, s):
        at = pl.ds(pl.multiple_of(k * 128, 128), 128)
        index = 4 * (2 * s + high) + 2 * low
        return jnp.concatenate([last[index, 0:128, at], last[index + 1, 0:128, at]], axis=0)

    value = apply(part, blocks, ids)
    side = ids[5]
    keep[...] = jnp.where(side == 0, value[0:128], value[128:256])
    give[...] = jnp.where(side == 0, value[128:256], value[0:128]).astype(bf16)
    sums = [image_sum(value), image_sum(value * blocks[0][...].astype(f32))]
    terms = None
    for i in range(8):
        term = last[2 * i + side, 128:160].astype(f32)
        terms = term if terms is None else terms + term
    row = lax.broadcasted_iota(jnp.int32, (32, 256), 0) % 8
    loss = image_sum(jnp.where((row == 4) | (row == 5), terms, 0.0)) / (2.0 * BATCH)
    products = []
    for j in range(4):
        products.append(terms[8 * j + 6 : 8 * j + 7] + terms[8 * j + 7 : 8 * j + 8])
        corr = products[-1] / BATCH
        miss = 1.0 - corr
        loss = loss + miss * miss - off_weight * corr * corr
    sums.append(jnp.concatenate([loss, jnp.zeros((1, 768), f32)], axis=1))
    sums.append(jnp.concatenate([terms[8 * j + 2 : 8 * j + 3] for j in range(4)], axis=1))
    sums.append(jnp.concatenate(products, axis=1))
    for j in range(8):
        out[j : j + 1, :] = sums[j] if j < 5 else jnp.zeros((1, 1024), f32)
    for away in send_all(out, result, 0, 8, sems, 0):
        away.wait()


def first_view(ids, last, blocks):
    out = [
        jax.ShapeDtypeStruct((128, 1024), f32),
        jax.ShapeDtypeStruct((128, 1024), bf16),
        jax.ShapeDtypeStruct((16, 8, 1024), f32),
    ]
    scratch = [pltpu.VMEM((8, 1024), f32), pltpu.SemaphoreType.DMA((16,))]
    return call(first_kernel, out, 1, "first_view", scratch=scratch, far=(2,))(ids, last, *blocks)


def finish(up, up_norm, partner, partner_norm, count):
    corr = partner_norm / count
    diag = -2.0 * (1.0 - corr) - 2.0 * off_weight * corr
    return diag, (up + diag * partner) / count, (up_norm + diag * partner_norm) / count


def vmem_call(kernel, out_shape, args, name, flops):
    vmem = pl.BlockSpec(memory_space=pltpu.VMEM)
    smem = pl.BlockSpec(memory_space=pltpu.SMEM)
    return pl.pallas_call(
        kernel,
        out_shape=out_shape,
        in_specs=[smem] + [vmem] * (len(args) - 1),
        out_specs=vmem,
        compiler_params=pltpu.CompilerParams(vmem_limit_bytes=14 * 1024 * 1024),
        cost_estimate=pl.CostEstimate(flops=flops, bytes_accessed=1 << 20, transcendentals=0),
        name=name,
    )(*args)


def partner_kernel(ids, other, half, out):
    other = other[...].astype(f32)
    out[0:1, :] = image_sum(other)
    out[1:2, :] = image_sum(other * half[...].astype(f32))


def arrange_kernel(ids, early, mid, late, out):
    for half in range(2):
        columns = slice(1024 * half, 1024 * (half + 1))
        out[0:64, columns] = jnp.where(ids[1] == half, early[...], late[0:64])
        out[64:128, columns] = jnp.where(ids[1] == half, mid[...], late[64:128])


def finish_kernel(ids, sums, scales, view, keep, traded, block, grad, loss):
    xl, row = ids[0], ids[2]
    loss[0, 0] = jnp.sum(sums[:, 2, :]) / FEAT
    for half in range(2):
        columns = slice(1024 * half, 1024 * (half + 1))
        total = sums[8 * half]
        for i in range(1, 8):
            total = total + sums[8 * half + i]
        partner = sums[2 * row + half]
        diag, first, second = finish(total[0:1], total[1:2], partner[3:4], partner[4:5], BATCH)
        mean, inv = scales[0:1, columns], scales[1:2, columns]
        up = jnp.where(xl == half, keep[...], traded[...].astype(f32))
        norm = (view[:, columns] - mean) * inv
        grad[:, columns] = inv * (up + diag * block[:, columns].astype(f32) - first - norm * second)


def finish_first(ids, *args):
    vmem = pl.BlockSpec(memory_space=pltpu.VMEM)
    smem = pl.BlockSpec(memory_space=pltpu.SMEM)
    return pl.pallas_call(
        finish_kernel,
        out_shape=[jax.ShapeDtypeStruct((128, 2048), f32), jax.ShapeDtypeStruct((1, 1), f32)],
        in_specs=[smem] + [vmem] * len(args),
        out_specs=[vmem, smem],
        compiler_params=pltpu.CompilerParams(vmem_limit_bytes=14 * 1024 * 1024),
        cost_estimate=pl.CostEstimate(flops=1 << 22, bytes_accessed=4 << 20, transcendentals=0),
        name="finish_first",
    )(ids, *args)


def row_sum(x):
    x = x + sum(lax.ppermute(x, ("y1", "y0"), [(i, (i + step) % 4) for i in range(4)]) for step in (1, 2, 3))
    return x + lax.ppermute(x, "xh", SWAP)


def local(view_a, view_b):
    count = BATCH
    core = lax.axis_index("k")
    xl = lax.axis_index("xl")
    device = lax.axis_index(ROW + COL)
    pairs_a, wanted_a, pairs_b, wanted_b = crossing_tables()
    ids_a = jnp.concatenate([jnp.stack([lax.axis_index(("z1", "z0")), core]), jnp.array(wanted_a)[device], xl[None]])
    ids_b = jnp.concatenate([jnp.stack([lax.axis_index(("y1", "y0")), lax.axis_index("xh")]), jnp.array(wanted_b)[device], core[None]])

    stats_a, late_b = tie(stats(view_a), view_b)
    norm_a, mean_a, inv_a = finish_stats(jnp.sum(spread(stats_a, COL, 16), axis=0), count, view_a)
    norm_b, _, inv_b = finish_stats(row_sum(stats(late_b)), count, view_b)
    half_a = norm_a.astype(bf16)
    half_b = norm_b.astype(bf16)

    zs, ys = ("z1", "z0"), ("y1", "y0")
    parts_a = jnp.transpose(half_a.reshape(128, 2, 1024), (1, 0, 2))
    own_a = both(xl, pick(parts_a, xl), lax.ppermute(pick(parts_a, 1 - xl), "xl", SWAP), 0)
    near_b = ring_near(half_b, ys)
    own_a, late_half_b = tie(own_a, half_b)
    near_a = ring_near(own_a, zs)
    other_own_a = trade([own_a], "k")
    other_own_b = trade([late_half_b], "xh")
    *near_a, near_b[0], near_b[1], other_own_b[0] = tie(*near_a, *near_b, *other_own_b)
    far_pairs = [(2 * i + k, 2 * ((i + (3 if k else 1)) % 4) + k) for i in range(4) for k in range(2)]
    far_a = lax.ppermute(jnp.where(core == 0, near_a[0], near_a[1]), zs + ("k",), far_pairs)
    other_near_a = trade(near_a, "k")
    other_near_b = ring_near(other_own_b[0], ys)
    far_b = lax.ppermute(near_b[0], ys, AHEAD)
    other_far_a, *other_near_b = tie(*trade([far_a], "k"), *other_near_b)
    other_far_b = lax.ppermute(other_near_b[1], ys, BACK)
    blocks_a = [own_a, *near_a, far_a, *other_own_a, *other_near_a, other_far_a]

    part_a, send_a = gram_part(True, ids_a, blocks_a)
    part_a, far_b, other_far_b = tie(part_a, far_b, other_far_b)
    blocks_b = [half_b, *near_b, far_b, *other_own_b, *other_near_b, other_far_b]
    other_a = lax.ppermute(send_a.reshape(256, 1024), ROW + COL, pairs_a)
    piece_a = lax.all_to_all(part_a.reshape(16, 256, 128), ("y1", "y0", "xh", "xl"), 0, 0)
    mine_b, give_b, *send_b = gram_part(False, ids_b, blocks_b)
    mixed = blend(mine_b, lax.ppermute(give_b, "k", SWAP), piece_a)
    ids = jnp.stack([xl, core, lax.axis_index(ROW)])
    partner = vmem_call(partner_kernel, jax.ShapeDtypeStruct((2, 1024), f32), (ids, other_a, half_b), "partner", 1 << 34)
    mixed, partner = tie(mixed, partner)
    mixed = lax.all_to_all(mixed, ("xl", "z1", "z0"), 0, 0)

    mixed, early = tie(mixed, send_b[0])
    early = lax.ppermute(early, ROW + COL, pairs_b[0])
    traded = lax.ppermute(mixed[:, 128:], "k", SWAP)
    up_b, last = second_view(ids_b, mixed, traded, partner, blocks_b)
    last, early = tie(last, early)
    last = lax.all_to_all(last, ("y1", "y0", "xh", "xl"), 0, 0)
    last, *late = tie(last, *send_b[1:])
    late = [lax.ppermute(x, ROW + COL, pairs) for x, pairs in zip(late, pairs_b)]
    block = jax.ShapeDtypeStruct((128, 2048), bf16)
    block = vmem_call(arrange_kernel, block, (ids, early, *late), "arrange", 1 << 34)

    keep, give, sums_a = first_view(ids_a, last, blocks_a)
    sums_a, keep, give, up_b, last = tie(sums_a, keep, give, up_b, last)
    sums_a = lax.all_to_all(sums_a, COL, 0, 0)

    sums_b = pick(jnp.moveaxis(last[:, 128:].reshape(8, 2, 4, 8, 256), 1, 0), xl)
    sums_b = jnp.swapaxes(jnp.sum(sums_b.astype(f32), axis=0), 0, 1).reshape(8, 1024)
    partner_norm = sums_b[6] + sums_b[7]
    diag_b, first_b, second_b = finish(sums_b[0], sums_b[4] + sums_b[5], sums_b[1], partner_norm, count)
    grad_b = inv_b * (up_b + diag_b * other_a.astype(f32) - first_b - norm_b * second_b)

    traded = lax.ppermute(give, "xl", SWAP)
    grad_a, loss_value = finish_first(ids, sums_a, jnp.stack([mean_a, inv_a]), view_a, keep, traded, block)
    return (loss_value[0, 0], grad_a, grad_b)


def solution(mesh):
    fine = Mesh(mesh.devices.reshape((2,) * 7), NAMES)
    return jax.shard_map(
        local,
        mesh=fine,
        in_specs=(P(COL, ROW), P(ROW, COL)),
        out_specs=(P(), P(COL, ROW), P(ROW, COL)),
        check_vma=False,
    )
```

```python
import functools

import jax
import jax.numpy as jnp
from jax import lax
from jax.experimental import pallas as pl
from jax.experimental.pallas import tpu as pltpu
from jax.sharding import Mesh, PartitionSpec as P

FEAT = 16384
BATCH = 2048

off_weight = 0.0051
eps_value = 1e-05

f32 = jnp.float32
bf16 = jnp.bfloat16

NAMES = ("y1", "y0", "xh", "xl", "z1", "z0", "k")
ROW = ("y1", "y0", "xh")
COL = ("xl", "z1", "z0", "k")
SWAP = [(0, 1), (1, 0)]
AHEAD = [(i, (i + 1) % 4) for i in range(4)]
BACK = [(i, (i + 3) % 4) for i in range(4)]


TURN_A = (((0, 1, 0), (1, 0, 0), (1, 0, 1)), ((0, 1, 0, 1), (1, 1, 1, 0), (0, 1, 0, 1)))
TURN_B = ((((0, 0, 1), (0, 1, 0), (1, 0, 0)), ((0, 1, 1, 1), (1, 0, 1, 1), (1, 0, 1, 0))),) * 2


def spread(x, axes, n):
    return lax.all_to_all(jnp.broadcast_to(x[None], (n,) + x.shape), axes, 0, 0)


def bits(n):
    return [(n >> s) & 1 for s in range(6, -1, -1)]


def number(p):
    return sum(v << s for v, s in zip(p, range(6, -1, -1)))


def turned(first, second, rows):
    matrix, shift = rows
    out = []
    for m, v in zip(matrix, shift):
        out.append((sum(a * b for a, b in zip(m, first)) + sum(a * b for a, b in zip(v, second))) % 2)
    return out


def crossing_tables():
    pairs_a, wanted_a = [], [[0, 0, 0]] * 128
    pairs_b, wanted_b = [[], []], [[0] * 8 for _ in range(128)]
    for target in range(128):
        y1, y0, xh, xl, z1, z0, k = bits(target)
        g = turned((y1, y0, xh), (xl, z1, z0, k), TURN_A)
        source = number((xl, z1, z0, k, g[0], g[1], g[2]))
        pairs_a.append((source, target))
        wanted_a[source] = [y0, xh, y1]
        for step in range(2):
            g = turned((xl, z1, z0), (y1, y0, xh, k), TURN_B[step])
            source = number((g[0], g[1], g[2], y1, y0, xh, k ^ step))
            pairs_b[step].append((source, target))
            wanted_b[source][4 * step : 4 * step + 4] = [xl, z1, z0, k]
    return pairs_a, wanted_a, pairs_b, wanted_b


def finish_stats(sums, count, view):
    mean = sums[0] / count
    inv = lax.rsqrt(sums[1] / count - mean * mean + eps_value)
    return ((view - mean) * inv, mean, inv)


def stats(view):
    return jnp.stack([jnp.sum(view, axis=0), jnp.sum(view * view, axis=0)])


def dot(x, y, dims):
    return lax.dot_general(x, y, (dims, ((), ())), preferred_element_type=f32)


def pick(x, index):
    return lax.dynamic_index_in_dim(x, index, 0, keepdims=False)


def both(which, mine, other, axis):
    return jnp.concatenate([jnp.where(which == 0, mine, other), jnp.where(which == 0, other, mine)], axis=axis)


def tie(*xs):
    return lax.optimization_barrier(xs)


def ring_near(own, ring):
    return [lax.ppermute(own, ring, AHEAD), lax.ppermute(own, ring, BACK)]


def trade(blocks, axis):
    return [lax.ppermute(x, axis, SWAP) for x in blocks]


OFFSETS = (0, 3, 1, 2)


def places(ids):
    return [((ids[0] + offset) & 3, ids[1] ^ flip) for flip in range(2) for offset in OFFSETS]


def gram_kernel(first, ids, *refs):
    if first:
        out, send, held, sems = refs[8:]
    else:
        mine, give, *sends, held, sems = refs[8:]
    copies = []
    for i, ref in enumerate(refs[:8]):
        slot = held.at[i // 4, pl.ds(256 * (i % 4), 256), :]
        copies.append(pltpu.make_async_copy(ref, slot, sems.at[i]))
        copies[-1].start()
    copies[0].wait()
    own = held[0, 0:256, :].T
    for flip in range(2):
        for index in range(4 * flip, 4 * flip + 4):
            if index:
                copies[index].wait()
        prod = dot(held[flip], own, ((1,), (0,))).astype(bf16)
        for index in range(4 * flip, 4 * flip + 4):
            p, k = places(ids)[index]
            high, low = p >> 1, p & 1
            for s in range(2):
                at = 256 * (index % 4) + 128 * s
                part = prod[at : at + 128]
                if first:
                    rows = pl.ds(pl.multiple_of(128 * k, 128), 128)
                    for half in range(2):
                        out[2 * (2 * s + high) + low, half, rows, :] = part[:, 128 * half : 128 * (half + 1)]
                    wanted = (high == ids[2]) & (low == ids[3]) & (s == ids[4])

                    @pl.when(wanted)
                    def _():
                        send[k] = held[flip, at : at + 128, :]

                else:

                    @pl.when(ids[10] == s)
                    def _():
                        mine[2 * p + k] = part

                    @pl.when(ids[10] != s)
                    def _():
                        give[2 * p + k] = part

                    for step in range(2):
                        place = [ids[2 + 4 * step + j] for j in range(4)]
                        wanted = (high == place[0]) & (low == place[1]) & (k == place[2]) & (s == place[3])

                        @pl.when(wanted)
                        def _():
                            if step == 0:
                                sends[0][...] = held[flip, at : at + 64, :]
                                sends[1][...] = held[flip, at + 64 : at + 128, :]
                            else:
                                sends[2][...] = held[flip, at : at + 128, :]


def call(kernel, out_shape, extra, name, space=pltpu.VMEM, scratch=(), flops=2 * 256 * 2048 * 1024):
    vmem = pl.BlockSpec(memory_space=pltpu.VMEM)
    return pl.pallas_call(
        kernel,
        out_shape=out_shape,
        in_specs=[pl.BlockSpec(memory_space=pltpu.SMEM)] + [vmem] * extra + [pl.BlockSpec(memory_space=space)] * 8,
        out_specs=[vmem] * len(out_shape),
        scratch_shapes=list(scratch),
        compiler_params=pltpu.CompilerParams(vmem_limit_bytes=14 * 1024 * 1024),
        cost_estimate=pl.CostEstimate(flops=flops, bytes_accessed=flops >> 8, transcendentals=0),
        name=name,
    )


def gram_part(first, ids, blocks):
    if first:
        shapes = [(8, 2, 256, 128), (2, 128, 1024)]
    else:
        shapes = [(8, 128, 256), (8, 128, 256), (64, 1024), (64, 1024), (128, 1024)]
    out = [jax.ShapeDtypeStruct(shape, bf16) for shape in shapes]
    scratch = [pltpu.VMEM((2, 1024, 1024), bf16), pltpu.SemaphoreType.DMA((8,))]
    flops = 2 * 256 * 2048 * 1024 if first else 1 << 20
    return call(functools.partial(gram_kernel, first), out, 0, "gram_part", pl.ANY, scratch, flops)(ids, *blocks)


def blend_kernel(mine, traded, received, out):
    piece = received[0].astype(f32)
    for i in range(1, 16):
        piece = piece + received[i].astype(f32)
    piece = piece.astype(bf16)
    for i in range(8):
        out[i, 0:128] = (mine[i].astype(f32) + traded[i].astype(f32)).astype(bf16)
        out[i, 128:256, 0:128] = piece[0:128]
        out[i, 128:256, 128:256] = piece[128:256]


def blend(mine, traded, received):
    vmem = pl.BlockSpec(memory_space=pltpu.VMEM)
    return pl.pallas_call(
        blend_kernel,
        out_shape=jax.ShapeDtypeStruct((8, 256, 256), bf16),
        in_specs=[vmem] * 3,
        out_specs=vmem,
        compiler_params=pltpu.CompilerParams(vmem_limit_bytes=14 * 1024 * 1024),
        cost_estimate=pl.CostEstimate(flops=1 << 20, bytes_accessed=4 << 20, transcendentals=0),
        name="blend",
    )(mine, traded, received)


def apply(part, blocks, ids):
    out = None
    for ref, (p, k) in zip(blocks, places(ids)):
        left = jnp.concatenate([part(p >> 1, p & 1, k, s) for s in range(2)], axis=1)
        prod = dot(left, ref[...], ((1,), (0,)))
        out = prod if out is None else out + prod
    return out * (2.0 * off_weight / BATCH)


def image_sum(x):
    return jnp.sum(x, axis=0, keepdims=True)


def split(x):
    high = x.astype(bf16).astype(f32)
    return [high, x - high]


def second_kernel(ids, mixed, traded, partner, *refs):
    blocks, up, out = refs[:8], refs[8], refs[9]

    def part(high, low, k, s):
        index = 4 * high + 2 * low + k
        rows = jnp.where(ids[10] == s, mixed[index, 128:256, :], traded[index])
        return jnp.concatenate([rows[:, 0:128], rows[:, 128:256]], axis=0)

    piece = mixed[0, 0:128].astype(f32)
    for i in range(1, 8):
        piece = piece + mixed[i, 0:128].astype(f32)
    piece = piece.astype(bf16)
    for i in range(16):
        out[i, 0:128] = piece
    value = apply(part, blocks, ids)
    up[...] = value
    norm = blocks[0][...].astype(f32)
    sums = [image_sum(value), partner[0:1], image_sum(norm), jnp.zeros((1, 1024), f32)]
    sums += split(image_sum(value * norm)) + split(partner[1:2])
    row = lax.broadcasted_iota(jnp.int32, (8, 1024), 0)
    rows = jnp.zeros((8, 1024), f32)
    for i in range(8):
        rows = jnp.where(row == i, sums[i], rows)
    rows = jnp.concatenate([rows[:, 256 * i : 256 * (i + 1)] for i in range(4)], axis=0).astype(bf16)
    for i in range(16):
        out[i, 128:160] = rows


def second_view(ids, mixed, traded, partner, blocks):
    out = [jax.ShapeDtypeStruct((256, 1024), f32), jax.ShapeDtypeStruct((16, 160, 256), bf16)]
    return call(second_kernel, out, 3, "second_view")(ids, mixed, traded, partner, *blocks)


def first_kernel(ids, last, *refs):
    blocks, (keep, give, out, second_sums) = refs[:8], refs[8:]

    def part(high, low, k, s):
        at = pl.ds(pl.multiple_of(k * 128, 128), 128)
        index = 4 * (2 * s + high) + 2 * low
        return jnp.concatenate([last[index, 0:128, at], last[index + 1, 0:128, at]], axis=0)

    value = apply(part, blocks, ids)
    side = ids[5]
    keep[...] = jnp.where(side == 0, value[0:128], value[128:256])
    give[...] = jnp.where(side == 0, value[128:256], value[0:128]).astype(bf16)
    sums = [image_sum(value), image_sum(value * blocks[0][...].astype(f32))]
    terms = None
    for i in range(8):
        term = last[2 * i + side, 128:160].astype(f32)
        terms = term if terms is None else terms + term
    second_sums[...] = terms
    row = lax.broadcasted_iota(jnp.int32, (32, 256), 0) % 8
    loss = image_sum(jnp.where((row == 4) | (row == 5), terms, 0.0)) / (2.0 * BATCH)
    products = []
    for j in range(4):
        products.append(terms[8 * j + 6 : 8 * j + 7] + terms[8 * j + 7 : 8 * j + 8])
        corr = products[-1] / BATCH
        miss = 1.0 - corr
        loss = loss + miss * miss - off_weight * corr * corr
    sums.append(jnp.concatenate([loss, jnp.zeros((1, 768), f32)], axis=1))
    sums.append(jnp.concatenate([terms[8 * j + 2 : 8 * j + 3] for j in range(4)], axis=1))
    sums.append(jnp.concatenate(products, axis=1))
    for i in range(16):
        for j in range(5):
            out[i, j : j + 1, :] = sums[j]


def first_view(ids, last, blocks):
    out = [
        jax.ShapeDtypeStruct((128, 1024), f32),
        jax.ShapeDtypeStruct((128, 1024), bf16),
        jax.ShapeDtypeStruct((16, 5, 1024), f32),
        jax.ShapeDtypeStruct((32, 256), f32),
    ]
    return call(first_kernel, out, 1, "first_view", flops=1 << 20)(ids, last, *blocks)


def finish(up, up_norm, partner, partner_norm, count):
    corr = partner_norm / count
    diag = -2.0 * (1.0 - corr) - 2.0 * off_weight * corr
    return diag, (up + diag * partner) / count, (up_norm + diag * partner_norm) / count


def vmem_call(kernel, out_shape, args, name, flops):
    vmem = pl.BlockSpec(memory_space=pltpu.VMEM)
    smem = pl.BlockSpec(memory_space=pltpu.SMEM)
    return pl.pallas_call(
        kernel,
        out_shape=out_shape,
        in_specs=[smem] + [vmem] * (len(args) - 1),
        out_specs=jax.tree.map(lambda _: vmem, out_shape),
        compiler_params=pltpu.CompilerParams(vmem_limit_bytes=14 * 1024 * 1024),
        cost_estimate=pl.CostEstimate(flops=flops, bytes_accessed=1 << 16, transcendentals=0),
        name=name,
    )(*args)


def partner_kernel(ids, other, half, out):
    other = other[...].astype(f32)
    out[0:1, :] = image_sum(other)
    out[1:2, :] = image_sum(other * half[...].astype(f32))


def arrange_kernel(ids, early, mid, late, keep, traded, block, up):
    for half in range(2):
        columns = slice(1024 * half, 1024 * (half + 1))
        block[0:64, columns] = jnp.where(ids[1] == half, early[...], late[0:64])
        block[64:128, columns] = jnp.where(ids[1] == half, mid[...], late[64:128])
        up[:, columns] = jnp.where(ids[0] == half, keep[...], traded[...].astype(f32))


def finish_second_kernel(ids, terms, scales, view, up, partner, grad):
    for part in range(4):
        columns = slice(256 * part, 256 * (part + 1))
        rows = [terms[8 * part + i : 8 * part + i + 1] for i in range(8)]
        diag, first, second = finish(rows[0], rows[4] + rows[5], rows[1], rows[6] + rows[7], BATCH)
        mean, inv = scales[0:1, columns], scales[1:2, columns]
        norm = (view[:, columns] - mean) * inv
        grad[:, columns] = inv * (up[:, columns] + diag * partner[:, columns].astype(f32) - first - norm * second)


def finish_kernel(ids, sums, scales, view, up, block, grad, loss):
    row = ids[2]
    loss[0, 0] = jnp.sum(sums[:, 2, :]) / FEAT
    for half in range(2):
        columns = slice(1024 * half, 1024 * (half + 1))
        total = sums[8 * half]
        for i in range(1, 8):
            total = total + sums[8 * half + i]
        partner = sums[2 * row + half]
        diag, first, second = finish(total[0:1], total[1:2], partner[3:4], partner[4:5], BATCH)
        mean, inv = scales[0:1, columns], scales[1:2, columns]
        norm = (view[:, columns] - mean) * inv
        grad[:, columns] = inv * (up[:, columns] + diag * block[:, columns].astype(f32) - first - norm * second)


def finish_first(ids, *args):
    vmem = pl.BlockSpec(memory_space=pltpu.VMEM)
    smem = pl.BlockSpec(memory_space=pltpu.SMEM)
    return pl.pallas_call(
        finish_kernel,
        out_shape=[jax.ShapeDtypeStruct((128, 2048), f32), jax.ShapeDtypeStruct((1, 1), f32)],
        in_specs=[smem] + [vmem] * len(args),
        out_specs=[vmem, smem],
        compiler_params=pltpu.CompilerParams(vmem_limit_bytes=14 * 1024 * 1024),
        cost_estimate=pl.CostEstimate(flops=1 << 20, bytes_accessed=1 << 16, transcendentals=0),
        name="finish_first",
    )(ids, *args)


def row_sum(x):
    x = x + sum(lax.ppermute(x, ("y1", "y0"), [(i, (i + step) % 4) for i in range(4)]) for step in (1, 2, 3))
    return x + lax.ppermute(x, "xh", SWAP)


def local(view_a, view_b):
    count = BATCH
    core = lax.axis_index("k")
    xl = lax.axis_index("xl")
    device = lax.axis_index(ROW + COL)
    pairs_a, wanted_a, pairs_b, wanted_b = crossing_tables()
    ids_a = jnp.concatenate([jnp.stack([lax.axis_index(("z1", "z0")), core]), jnp.array(wanted_a)[device], xl[None]])
    ids_b = jnp.concatenate([jnp.stack([lax.axis_index(("y1", "y0")), lax.axis_index("xh")]), jnp.array(wanted_b)[device], core[None]])

    stats_a, late_b = tie(stats(view_a), view_b)
    norm_a, mean_a, inv_a = finish_stats(jnp.sum(spread(stats_a, COL, 16), axis=0), count, view_a)
    norm_b, mean_b, inv_b = finish_stats(row_sum(stats(late_b)), count, view_b)
    half_a = norm_a.astype(bf16)
    half_b = norm_b.astype(bf16)

    zs, ys = ("z1", "z0"), ("y1", "y0")
    parts_a = jnp.transpose(half_a.reshape(128, 2, 1024), (1, 0, 2))
    own_a = both(xl, pick(parts_a, xl), lax.ppermute(pick(parts_a, 1 - xl), "xl", SWAP), 0)
    near_b = ring_near(half_b, ys)
    own_a, late_half_b = tie(own_a, half_b)
    near_a = ring_near(own_a, zs)
    other_own_a = trade([own_a], "k")
    other_own_b = trade([late_half_b], "xh")
    *near_a, near_b[0], near_b[1], other_own_b[0] = tie(*near_a, *near_b, *other_own_b)
    far_pairs = [(2 * i + k, 2 * ((i + (3 if k else 1)) % 4) + k) for i in range(4) for k in range(2)]
    far_a = lax.ppermute(jnp.where(core == 0, near_a[0], near_a[1]), zs + ("k",), far_pairs)
    other_near_a = trade(near_a, "k")
    other_near_b = ring_near(other_own_b[0], ys)
    far_b = lax.ppermute(near_b[0], ys, AHEAD)
    other_far_a, *other_near_b = tie(*trade([far_a], "k"), *other_near_b)
    other_far_b = lax.ppermute(other_near_b[1], ys, BACK)
    blocks_a = [own_a, *near_a, far_a, *other_own_a, *other_near_a, other_far_a]

    part_a, send_a = gram_part(True, ids_a, blocks_a)
    part_a, far_b, other_far_b = tie(part_a, far_b, other_far_b)
    blocks_b = [half_b, *near_b, far_b, *other_own_b, *other_near_b, other_far_b]
    other_a = lax.ppermute(send_a.reshape(256, 1024), ROW + COL, pairs_a)
    piece_a = lax.all_to_all(part_a.reshape(16, 256, 128), ("y1", "y0", "xh", "xl"), 0, 0)
    mine_b, give_b, *send_b = gram_part(False, ids_b, blocks_b)
    mixed = blend(mine_b, lax.ppermute(give_b, "k", SWAP), piece_a)
    ids = jnp.stack([xl, core, lax.axis_index(ROW)])
    partner = vmem_call(partner_kernel, jax.ShapeDtypeStruct((2, 1024), f32), (ids, other_a, half_b), "partner", 1 << 34)
    mixed, partner = tie(mixed, partner)
    mixed = lax.all_to_all(mixed, ("xl", "z1", "z0"), 0, 0)

    mixed, early = tie(mixed, send_b[0])
    early = lax.ppermute(early, ROW + COL, pairs_b[0])
    traded = lax.ppermute(mixed[:, 128:], "k", SWAP)
    up_b, last = second_view(ids_b, mixed, traded, partner, blocks_b)
    last, early = tie(last, early)
    last = lax.all_to_all(last, ("y1", "y0", "xh", "xl"), 0, 0)
    last, *late = tie(last, *send_b[1:])
    late = [lax.ppermute(x, ROW + COL, pairs) for x, pairs in zip(late, pairs_b)]

    keep, give, sums_a, sums_b = first_view(ids_a, last, blocks_a)
    traded = lax.ppermute(give, "xl", SWAP)
    out = [jax.ShapeDtypeStruct((128, 2048), bf16), jax.ShapeDtypeStruct((128, 2048), f32)]
    block, up_own = vmem_call(arrange_kernel, out, (ids, early, *late, keep, traded), "arrange", 1 << 34)
    sums_a, sums_b = tie(sums_a, sums_b)
    sums_a = lax.all_to_all(sums_a, COL, 0, 0)

    args = (ids, sums_b, jnp.stack([mean_b, inv_b]), view_b, up_b, other_a)
    grad_b = vmem_call(finish_second_kernel, jax.ShapeDtypeStruct((256, 1024), f32), args, "finish_second", 1 << 20)
    grad_a, loss_value = finish_first(ids, sums_a, jnp.stack([mean_a, inv_a]), view_a, up_own, block)
    return (loss_value[0, 0], grad_a, grad_b)


def solution(mesh):
    fine = Mesh(mesh.devices.reshape((2,) * 7), NAMES)
    return jax.shard_map(
        local,
        mesh=fine,
        in_specs=(P(COL, ROW), P(ROW, COL)),
        out_specs=(P(), P(COL, ROW), P(ROW, COL)),
        check_vma=False,
    )
```

```python
import functools

import jax
import jax.numpy as jnp
from jax import lax
from jax.experimental import pallas as pl
from jax.experimental.pallas import tpu as pltpu
from jax.sharding import Mesh, PartitionSpec as P

FEAT = 16384
BATCH = 2048

off_weight = 0.0051
eps_value = 1e-05

f32 = jnp.float32
bf16 = jnp.bfloat16

NAMES = ("y1", "y0", "xh", "xl", "z1", "z0", "k")
ROW = ("y1", "y0", "xh")
COL = ("xl", "z1", "z0", "k")
SWAP = [(0, 1), (1, 0)]
AHEAD = [(i, (i + 1) % 4) for i in range(4)]
BACK = [(i, (i + 3) % 4) for i in range(4)]


TURN_A = (((0, 1, 0), (1, 0, 0), (1, 0, 1)), ((0, 1, 0, 1), (1, 1, 1, 0), (0, 1, 0, 1)))
TURN_B = ((((0, 0, 1), (0, 1, 0), (1, 0, 0)), ((0, 1, 1, 1), (1, 0, 1, 1), (1, 0, 1, 0))),) * 2


def spread(x, axes, n):
    return lax.all_to_all(jnp.broadcast_to(x[None], (n,) + x.shape), axes, 0, 0)


def bits(n):
    return [(n >> s) & 1 for s in range(6, -1, -1)]


def number(p):
    return sum(v << s for v, s in zip(p, range(6, -1, -1)))


def turned(first, second, rows):
    matrix, shift = rows
    out = []
    for m, v in zip(matrix, shift):
        out.append((sum(a * b for a, b in zip(m, first)) + sum(a * b for a, b in zip(v, second))) % 2)
    return out


def crossing_tables():
    pairs_a, wanted_a = [], [[0, 0, 0]] * 128
    pairs_b, wanted_b = [[], []], [[0] * 8 for _ in range(128)]
    for target in range(128):
        y1, y0, xh, xl, z1, z0, k = bits(target)
        g = turned((y1, y0, xh), (xl, z1, z0, k), TURN_A)
        source = number((xl, z1, z0, k, g[0], g[1], g[2]))
        pairs_a.append((source, target))
        wanted_a[source] = [y0, xh, y1]
        for step in range(2):
            g = turned((xl, z1, z0), (y1, y0, xh, k), TURN_B[step])
            source = number((g[0], g[1], g[2], y1, y0, xh, k ^ step))
            pairs_b[step].append((source, target))
            wanted_b[source][4 * step : 4 * step + 4] = [xl, z1, z0, k]
    return pairs_a, wanted_a, pairs_b, wanted_b


def finish_stats(sums, count, view):
    mean = sums[0] / count
    inv = lax.rsqrt(sums[1] / count - mean * mean + eps_value)
    return ((view - mean) * inv, mean, inv)


def stats(view):
    return jnp.stack([jnp.sum(view, axis=0), jnp.sum(view * view, axis=0)])


def dot(x, y, dims):
    return lax.dot_general(x, y, (dims, ((), ())), preferred_element_type=f32)


def pick(x, index):
    return lax.dynamic_index_in_dim(x, index, 0, keepdims=False)


def both(which, mine, other, axis):
    return jnp.concatenate([jnp.where(which == 0, mine, other), jnp.where(which == 0, other, mine)], axis=axis)


def tie(*xs):
    return lax.optimization_barrier(xs)


def ring_near(own, ring):
    return [lax.ppermute(own, ring, AHEAD), lax.ppermute(own, ring, BACK)]


def trade(blocks, axis):
    return [lax.ppermute(x, axis, SWAP) for x in blocks]


OFFSETS = (0, 3, 1, 2)


def places(ids):
    return [((ids[0] + offset) & 3, ids[1] ^ flip) for flip in range(2) for offset in OFFSETS]


def gram_kernel(first, ids, *refs):
    if first:
        out, send, held, sems = refs[8:]
    else:
        mine, give, *sends, held, sems = refs[8:]
    copies = []
    for i, ref in enumerate(refs[:8]):
        slot = held.at[i // 4, pl.ds(256 * (i % 4), 256), :]
        copies.append(pltpu.make_async_copy(ref, slot, sems.at[i]))
        copies[-1].start()
    copies[0].wait()
    own = held[0, 0:256, :].T
    for flip in range(2):
        for index in range(4 * flip, 4 * flip + 4):
            if index:
                copies[index].wait()
        prod = dot(held[flip], own, ((1,), (0,))).astype(bf16)
        for index in range(4 * flip, 4 * flip + 4):
            p, k = places(ids)[index]
            high, low = p >> 1, p & 1
            for s in range(2):
                at = 256 * (index % 4) + 128 * s
                part = prod[at : at + 128]
                if first:
                    rows = pl.ds(pl.multiple_of(128 * k, 128), 128)
                    for half in range(2):
                        out[2 * (2 * s + high) + low, half, rows, :] = part[:, 128 * half : 128 * (half + 1)]
                    wanted = (high == ids[2]) & (low == ids[3]) & (s == ids[4])

                    @pl.when(wanted)
                    def _():
                        send[k] = held[flip, at : at + 128, :]

                else:

                    @pl.when(ids[10] == s)
                    def _():
                        mine[2 * p + k] = part

                    @pl.when(ids[10] != s)
                    def _():
                        give[2 * p + k] = part

                    for step in range(2):
                        place = [ids[2 + 4 * step + j] for j in range(4)]
                        wanted = (high == place[0]) & (low == place[1]) & (k == place[2]) & (s == place[3])

                        @pl.when(wanted)
                        def _():
                            if step == 0:
                                sends[0][...] = held[flip, at : at + 64, :]
                                sends[1][...] = held[flip, at + 64 : at + 128, :]
                            else:
                                sends[2][...] = held[flip, at : at + 128, :]


def call(kernel, out_shape, extra, name, space=pltpu.VMEM, scratch=(), flops=2 * 256 * 2048 * 1024):
    vmem = pl.BlockSpec(memory_space=pltpu.VMEM)
    return pl.pallas_call(
        kernel,
        out_shape=out_shape,
        in_specs=[pl.BlockSpec(memory_space=pltpu.SMEM)] + [vmem] * extra + [pl.BlockSpec(memory_space=space)] * 8,
        out_specs=[vmem] * len(out_shape),
        scratch_shapes=list(scratch),
        compiler_params=pltpu.CompilerParams(vmem_limit_bytes=14 * 1024 * 1024),
        cost_estimate=pl.CostEstimate(flops=flops, bytes_accessed=flops >> 8, transcendentals=0),
        name=name,
    )


def gram_part(first, ids, blocks):
    if first:
        shapes = [(8, 2, 256, 128), (2, 128, 1024)]
    else:
        shapes = [(8, 128, 256), (8, 128, 256), (64, 1024), (64, 1024), (128, 1024)]
    out = [jax.ShapeDtypeStruct(shape, bf16) for shape in shapes]
    scratch = [pltpu.VMEM((2, 1024, 1024), bf16), pltpu.SemaphoreType.DMA((8,))]
    flops = 2 * 256 * 2048 * 1024 if first else 1 << 20
    return call(functools.partial(gram_kernel, first), out, 0, "gram_part", pl.ANY, scratch, flops)(ids, *blocks)


def blend_kernel(mine, traded, received, out, held_mine, held_traded, held, sems):
    pairs = ((received, held), (mine, held_mine), (traded, held_traded))
    copies = [pltpu.make_async_copy(ref, slot, sems.at[i]) for i, (ref, slot) in enumerate(pairs)]
    for copy in copies:
        copy.start()
    copies[0].wait()
    piece = held[0].astype(f32)
    for i in range(1, 16):
        piece = piece + held[i].astype(f32)
    piece = piece.astype(bf16)
    for copy in copies[1:]:
        copy.wait()
    for i in range(8):
        out[i, 0:128] = (held_mine[i].astype(f32) + held_traded[i].astype(f32)).astype(bf16)
        out[i, 128:256, 0:128] = piece[0:128]
        out[i, 128:256, 128:256] = piece[128:256]


def blend(mine, traded, received):
    return pl.pallas_call(
        blend_kernel,
        out_shape=jax.ShapeDtypeStruct((8, 256, 256), bf16),
        in_specs=[pl.BlockSpec(memory_space=pl.ANY)] * 3,
        out_specs=pl.BlockSpec(memory_space=pltpu.VMEM),
        scratch_shapes=[pltpu.VMEM(x.shape, bf16) for x in (mine, traded, received)] + [pltpu.SemaphoreType.DMA((3,))],
        compiler_params=pltpu.CompilerParams(vmem_limit_bytes=14 * 1024 * 1024),
        cost_estimate=pl.CostEstimate(flops=1 << 20, bytes_accessed=4 << 20, transcendentals=0),
        name="blend",
    )(mine, traded, received)


def apply(part, blocks, ids):
    out = None
    for ref, (p, k) in zip(blocks, places(ids)):
        left = jnp.concatenate([part(p >> 1, p & 1, k, s) for s in range(2)], axis=1)
        prod = dot(left, ref[...], ((1,), (0,)))
        out = prod if out is None else out + prod
    return out * (2.0 * off_weight / BATCH)


def image_sum(x):
    return jnp.sum(x, axis=0, keepdims=True)


def split(x):
    high = x.astype(bf16).astype(f32)
    return [high, x - high]


def second_kernel(ids, mixed, traded, partner, *refs):
    blocks, up, out = refs[:8], refs[8], refs[9]

    def part(high, low, k, s):
        index = 4 * high + 2 * low + k
        rows = jnp.where(ids[10] == s, mixed[index, 128:256, :], traded[index])
        return jnp.concatenate([rows[:, 0:128], rows[:, 128:256]], axis=0)

    piece = mixed[0, 0:128].astype(f32)
    for i in range(1, 8):
        piece = piece + mixed[i, 0:128].astype(f32)
    piece = piece.astype(bf16)
    for i in range(16):
        out[i, 0:128] = piece
    value = apply(part, blocks, ids)
    up[...] = value
    norm = blocks[0][...].astype(f32)
    sums = [image_sum(value), partner[0:1], image_sum(norm), jnp.zeros((1, 1024), f32)]
    sums += split(image_sum(value * norm)) + split(partner[1:2])
    row = lax.broadcasted_iota(jnp.int32, (8, 1024), 0)
    rows = jnp.zeros((8, 1024), f32)
    for i in range(8):
        rows = jnp.where(row == i, sums[i], rows)
    rows = jnp.concatenate([rows[:, 256 * i : 256 * (i + 1)] for i in range(4)], axis=0).astype(bf16)
    for i in range(16):
        out[i, 128:160] = rows


def second_view(ids, mixed, traded, partner, blocks):
    out = [jax.ShapeDtypeStruct((256, 1024), f32), jax.ShapeDtypeStruct((16, 160, 256), bf16)]
    return call(second_kernel, out, 3, "second_view")(ids, mixed, traded, partner, *blocks)


def first_kernel(ids, last, *refs):
    blocks, (keep, give, out, second_sums) = refs[:8], refs[8:]

    def part(high, low, k, s):
        at = pl.ds(pl.multiple_of(k * 128, 128), 128)
        index = 4 * (2 * s + high) + 2 * low
        return jnp.concatenate([last[index, 0:128, at], last[index + 1, 0:128, at]], axis=0)

    value = apply(part, blocks, ids)
    side = ids[5]
    keep[...] = jnp.where(side == 0, value[0:128], value[128:256])
    give[...] = jnp.where(side == 0, value[128:256], value[0:128]).astype(bf16)
    sums = [image_sum(value), image_sum(value * blocks[0][...].astype(f32))]
    terms = None
    for i in range(8):
        term = last[2 * i + side, 128:160].astype(f32)
        terms = term if terms is None else terms + term
    second_sums[...] = terms
    row = lax.broadcasted_iota(jnp.int32, (32, 256), 0) % 8
    loss = image_sum(jnp.where((row == 4) | (row == 5), terms, 0.0)) / (2.0 * BATCH)
    products = []
    for j in range(4):
        products.append(terms[8 * j + 6 : 8 * j + 7] + terms[8 * j + 7 : 8 * j + 8])
        corr = products[-1] / BATCH
        miss = 1.0 - corr
        loss = loss + miss * miss - off_weight * corr * corr
    sums.append(jnp.concatenate([loss, jnp.zeros((1, 768), f32)], axis=1))
    sums.append(jnp.concatenate([terms[8 * j + 2 : 8 * j + 3] for j in range(4)], axis=1))
    sums.append(jnp.concatenate(products, axis=1))
    for i in range(16):
        for j in range(5):
            out[i, j : j + 1, :] = sums[j]


def first_view(ids, last, blocks):
    out = [
        jax.ShapeDtypeStruct((128, 1024), f32),
        jax.ShapeDtypeStruct((128, 1024), bf16),
        jax.ShapeDtypeStruct((16, 5, 1024), f32),
        jax.ShapeDtypeStruct((32, 256), f32),
    ]
    return call(first_kernel, out, 1, "first_view", flops=1 << 20)(ids, last, *blocks)


def finish(up, up_norm, partner, partner_norm, count):
    corr = partner_norm / count
    diag = -2.0 * (1.0 - corr) - 2.0 * off_weight * corr
    return diag, (up + diag * partner) / count, (up_norm + diag * partner_norm) / count


def vmem_call(kernel, out_shape, args, name, flops):
    vmem = pl.BlockSpec(memory_space=pltpu.VMEM)
    smem = pl.BlockSpec(memory_space=pltpu.SMEM)
    return pl.pallas_call(
        kernel,
        out_shape=out_shape,
        in_specs=[smem] + [vmem] * (len(args) - 1),
        out_specs=jax.tree.map(lambda _: vmem, out_shape),
        compiler_params=pltpu.CompilerParams(vmem_limit_bytes=14 * 1024 * 1024),
        cost_estimate=pl.CostEstimate(flops=flops, bytes_accessed=1 << 16, transcendentals=0),
        name=name,
    )(*args)


def partner_kernel(ids, other, half, out):
    other = other[...].astype(f32)
    out[0:1, :] = image_sum(other)
    out[1:2, :] = image_sum(other * half[...].astype(f32))


def arrange_kernel(ids, early, mid, late, keep, traded, block, up):
    for half in range(2):
        columns = slice(1024 * half, 1024 * (half + 1))
        block[0:64, columns] = jnp.where(ids[1] == half, early[...], late[0:64])
        block[64:128, columns] = jnp.where(ids[1] == half, mid[...], late[64:128])
        up[:, columns] = jnp.where(ids[0] == half, keep[...], traded[...].astype(f32))


def finish_second_kernel(ids, terms, scales, view, up, partner, grad):
    for part in range(4):
        columns = slice(256 * part, 256 * (part + 1))
        rows = [terms[8 * part + i : 8 * part + i + 1] for i in range(8)]
        diag, first, second = finish(rows[0], rows[4] + rows[5], rows[1], rows[6] + rows[7], BATCH)
        mean, inv = scales[0:1, columns], scales[1:2, columns]
        norm = (view[:, columns] - mean) * inv
        grad[:, columns] = inv * (up[:, columns] + diag * partner[:, columns].astype(f32) - first - norm * second)


def finish_kernel(ids, sums, scales, view, up, block, grad, loss):
    row = ids[2]
    loss[0, 0] = jnp.sum(sums[:, 2, :]) / FEAT
    for half in range(2):
        columns = slice(1024 * half, 1024 * (half + 1))
        total = sums[8 * half]
        for i in range(1, 8):
            total = total + sums[8 * half + i]
        partner = sums[2 * row + half]
        diag, first, second = finish(total[0:1], total[1:2], partner[3:4], partner[4:5], BATCH)
        mean, inv = scales[0:1, columns], scales[1:2, columns]
        norm = (view[:, columns] - mean) * inv
        grad[:, columns] = inv * (up[:, columns] + diag * block[:, columns].astype(f32) - first - norm * second)


def finish_first(ids, *args):
    vmem = pl.BlockSpec(memory_space=pltpu.VMEM)
    smem = pl.BlockSpec(memory_space=pltpu.SMEM)
    return pl.pallas_call(
        finish_kernel,
        out_shape=[jax.ShapeDtypeStruct((128, 2048), f32), jax.ShapeDtypeStruct((1, 1), f32)],
        in_specs=[smem] + [vmem] * len(args),
        out_specs=[vmem, smem],
        compiler_params=pltpu.CompilerParams(vmem_limit_bytes=14 * 1024 * 1024),
        cost_estimate=pl.CostEstimate(flops=1 << 20, bytes_accessed=1 << 16, transcendentals=0),
        name="finish_first",
    )(ids, *args)


def row_sum(x):
    x = x + sum(lax.ppermute(x, ("y1", "y0"), [(i, (i + step) % 4) for i in range(4)]) for step in (1, 2, 3))
    return x + lax.ppermute(x, "xh", SWAP)


def local(view_a, view_b):
    count = BATCH
    core = lax.axis_index("k")
    xl = lax.axis_index("xl")
    device = lax.axis_index(ROW + COL)
    pairs_a, wanted_a, pairs_b, wanted_b = crossing_tables()
    ids_a = jnp.concatenate([jnp.stack([lax.axis_index(("z1", "z0")), core]), jnp.array(wanted_a)[device], xl[None]])
    ids_b = jnp.concatenate([jnp.stack([lax.axis_index(("y1", "y0")), lax.axis_index("xh")]), jnp.array(wanted_b)[device], core[None]])

    stats_a, late_b = tie(stats(view_a), view_b)
    norm_a, mean_a, inv_a = finish_stats(jnp.sum(spread(stats_a, COL, 16), axis=0), count, view_a)
    norm_b, mean_b, inv_b = finish_stats(row_sum(stats(late_b)), count, view_b)
    half_a = norm_a.astype(bf16)
    half_b = norm_b.astype(bf16)

    zs, ys = ("z1", "z0"), ("y1", "y0")
    parts_a = jnp.transpose(half_a.reshape(128, 2, 1024), (1, 0, 2))
    own_a = both(xl, pick(parts_a, xl), lax.ppermute(pick(parts_a, 1 - xl), "xl", SWAP), 0)
    near_b = ring_near(half_b, ys)
    own_a, late_half_b = tie(own_a, half_b)
    near_a = ring_near(own_a, zs)
    other_own_a = trade([own_a], "k")
    other_own_b = trade([late_half_b], "xh")
    *near_a, near_b[0], near_b[1], other_own_b[0] = tie(*near_a, *near_b, *other_own_b)
    far_pairs = [(2 * i + k, 2 * ((i + (3 if k else 1)) % 4) + k) for i in range(4) for k in range(2)]
    far_a = lax.ppermute(jnp.where(core == 0, near_a[0], near_a[1]), zs + ("k",), far_pairs)
    other_near_a = trade(near_a, "k")
    other_near_b = ring_near(other_own_b[0], ys)
    far_b = lax.ppermute(near_b[0], ys, AHEAD)
    other_far_a, *other_near_b = tie(*trade([far_a], "k"), *other_near_b)
    other_far_b = lax.ppermute(other_near_b[1], ys, BACK)
    blocks_a = [own_a, *near_a, far_a, *other_own_a, *other_near_a, other_far_a]

    part_a, send_a = gram_part(True, ids_a, blocks_a)
    send_a, far_b, other_far_b = tie(send_a, far_b, other_far_b)
    blocks_b = [half_b, *near_b, far_b, *other_own_b, *other_near_b, other_far_b]
    other_a = lax.ppermute(send_a.reshape(256, 1024), ROW + COL, pairs_a)
    piece_a = lax.all_to_all(part_a.reshape(16, 256, 128), ("y1", "y0", "xh", "xl"), 0, 0)
    mine_b, give_b, *send_b = gram_part(False, ids_b, blocks_b)
    mixed = blend(mine_b, lax.ppermute(give_b, "k", SWAP), piece_a)
    ids = jnp.stack([xl, core, lax.axis_index(ROW)])
    partner = vmem_call(partner_kernel, jax.ShapeDtypeStruct((2, 1024), f32), (ids, other_a, half_b), "partner", 1 << 34)
    mixed, partner = tie(mixed, partner)
    early = lax.ppermute(send_b[0], ROW + COL, pairs_b[0])
    mixed = lax.all_to_all(mixed, ("xl", "z1", "z0"), 0, 0)

    mixed, early, mid = tie(mixed, early, send_b[1])
    mid = lax.ppermute(mid, ROW + COL, pairs_b[0])
    traded = lax.ppermute(mixed[:, 128:], "k", SWAP)
    up_b, last = second_view(ids_b, mixed, traded, partner, blocks_b)
    last, mid = tie(last, mid)
    last = lax.all_to_all(last, ("y1", "y0", "xh", "xl"), 0, 0)
    last, late = tie(last, send_b[2])
    late = lax.ppermute(late, ROW + COL, pairs_b[1])

    keep, give, sums_a, sums_b = first_view(ids_a, last, blocks_a)
    traded = lax.ppermute(give, "xl", SWAP)
    out = [jax.ShapeDtypeStruct((128, 2048), bf16), jax.ShapeDtypeStruct((128, 2048), f32)]
    block, up_own = vmem_call(arrange_kernel, out, (ids, early, mid, late, keep, traded), "arrange", 1 << 34)
    sums_a, sums_b = tie(sums_a, sums_b)
    sums_a = lax.all_to_all(sums_a, COL, 0, 0)

    args = (ids, sums_b, jnp.stack([mean_b, inv_b]), view_b, up_b, other_a)
    grad_b = vmem_call(finish_second_kernel, jax.ShapeDtypeStruct((256, 1024), f32), args, "finish_second", 1 << 20)
    grad_a, loss_value = finish_first(ids, sums_a, jnp.stack([mean_a, inv_a]), view_a, up_own, block)
    return (loss_value[0, 0], grad_a, grad_b)


def solution(mesh):
    fine = Mesh(mesh.devices.reshape((2,) * 7), NAMES)
    return jax.shard_map(
        local,
        mesh=fine,
        in_specs=(P(COL, ROW), P(ROW, COL)),
        out_specs=(P(), P(COL, ROW), P(ROW, COL)),
        check_vma=False,
    )
```

```python
import functools

import jax
import jax.numpy as jnp
from jax import lax
from jax.experimental import pallas as pl
from jax.experimental.pallas import tpu as pltpu
from jax.sharding import Mesh, PartitionSpec as P

FEAT = 16384
BATCH = 2048

off_weight = 0.0051
eps_value = 1e-05

f32 = jnp.float32
bf16 = jnp.bfloat16

NAMES = ("y1", "y0", "xh", "xl", "z1", "z0", "k")
ROW = ("y1", "y0", "xh")
COL = ("xl", "z1", "z0", "k")
SWAP = [(0, 1), (1, 0)]
AHEAD = [(i, (i + 1) % 4) for i in range(4)]
BACK = [(i, (i + 3) % 4) for i in range(4)]


TURN_A = (((0, 1, 0), (1, 0, 0), (1, 0, 1)), ((0, 1, 0, 1), (1, 1, 1, 0), (0, 1, 0, 1)))
TURN_B = ((((0, 0, 1), (0, 1, 0), (1, 0, 0)), ((0, 1, 1, 1), (1, 0, 1, 1), (1, 0, 1, 0))),) * 2


def spread(x, axes, n):
    return lax.all_to_all(jnp.broadcast_to(x[None], (n,) + x.shape), axes, 0, 0)


def bits(n):
    return [(n >> s) & 1 for s in range(6, -1, -1)]


def number(p):
    return sum(v << s for v, s in zip(p, range(6, -1, -1)))


def turned(first, second, rows):
    matrix, shift = rows
    out = []
    for m, v in zip(matrix, shift):
        out.append((sum(a * b for a, b in zip(m, first)) + sum(a * b for a, b in zip(v, second))) % 2)
    return out


def crossing_tables():
    pairs_a, wanted_a = [], [[0, 0, 0]] * 128
    pairs_b, wanted_b = [[], []], [[0] * 8 for _ in range(128)]
    for target in range(128):
        y1, y0, xh, xl, z1, z0, k = bits(target)
        g = turned((y1, y0, xh), (xl, z1, z0, k), TURN_A)
        source = number((xl, z1, z0, k, g[0], g[1], g[2]))
        pairs_a.append((source, target))
        wanted_a[source] = [y0, xh, y1]
        for step in range(2):
            g = turned((xl, z1, z0), (y1, y0, xh, k), TURN_B[step])
            source = number((g[0], g[1], g[2], y1, y0, xh, k ^ step))
            pairs_b[step].append((source, target))
            wanted_b[source][4 * step : 4 * step + 4] = [xl, z1, z0, k]
    return pairs_a, wanted_a, pairs_b, wanted_b


def finish_stats(sums, count, view):
    mean = sums[0] / count
    inv = lax.rsqrt(sums[1] / count - mean * mean + eps_value)
    return ((view - mean) * inv, mean, inv)


def stats(view):
    return jnp.stack([jnp.sum(view, axis=0), jnp.sum(view * view, axis=0)])


def dot(x, y, dims):
    return lax.dot_general(x, y, (dims, ((), ())), preferred_element_type=f32)


def pick(x, index):
    return lax.dynamic_index_in_dim(x, index, 0, keepdims=False)


def both(which, mine, other, axis):
    return jnp.concatenate([jnp.where(which == 0, mine, other), jnp.where(which == 0, other, mine)], axis=axis)


def tie(*xs):
    return lax.optimization_barrier(xs)


def ring_near(own, ring):
    return [lax.ppermute(own, ring, AHEAD), lax.ppermute(own, ring, BACK)]


def trade(blocks, axis):
    return [lax.ppermute(x, axis, SWAP) for x in blocks]


OFFSETS = (0, 3, 1, 2)


def places(ids):
    return [((ids[0] + offset) & 3, ids[1] ^ flip) for flip in range(2) for offset in OFFSETS]


def gram_kernel(first, ids, *refs):
    if first:
        out, send, held, sems = refs[8:]
    else:
        mine, give, *sends, held, sems = refs[8:]
    copies = []
    for i, ref in enumerate(refs[:8]):
        slot = held.at[i // 4, pl.ds(256 * (i % 4), 256), :]
        copies.append(pltpu.make_async_copy(ref, slot, sems.at[i]))
        copies[-1].start()
    copies[0].wait()
    own = held[0, 0:256, :].T
    for flip in range(2):
        for index in range(4 * flip, 4 * flip + 4):
            if index:
                copies[index].wait()
        prod = dot(held[flip], own, ((1,), (0,))).astype(bf16)
        for index in range(4 * flip, 4 * flip + 4):
            p, k = places(ids)[index]
            high, low = p >> 1, p & 1
            for s in range(2):
                at = 256 * (index % 4) + 128 * s
                part = prod[at : at + 128]
                if first:
                    rows = pl.ds(pl.multiple_of(128 * k, 128), 128)
                    for half in range(2):
                        out[2 * (2 * s + high) + low, half, rows, :] = part[:, 128 * half : 128 * (half + 1)]
                    wanted = (high == ids[2]) & (low == ids[3]) & (s == ids[4])

                    @pl.when(wanted)
                    def _():
                        send[k] = held[flip, at : at + 128, :]

                else:

                    @pl.when(ids[10] == s)
                    def _():
                        mine[2 * p + k] = part

                    @pl.when(ids[10] != s)
                    def _():
                        give[2 * p + k] = part

                    for step in range(2):
                        place = [ids[2 + 4 * step + j] for j in range(4)]
                        wanted = (high == place[0]) & (low == place[1]) & (k == place[2]) & (s == place[3])

                        @pl.when(wanted)
                        def _():
                            sends[step][...] = held[flip, at : at + 128, :]


def call(kernel, out_shape, extra, name, space=pltpu.VMEM, scratch=(), flops=2 * 256 * 2048 * 1024):
    vmem = pl.BlockSpec(memory_space=pltpu.VMEM)
    return pl.pallas_call(
        kernel,
        out_shape=out_shape,
        in_specs=[pl.BlockSpec(memory_space=pltpu.SMEM)] + [vmem] * extra + [pl.BlockSpec(memory_space=space)] * 8,
        out_specs=[vmem] * len(out_shape),
        scratch_shapes=list(scratch),
        compiler_params=pltpu.CompilerParams(vmem_limit_bytes=14 * 1024 * 1024),
        cost_estimate=pl.CostEstimate(flops=flops, bytes_accessed=flops >> 8, transcendentals=0),
        name=name,
    )


def gram_part(first, ids, blocks):
    if first:
        shapes = [(8, 2, 256, 128), (2, 128, 1024)]
    else:
        shapes = [(8, 128, 256), (8, 128, 256), (128, 1024), (128, 1024)]
    out = [jax.ShapeDtypeStruct(shape, bf16) for shape in shapes]
    scratch = [pltpu.VMEM((2, 1024, 1024), bf16), pltpu.SemaphoreType.DMA((8,))]
    flops = 2 * 256 * 2048 * 1024 if first else 1 << 20
    return call(functools.partial(gram_kernel, first), out, 0, "gram_part", pl.ANY, scratch, flops)(ids, *blocks)


def blend_kernel(mine, traded, received, out, held_mine, held_traded, held, sems):
    pairs = ((received, held), (mine, held_mine), (traded, held_traded))
    copies = [pltpu.make_async_copy(ref, slot, sems.at[i]) for i, (ref, slot) in enumerate(pairs)]
    for copy in copies:
        copy.start()
    copies[0].wait()
    piece = held[0].astype(f32)
    for i in range(1, 16):
        piece = piece + held[i].astype(f32)
    piece = piece.astype(bf16)
    for copy in copies[1:]:
        copy.wait()
    for i in range(8):
        out[i, 0:128] = (held_mine[i].astype(f32) + held_traded[i].astype(f32)).astype(bf16)
        out[i, 128:256, 0:128] = piece[0:128]
        out[i, 128:256, 128:256] = piece[128:256]


def blend(mine, traded, received):
    return pl.pallas_call(
        blend_kernel,
        out_shape=jax.ShapeDtypeStruct((8, 256, 256), bf16),
        in_specs=[pl.BlockSpec(memory_space=pl.ANY)] * 3,
        out_specs=pl.BlockSpec(memory_space=pltpu.VMEM),
        scratch_shapes=[pltpu.VMEM(x.shape, bf16) for x in (mine, traded, received)] + [pltpu.SemaphoreType.DMA((3,))],
        compiler_params=pltpu.CompilerParams(vmem_limit_bytes=14 * 1024 * 1024),
        cost_estimate=pl.CostEstimate(flops=1 << 20, bytes_accessed=4 << 20, transcendentals=0),
        name="blend",
    )(mine, traded, received)


def apply(part, blocks, ids):
    out = None
    for ref, (p, k) in zip(blocks, places(ids)):
        left = jnp.concatenate([part(p >> 1, p & 1, k, s) for s in range(2)], axis=1)
        prod = dot(left, ref[...], ((1,), (0,)))
        out = prod if out is None else out + prod
    return out * (2.0 * off_weight / BATCH)


def image_sum(x):
    return jnp.sum(x, axis=0, keepdims=True)


def split(x):
    high = x.astype(bf16).astype(f32)
    return [high, x - high]


def second_kernel(ids, mixed, traded, partner, *refs):
    blocks, up, out = refs[:8], refs[8], refs[9]

    def part(high, low, k, s):
        index = 4 * high + 2 * low + k
        rows = jnp.where(ids[10] == s, mixed[index, 128:256, :], traded[index])
        return jnp.concatenate([rows[:, 0:128], rows[:, 128:256]], axis=0)

    piece = mixed[0, 0:128].astype(f32)
    for i in range(1, 8):
        piece = piece + mixed[i, 0:128].astype(f32)
    piece = piece.astype(bf16)
    for i in range(16):
        out[i, 0:128] = piece
    value = apply(part, blocks, ids)
    up[...] = value
    norm = blocks[0][...].astype(f32)
    sums = [image_sum(value), partner[0:1], image_sum(norm), jnp.zeros((1, 1024), f32)]
    sums += split(image_sum(value * norm)) + split(partner[1:2])
    row = lax.broadcasted_iota(jnp.int32, (8, 1024), 0)
    rows = jnp.zeros((8, 1024), f32)
    for i in range(8):
        rows = jnp.where(row == i, sums[i], rows)
    rows = jnp.concatenate([rows[:, 256 * i : 256 * (i + 1)] for i in range(4)], axis=0).astype(bf16)
    for i in range(16):
        out[i, 128:160] = rows


def second_view(ids, mixed, traded, partner, blocks):
    out = [jax.ShapeDtypeStruct((256, 1024), f32), jax.ShapeDtypeStruct((16, 160, 256), bf16)]
    return call(second_kernel, out, 3, "second_view")(ids, mixed, traded, partner, *blocks)


def first_kernel(ids, last, *refs):
    blocks, (keep, give, out, second_sums) = refs[:8], refs[8:]

    def part(high, low, k, s):
        at = pl.ds(pl.multiple_of(k * 128, 128), 128)
        index = 4 * (2 * s + high) + 2 * low
        return jnp.concatenate([last[index, 0:128, at], last[index + 1, 0:128, at]], axis=0)

    value = apply(part, blocks, ids)
    side = ids[5]
    keep[...] = jnp.where(side == 0, value[0:128], value[128:256])
    give[...] = jnp.where(side == 0, value[128:256], value[0:128]).astype(bf16)
    sums = [image_sum(value), image_sum(value * blocks[0][...].astype(f32))]
    terms = None
    for i in range(8):
        term = last[2 * i + side, 128:160].astype(f32)
        terms = term if terms is None else terms + term
    second_sums[...] = terms
    row = lax.broadcasted_iota(jnp.int32, (32, 256), 0) % 8
    loss = image_sum(jnp.where((row == 4) | (row == 5), terms, 0.0)) / (2.0 * BATCH)
    products = []
    for j in range(4):
        products.append(terms[8 * j + 6 : 8 * j + 7] + terms[8 * j + 7 : 8 * j + 8])
        corr = products[-1] / BATCH
        miss = 1.0 - corr
        loss = loss + miss * miss - off_weight * corr * corr
    sums.append(jnp.concatenate([loss, jnp.zeros((1, 768), f32)], axis=1))
    sums.append(jnp.concatenate([terms[8 * j + 2 : 8 * j + 3] for j in range(4)], axis=1))
    sums.append(jnp.concatenate(products, axis=1))
    for i in range(16):
        for j in range(5):
            out[i, j : j + 1, :] = sums[j]


def first_view(ids, last, blocks):
    out = [
        jax.ShapeDtypeStruct((128, 1024), f32),
        jax.ShapeDtypeStruct((128, 1024), bf16),
        jax.ShapeDtypeStruct((16, 5, 1024), f32),
        jax.ShapeDtypeStruct((32, 256), f32),
    ]
    return call(first_kernel, out, 1, "first_view", flops=1 << 20)(ids, last, *blocks)


def finish(up, up_norm, partner, partner_norm, count):
    corr = partner_norm / count
    diag = -2.0 * (1.0 - corr) - 2.0 * off_weight * corr
    return diag, (up + diag * partner) / count, (up_norm + diag * partner_norm) / count


def vmem_call(kernel, out_shape, args, name, flops):
    vmem = pl.BlockSpec(memory_space=pltpu.VMEM)
    smem = pl.BlockSpec(memory_space=pltpu.SMEM)
    return pl.pallas_call(
        kernel,
        out_shape=out_shape,
        in_specs=[smem] + [vmem] * (len(args) - 1),
        out_specs=jax.tree.map(lambda _: vmem, out_shape),
        compiler_params=pltpu.CompilerParams(vmem_limit_bytes=14 * 1024 * 1024),
        cost_estimate=pl.CostEstimate(flops=flops, bytes_accessed=1 << 16, transcendentals=0),
        name=name,
    )(*args)


def partner_kernel(ids, other, half, out):
    other = other[...].astype(f32)
    out[0:1, :] = image_sum(other)
    out[1:2, :] = image_sum(other * half[...].astype(f32))


def arrange_kernel(which, ids, same, other, out):
    for half in range(2):
        picked = jnp.where(ids[which] == half, same[...].astype(out.dtype), other[...].astype(out.dtype))
        out[:, 1024 * half : 1024 * (half + 1)] = picked


def finish_second_kernel(ids, terms, scales, view, up, partner, grad):
    for part in range(4):
        columns = slice(256 * part, 256 * (part + 1))
        rows = [terms[8 * part + i : 8 * part + i + 1] for i in range(8)]
        diag, first, second = finish(rows[0], rows[4] + rows[5], rows[1], rows[6] + rows[7], BATCH)
        mean, inv = scales[0:1, columns], scales[1:2, columns]
        norm = (view[:, columns] - mean) * inv
        grad[:, columns] = inv * (up[:, columns] + diag * partner[:, columns].astype(f32) - first - norm * second)


def finish_kernel(ids, sums, scales, view, up, block, grad, loss):
    row = ids[2]
    loss[0, 0] = jnp.sum(sums[:, 2, :]) / FEAT
    for half in range(2):
        columns = slice(1024 * half, 1024 * (half + 1))
        total = sums[8 * half]
        for i in range(1, 8):
            total = total + sums[8 * half + i]
        partner = sums[2 * row + half]
        diag, first, second = finish(total[0:1], total[1:2], partner[3:4], partner[4:5], BATCH)
        mean, inv = scales[0:1, columns], scales[1:2, columns]
        norm = (view[:, columns] - mean) * inv
        grad[:, columns] = inv * (up[:, columns] + diag * block[:, columns].astype(f32) - first - norm * second)


def finish_first(ids, *args):
    vmem = pl.BlockSpec(memory_space=pltpu.VMEM)
    smem = pl.BlockSpec(memory_space=pltpu.SMEM)
    return pl.pallas_call(
        finish_kernel,
        out_shape=[jax.ShapeDtypeStruct((128, 2048), f32), jax.ShapeDtypeStruct((1, 1), f32)],
        in_specs=[smem] + [vmem] * len(args),
        out_specs=[vmem, smem],
        compiler_params=pltpu.CompilerParams(vmem_limit_bytes=14 * 1024 * 1024),
        cost_estimate=pl.CostEstimate(flops=1 << 20, bytes_accessed=1 << 16, transcendentals=0),
        name="finish_first",
    )(ids, *args)


def row_sum(x):
    x = x + lax.ppermute(x, "xh", SWAP)
    return x + sum(lax.ppermute(x, ("y1", "y0"), [(i, (i + step) % 4) for i in range(4)]) for step in (1, 2, 3))


def vmem_call(kernel, out_shape, args, name, flops):
    vmem = pl.BlockSpec(memory_space=pltpu.VMEM)
    smem = pl.BlockSpec(memory_space=pltpu.SMEM)
    return pl.pallas_call(
        kernel,
        out_shape=out_shape,
        in_specs=[smem] + [vmem] * (len(args) - 1),
        out_specs=jax.tree.map(lambda _: vmem, out_shape),
        compiler_params=pltpu.CompilerParams(vmem_limit_bytes=14 * 1024 * 1024),
        cost_estimate=pl.CostEstimate(flops=flops, bytes_accessed=1 << 16, transcendentals=0),
        name=name,
    )(*args)


def partner_kernel(ids, other, half, out):
    other = other[...].astype(f32)
    out[0:1, :] = image_sum(other)
    out[1:2, :] = image_sum(other * half[...].astype(f32))


def arrange_kernel(which, ids, same, other, out):
    for half in range(2):
        picked = jnp.where(ids[which] == half, same[...].astype(out.dtype), other[...].astype(out.dtype))
        out[:, 1024 * half : 1024 * (half + 1)] = picked


def finish_second_kernel(ids, terms, scales, view, up, partner, grad):
    for part in range(4):
        columns = slice(256 * part, 256 * (part + 1))
        rows = [terms[8 * part + i : 8 * part + i + 1] for i in range(8)]
        diag, first, second = finish(rows[0], rows[4] + rows[5], rows[1], rows[6] + rows[7], BATCH)
        mean, inv = scales[0:1, columns], scales[1:2, columns]
        norm = (view[:, columns] - mean) * inv
        grad[:, columns] = inv * (up[:, columns] + diag * partner[:, columns].astype(f32) - first - norm * second)


def finish_kernel(ids, sums, scales, view, up, block, grad, loss):
    row = ids[2]
    loss[0, 0] = jnp.sum(sums[:, 2, :]) / FEAT
    for half in range(2):
        columns = slice(1024 * half, 1024 * (half + 1))
        total = sums[8 * half]
        for i in range(1, 8):
            total = total + sums[8 * half + i]
        partner = sums[2 * row + half]
        diag, first, second = finish(total[0:1], total[1:2], partner[3:4], partner[4:5], BATCH)
        mean, inv = scales[0:1, columns], scales[1:2, columns]
        norm = (view[:, columns] - mean) * inv
        grad[:, columns] = inv * (up[:, columns] + diag * block[:, columns].astype(f32) - first - norm * second)


def finish_first(ids, *args):
    vmem = pl.BlockSpec(memory_space=pltpu.VMEM)
    smem = pl.BlockSpec(memory_space=pltpu.SMEM)
    return pl.pallas_call(
        finish_kernel,
        out_shape=[jax.ShapeDtypeStruct((128, 2048), f32), jax.ShapeDtypeStruct((1, 1), f32)],
        in_specs=[smem] + [vmem] * len(args),
        out_specs=[vmem, smem],
        compiler_params=pltpu.CompilerParams(vmem_limit_bytes=14 * 1024 * 1024),
        cost_estimate=pl.CostEstimate(flops=1 << 20, bytes_accessed=1 << 16, transcendentals=0),
        name="finish_first",
    )(ids, *args)


def row_sum(x):
    x = x + sum(lax.ppermute(x, ("y1", "y0"), [(i, (i + step) % 4) for i in range(4)]) for step in (1, 2, 3))
    return x + lax.ppermute(x, "xh", SWAP)


def local(view_a, view_b):
    count = BATCH
    core = lax.axis_index("k")
    xl = lax.axis_index("xl")
    device = lax.axis_index(ROW + COL)
    pairs_a, wanted_a, pairs_b, wanted_b = crossing_tables()
    ids_a = jnp.concatenate([jnp.stack([lax.axis_index(("z1", "z0")), core]), jnp.array(wanted_a)[device], xl[None]])
    ids_b = jnp.concatenate([jnp.stack([lax.axis_index(("y1", "y0")), lax.axis_index("xh")]), jnp.array(wanted_b)[device], core[None]])

    stats_a, late_b = tie(stats(view_a), view_b)
    norm_a, mean_a, inv_a = finish_stats(jnp.sum(spread(stats_a, COL, 16), axis=0), count, view_a)
    norm_b, mean_b, inv_b = finish_stats(row_sum(stats(late_b)), count, view_b)
    half_a = norm_a.astype(bf16)
    half_b = norm_b.astype(bf16)

    zs, ys = ("z1", "z0"), ("y1", "y0")
    parts_a = jnp.transpose(half_a.reshape(128, 2, 1024), (1, 0, 2))
    own_a = both(xl, pick(parts_a, xl), lax.ppermute(pick(parts_a, 1 - xl), "xl", SWAP), 0)
    near_b = ring_near(half_b, ys)
    own_a, late_half_b = tie(own_a, half_b)
    near_a = ring_near(own_a, zs)
    other_own_a = trade([own_a], "k")
    other_own_b = trade([late_half_b], "xh")
    *near_a, near_b[0], near_b[1], other_own_b[0] = tie(*near_a, *near_b, *other_own_b)
    far_pairs = [(2 * i + k, 2 * ((i + (3 if k else 1)) % 4) + k) for i in range(4) for k in range(2)]
    far_a = lax.ppermute(jnp.where(core == 0, near_a[0], near_a[1]), zs + ("k",), far_pairs)
    other_near_a = trade(near_a, "k")
    other_near_b = ring_near(other_own_b[0], ys)
    far_b = lax.ppermute(near_b[0], ys, AHEAD)
    other_far_a, *other_near_b = tie(*trade([far_a], "k"), *other_near_b)
    other_far_b = lax.ppermute(other_near_b[1], ys, BACK)
    blocks_a = [own_a, *near_a, far_a, *other_own_a, *other_near_a, other_far_a]

    part_a, send_a = gram_part(True, ids_a, blocks_a)
    send_a, far_b, other_far_b = tie(send_a, far_b, other_far_b)
    blocks_b = [half_b, *near_b, far_b, *other_own_b, *other_near_b, other_far_b]
    other_a = lax.ppermute(send_a.reshape(256, 1024), ROW + COL, pairs_a)
    piece_a = lax.all_to_all(part_a.reshape(16, 256, 128), ("y1", "y0", "xh", "xl"), 0, 0)
    mine_b, give_b, *send_b = gram_part(False, ids_b, blocks_b)
    mixed = blend(mine_b, lax.ppermute(give_b, "k", SWAP), piece_a)
    ids = jnp.stack([xl, core, lax.axis_index(ROW)])
    partner = vmem_call(partner_kernel, jax.ShapeDtypeStruct((2, 1024), f32), (ids, other_a, half_b), "partner", 1 << 34)
    early = lax.ppermute(send_b[0], ROW + COL, pairs_b[0])
    mixed, partner, early = tie(mixed, partner, early)
    mixed = lax.all_to_all(mixed, ("xl", "z1", "z0"), 0, 0)

    traded = lax.ppermute(mixed[:, 128:], "k", SWAP)
    up_b, last = second_view(ids_b, mixed, traded, partner, blocks_b)
    last = lax.all_to_all(last, ("y1", "y0", "xh", "xl"), 0, 0)
    last, late = tie(last, send_b[1])
    late = lax.ppermute(late, ROW + COL, pairs_b[1])

    keep, give, sums_a, sums_b = first_view(ids_a, last, blocks_a)
    traded = lax.ppermute(give, "xl", SWAP)
    block = jax.ShapeDtypeStruct((128, 2048), bf16)
    block = vmem_call(functools.partial(arrange_kernel, 1), block, (ids, early, late), "arrange_block", 1 << 34)
    keep, block = tie(keep, block)
    up_own = jax.ShapeDtypeStruct((128, 2048), f32)
    up_own = vmem_call(functools.partial(arrange_kernel, 0), up_own, (ids, keep, traded), "arrange_up", 1 << 33)
    sums_a, sums_b = tie(sums_a, sums_b)
    sums_a = lax.all_to_all(sums_a, COL, 0, 0)

    args = (ids, sums_b, jnp.stack([mean_b, inv_b]), view_b, up_b, other_a)
    grad_b = vmem_call(finish_second_kernel, jax.ShapeDtypeStruct((256, 1024), f32), args, "finish_second", 1 << 20)
    grad_a, loss_value = finish_first(ids, sums_a, jnp.stack([mean_a, inv_a]), view_a, up_own, block)
    return (loss_value[0, 0], grad_a, grad_b)


def solution(mesh):
    fine = Mesh(mesh.devices.reshape((2,) * 7), NAMES)
    return jax.shard_map(
        local,
        mesh=fine,
        in_specs=(P(COL, ROW), P(ROW, COL)),
        out_specs=(P(), P(COL, ROW), P(ROW, COL)),
        check_vma=False,
    )
```

```python
import functools

import jax
import jax.numpy as jnp
from jax import lax
from jax.experimental import pallas as pl
from jax.experimental.pallas import tpu as pltpu
from jax.sharding import Mesh, PartitionSpec as P

FEAT = 16384
BATCH = 2048

off_weight = 0.0051
eps_value = 1e-05

f32 = jnp.float32
bf16 = jnp.bfloat16

NAMES = ("y1", "y0", "xh", "xl", "z1", "z0", "k")
ROW = ("y1", "y0", "xh")
COL = ("xl", "z1", "z0", "k")
SWAP = [(0, 1), (1, 0)]
AHEAD = [(i, (i + 1) % 4) for i in range(4)]
BACK = [(i, (i + 3) % 4) for i in range(4)]


TURN_A = (((0, 1, 0), (1, 0, 0), (1, 0, 1)), ((0, 1, 0, 1), (1, 1, 1, 0), (0, 1, 0, 1)))
TURN_B = ((((0, 0, 1), (0, 1, 0), (1, 0, 0)), ((0, 1, 1, 1), (1, 0, 1, 1), (1, 0, 1, 0))),) * 2


def spread(x, axes, n):
    return lax.all_to_all(jnp.broadcast_to(x[None], (n,) + x.shape), axes, 0, 0)


def bits(n):
    return [(n >> s) & 1 for s in range(6, -1, -1)]


def number(p):
    return sum(v << s for v, s in zip(p, range(6, -1, -1)))


def turned(first, second, rows):
    matrix, shift = rows
    out = []
    for m, v in zip(matrix, shift):
        out.append((sum(a * b for a, b in zip(m, first)) + sum(a * b for a, b in zip(v, second))) % 2)
    return out


def crossing_tables():
    pairs_a, wanted_a = [], [[0, 0, 0]] * 128
    pairs_b, wanted_b = [[], []], [[0] * 8 for _ in range(128)]
    for target in range(128):
        y1, y0, xh, xl, z1, z0, k = bits(target)
        g = turned((y1, y0, xh), (xl, z1, z0, k), TURN_A)
        source = number((xl, z1, z0, k, g[0], g[1], g[2]))
        pairs_a.append((source, target))
        wanted_a[source] = [y0, xh, y1]
        for step in range(2):
            g = turned((xl, z1, z0), (y1, y0, xh, k), TURN_B[step])
            source = number((g[0], g[1], g[2], y1, y0, xh, k ^ step))
            pairs_b[step].append((source, target))
            wanted_b[source][4 * step : 4 * step + 4] = [xl, z1, z0, k]
    return pairs_a, wanted_a, pairs_b, wanted_b


def finish_stats(sums, count, view):
    mean = sums[0] / count
    inv = lax.rsqrt(sums[1] / count - mean * mean + eps_value)
    return ((view - mean) * inv, mean, inv)


def stats(view):
    return jnp.stack([jnp.sum(view, axis=0), jnp.sum(view * view, axis=0)])


def dot(x, y, dims):
    return lax.dot_general(x, y, (dims, ((), ())), preferred_element_type=f32)


def pick(x, index):
    return lax.dynamic_index_in_dim(x, index, 0, keepdims=False)


def both(which, mine, other, axis):
    return jnp.concatenate([jnp.where(which == 0, mine, other), jnp.where(which == 0, other, mine)], axis=axis)


def tie(*xs):
    return lax.optimization_barrier(xs)


def ring_near(own, ring):
    return [lax.ppermute(own, ring, AHEAD), lax.ppermute(own, ring, BACK)]


def trade(blocks, axis):
    return [lax.ppermute(x, axis, SWAP) for x in blocks]


OFFSETS = (0, 3, 1, 2)


def places(ids):
    return [((ids[0] + offset) & 3, ids[1] ^ flip) for flip in range(2) for offset in OFFSETS]


def gram_kernel(first, ids, *refs):
    if first:
        out, send, held, sems = refs[8:]
    else:
        mine, give, *sends, held, sems = refs[8:]
    copies = []
    for i, ref in enumerate(refs[:8]):
        slot = held.at[i // 4, pl.ds(256 * (i % 4), 256), :]
        copies.append(pltpu.make_async_copy(ref, slot, sems.at[i]))
        copies[-1].start()
    copies[0].wait()
    own = held[0, 0:256, :].T
    for flip in range(2):
        for index in range(4 * flip, 4 * flip + 4):
            if index:
                copies[index].wait()
        prod = dot(held[flip], own, ((1,), (0,))).astype(bf16)
        for index in range(4 * flip, 4 * flip + 4):
            p, k = places(ids)[index]
            high, low = p >> 1, p & 1
            for s in range(2):
                at = 256 * (index % 4) + 128 * s
                part = prod[at : at + 128]
                if first:
                    rows = pl.ds(pl.multiple_of(128 * k, 128), 128)
                    for half in range(2):
                        out[2 * (2 * s + high) + low, half, rows, :] = part[:, 128 * half : 128 * (half + 1)]
                    wanted = (high == ids[2]) & (low == ids[3]) & (s == ids[4])

                    @pl.when(wanted)
                    def _():
                        send[k] = held[flip, at : at + 128, :]

                else:

                    @pl.when(ids[10] == s)
                    def _():
                        mine[2 * p + k] = part

                    @pl.when(ids[10] != s)
                    def _():
                        give[2 * p + k] = part

                    for step in range(2):
                        place = [ids[2 + 4 * step + j] for j in range(4)]
                        wanted = (high == place[0]) & (low == place[1]) & (k == place[2]) & (s == place[3])

                        @pl.when(wanted)
                        def _():
                            sends[step][...] = held[flip, at : at + 128, :]


def call(kernel, out_shape, extra, name, space=pltpu.VMEM, scratch=(), flops=2 * 256 * 2048 * 1024):
    vmem = pl.BlockSpec(memory_space=pltpu.VMEM)
    return pl.pallas_call(
        kernel,
        out_shape=out_shape,
        in_specs=[pl.BlockSpec(memory_space=pltpu.SMEM)] + [vmem] * extra + [pl.BlockSpec(memory_space=space)] * 8,
        out_specs=[vmem] * len(out_shape),
        scratch_shapes=list(scratch),
        compiler_params=pltpu.CompilerParams(vmem_limit_bytes=14 * 1024 * 1024),
        cost_estimate=pl.CostEstimate(flops=flops, bytes_accessed=flops >> 8, transcendentals=0),
        name=name,
    )


def gram_part(first, ids, blocks):
    if first:
        shapes = [(8, 2, 256, 128), (2, 128, 1024)]
    else:
        shapes = [(8, 128, 256), (8, 128, 256), (128, 1024), (128, 1024)]
    out = [jax.ShapeDtypeStruct(shape, bf16) for shape in shapes]
    scratch = [pltpu.VMEM((2, 1024, 1024), bf16), pltpu.SemaphoreType.DMA((8,))]
    flops = 2 * 256 * 2048 * 1024 if first else 1 << 20
    return call(functools.partial(gram_kernel, first), out, 0, "gram_part", pl.ANY, scratch, flops)(ids, *blocks)


def blend_kernel(mine, traded, received, out, held_mine, held_traded, held, sems):
    pairs = ((received, held), (mine, held_mine), (traded, held_traded))
    copies = [pltpu.make_async_copy(ref, slot, sems.at[i]) for i, (ref, slot) in enumerate(pairs)]
    for copy in copies:
        copy.start()
    copies[0].wait()
    piece = held[0].astype(f32)
    for i in range(1, 16):
        piece = piece + held[i].astype(f32)
    piece = piece.astype(bf16)
    for copy in copies[1:]:
        copy.wait()
    for i in range(8):
        out[i, 0:128] = (held_mine[i].astype(f32) + held_traded[i].astype(f32)).astype(bf16)
        out[i, 128:256, 0:128] = piece[0:128]
        out[i, 128:256, 128:256] = piece[128:256]


def blend(mine, traded, received):
    return pl.pallas_call(
        blend_kernel,
        out_shape=jax.ShapeDtypeStruct((8, 256, 256), bf16),
        in_specs=[pl.BlockSpec(memory_space=pl.ANY)] * 3,
        out_specs=pl.BlockSpec(memory_space=pltpu.VMEM),
        scratch_shapes=[pltpu.VMEM(x.shape, bf16) for x in (mine, traded, received)] + [pltpu.SemaphoreType.DMA((3,))],
        compiler_params=pltpu.CompilerParams(vmem_limit_bytes=14 * 1024 * 1024),
        cost_estimate=pl.CostEstimate(flops=1 << 20, bytes_accessed=4 << 20, transcendentals=0),
        name="blend",
    )(mine, traded, received)


def apply(part, blocks, ids):
    out = None
    for ref, (p, k) in zip(blocks, places(ids)):
        left = jnp.concatenate([part(p >> 1, p & 1, k, s) for s in range(2)], axis=1)
        prod = dot(left, ref[...], ((1,), (0,)))
        out = prod if out is None else out + prod
    return out * (2.0 * off_weight / BATCH)


def image_sum(x):
    return jnp.sum(x, axis=0, keepdims=True)


def split(x):
    high = x.astype(bf16).astype(f32)
    return [high, x - high]


def second_kernel(ids, mixed, traded, partner, *refs):
    blocks, up, out = refs[:8], refs[8], refs[9]

    def part(high, low, k, s):
        index = 4 * high + 2 * low + k
        rows = jnp.where(ids[10] == s, mixed[index, 128:256, :], traded[index])
        return jnp.concatenate([rows[:, 0:128], rows[:, 128:256]], axis=0)

    piece = mixed[0, 0:128].astype(f32)
    for i in range(1, 8):
        piece = piece + mixed[i, 0:128].astype(f32)
    piece = piece.astype(bf16)
    for i in range(16):
        out[i, 0:128] = piece
    value = apply(part, blocks, ids)
    up[...] = value
    norm = blocks[0][...].astype(f32)
    sums = [image_sum(value), partner[0:1], image_sum(norm), jnp.zeros((1, 1024), f32)]
    sums += split(image_sum(value * norm)) + split(partner[1:2])
    row = lax.broadcasted_iota(jnp.int32, (8, 1024), 0)
    rows = jnp.zeros((8, 1024), f32)
    for i in range(8):
        rows = jnp.where(row == i, sums[i], rows)
    rows = jnp.concatenate([rows[:, 256 * i : 256 * (i + 1)] for i in range(4)], axis=0).astype(bf16)
    for i in range(16):
        out[i, 128:160] = rows


def second_view(ids, mixed, traded, partner, blocks):
    out = [jax.ShapeDtypeStruct((256, 1024), f32), jax.ShapeDtypeStruct((16, 160, 256), bf16)]
    return call(second_kernel, out, 3, "second_view")(ids, mixed, traded, partner, *blocks)


def first_kernel(ids, last, *refs):
    blocks, (keep, give, out, second_sums) = refs[:8], refs[8:]

    def part(high, low, k, s):
        at = pl.ds(pl.multiple_of(k * 128, 128), 128)
        index = 4 * (2 * s + high) + 2 * low
        return jnp.concatenate([last[index, 0:128, at], last[index + 1, 0:128, at]], axis=0)

    value = apply(part, blocks, ids)
    side = ids[5]
    keep[...] = jnp.where(side == 0, value[0:128], value[128:256])
    give[...] = jnp.where(side == 0, value[128:256], value[0:128]).astype(bf16)
    sums = [image_sum(value), image_sum(value * blocks[0][...].astype(f32))]
    terms = None
    for i in range(8):
        term = last[2 * i + side, 128:160].astype(f32)
        terms = term if terms is None else terms + term
    second_sums[...] = terms
    row = lax.broadcasted_iota(jnp.int32, (32, 256), 0) % 8
    loss = image_sum(jnp.where((row == 4) | (row == 5), terms, 0.0)) / (2.0 * BATCH)
    products = []
    for j in range(4):
        products.append(terms[8 * j + 6 : 8 * j + 7] + terms[8 * j + 7 : 8 * j + 8])
        corr = products[-1] / BATCH
        miss = 1.0 - corr
        loss = loss + miss * miss - off_weight * corr * corr
    sums.append(jnp.concatenate([loss, jnp.zeros((1, 768), f32)], axis=1))
    sums.append(jnp.concatenate([terms[8 * j + 2 : 8 * j + 3] for j in range(4)], axis=1))
    sums.append(jnp.concatenate(products, axis=1))
    for i in range(16):
        for j in range(5):
            out[i, j : j + 1, :] = sums[j]


def first_view(ids, last, blocks):
    out = [
        jax.ShapeDtypeStruct((128, 1024), f32),
        jax.ShapeDtypeStruct((128, 1024), bf16),
        jax.ShapeDtypeStruct((16, 5, 1024), f32),
        jax.ShapeDtypeStruct((32, 256), f32),
    ]
    return call(first_kernel, out, 1, "first_view", flops=1 << 20)(ids, last, *blocks)


def finish(up, up_norm, partner, partner_norm, count):
    corr = partner_norm / count
    diag = -2.0 * (1.0 - corr) - 2.0 * off_weight * corr
    return diag, (up + diag * partner) / count, (up_norm + diag * partner_norm) / count


def vmem_call(kernel, out_shape, args, name, flops):
    vmem = pl.BlockSpec(memory_space=pltpu.VMEM)
    smem = pl.BlockSpec(memory_space=pltpu.SMEM)
    return pl.pallas_call(
        kernel,
        out_shape=out_shape,
        in_specs=[smem] + [vmem] * (len(args) - 1),
        out_specs=jax.tree.map(lambda _: vmem, out_shape),
        compiler_params=pltpu.CompilerParams(vmem_limit_bytes=14 * 1024 * 1024),
        cost_estimate=pl.CostEstimate(flops=flops, bytes_accessed=1 << 16, transcendentals=0),
        name=name,
    )(*args)


def partner_kernel(ids, other, half, out):
    other = other[...].astype(f32)
    out[0:1, :] = image_sum(other)
    out[1:2, :] = image_sum(other * half[...].astype(f32))


def arrange_kernel(which, ids, same, other, out):
    for half in range(2):
        picked = jnp.where(ids[which] == half, same[...].astype(out.dtype), other[...].astype(out.dtype))
        out[:, 1024 * half : 1024 * (half + 1)] = picked


def finish_second_kernel(ids, terms, scales, view, up, partner, grad):
    for part in range(4):
        columns = slice(256 * part, 256 * (part + 1))
        rows = [terms[8 * part + i : 8 * part + i + 1] for i in range(8)]
        diag, first, second = finish(rows[0], rows[4] + rows[5], rows[1], rows[6] + rows[7], BATCH)
        mean, inv = scales[0:1, columns], scales[1:2, columns]
        norm = (view[:, columns] - mean) * inv
        grad[:, columns] = inv * (up[:, columns] + diag * partner[:, columns].astype(f32) - first - norm * second)


def finish_kernel(ids, sums, scales, view, up, block, grad, loss):
    row = ids[2]
    loss[0, 0] = jnp.sum(sums[:, 2, :]) / FEAT
    for half in range(2):
        columns = slice(1024 * half, 1024 * (half + 1))
        total = sums[8 * half]
        for i in range(1, 8):
            total = total + sums[8 * half + i]
        partner = sums[2 * row + half]
        diag, first, second = finish(total[0:1], total[1:2], partner[3:4], partner[4:5], BATCH)
        mean, inv = scales[0:1, columns], scales[1:2, columns]
        norm = (view[:, columns] - mean) * inv
        grad[:, columns] = inv * (up[:, columns] + diag * block[:, columns].astype(f32) - first - norm * second)


def finish_first(ids, *args):
    vmem = pl.BlockSpec(memory_space=pltpu.VMEM)
    smem = pl.BlockSpec(memory_space=pltpu.SMEM)
    return pl.pallas_call(
        finish_kernel,
        out_shape=[jax.ShapeDtypeStruct((128, 2048), f32), jax.ShapeDtypeStruct((1, 1), f32)],
        in_specs=[smem] + [vmem] * len(args),
        out_specs=[vmem, smem],
        compiler_params=pltpu.CompilerParams(vmem_limit_bytes=14 * 1024 * 1024),
        cost_estimate=pl.CostEstimate(flops=1 << 20, bytes_accessed=1 << 16, transcendentals=0),
        name="finish_first",
    )(ids, *args)


def row_sum(x):
    x = x + lax.ppermute(x, "xh", SWAP)
    return x + sum(lax.ppermute(x, ("y1", "y0"), [(i, (i + step) % 4) for i in range(4)]) for step in (1, 2, 3))


def local(view_a, view_b):
    count = BATCH
    core = lax.axis_index("k")
    xl = lax.axis_index("xl")
    device = lax.axis_index(ROW + COL)
    pairs_a, wanted_a, pairs_b, wanted_b = crossing_tables()
    ids_a = jnp.concatenate([jnp.stack([lax.axis_index(("z1", "z0")), core]), jnp.array(wanted_a)[device], xl[None]])
    ids_b = jnp.concatenate([jnp.stack([lax.axis_index(("y1", "y0")), lax.axis_index("xh")]), jnp.array(wanted_b)[device], core[None]])

    stats_a, late_b = tie(stats(view_a), view_b)
    norm_a, mean_a, inv_a = finish_stats(jnp.sum(spread(stats_a, COL, 16), axis=0), count, view_a)
    norm_b, mean_b, inv_b = finish_stats(row_sum(stats(late_b)), count, view_b)
    half_a = norm_a.astype(bf16)
    half_b = norm_b.astype(bf16)

    zs, ys = ("z1", "z0"), ("y1", "y0")
    parts_a = jnp.transpose(half_a.reshape(128, 2, 1024), (1, 0, 2))
    own_a = both(xl, pick(parts_a, xl), lax.ppermute(pick(parts_a, 1 - xl), "xl", SWAP), 0)
    near_b = ring_near(half_b, ys)
    own_a, late_half_b = tie(own_a, half_b)
    near_a = ring_near(own_a, zs)
    other_own_a = trade([own_a], "k")
    other_own_b = trade([late_half_b], "xh")
    *near_a, near_b[0], near_b[1], other_own_b[0] = tie(*near_a, *near_b, *other_own_b)
    far_pairs = [(2 * i + k, 2 * ((i + (3 if k else 1)) % 4) + k) for i in range(4) for k in range(2)]
    far_a = lax.ppermute(jnp.where(core == 0, near_a[0], near_a[1]), zs + ("k",), far_pairs)
    other_near_a = trade(near_a, "k")
    other_near_b = ring_near(other_own_b[0], ys)
    far_b = lax.ppermute(near_b[0], ys, AHEAD)
    other_far_a, *other_near_b = tie(*trade([far_a], "k"), *other_near_b)
    other_far_b = lax.ppermute(other_near_b[1], ys, BACK)
    blocks_a = [own_a, *near_a, far_a, *other_own_a, *other_near_a, other_far_a]

    part_a, send_a = gram_part(True, ids_a, blocks_a)
    send_a, far_b, other_far_b = tie(send_a, far_b, other_far_b)
    blocks_b = [half_b, *near_b, far_b, *other_own_b, *other_near_b, other_far_b]
    other_a = lax.ppermute(send_a.reshape(256, 1024), ROW + COL, pairs_a)
    piece_a = lax.all_to_all(part_a.reshape(16, 256, 128), ("y1", "y0", "xh", "xl"), 0, 0)
    mine_b, give_b, *send_b = gram_part(False, ids_b, blocks_b)
    mixed = blend(mine_b, lax.ppermute(give_b, "k", SWAP), piece_a)
    ids = jnp.stack([xl, core, lax.axis_index(ROW)])
    partner = vmem_call(partner_kernel, jax.ShapeDtypeStruct((2, 1024), f32), (ids, other_a, half_b), "partner", 1 << 34)
    early = lax.ppermute(send_b[0], ROW + COL, pairs_b[0])
    mixed, partner, early = tie(mixed, partner, early)
    mixed = lax.all_to_all(mixed, ("xl", "z1", "z0"), 0, 0)

    traded = lax.ppermute(mixed[:, 128:], "k", SWAP)
    up_b, last = second_view(ids_b, mixed, traded, partner, blocks_b)
    last = lax.all_to_all(last, ("y1", "y0", "xh", "xl"), 0, 0)
    last, late = tie(last, send_b[1])
    late = lax.ppermute(late, ROW + COL, pairs_b[1])

    keep, give, sums_a, sums_b = first_view(ids_a, last, blocks_a)
    traded = lax.ppermute(lax.ppermute(give, ("xl", "k"), [(i, 3 - i) for i in range(4)]), "k", SWAP)
    block = jax.ShapeDtypeStruct((128, 2048), bf16)
    block = vmem_call(functools.partial(arrange_kernel, 1), block, (ids, early, late), "arrange_block", 1 << 34)
    keep, block = tie(keep, block)
    up_own = jax.ShapeDtypeStruct((128, 2048), f32)
    up_own = vmem_call(functools.partial(arrange_kernel, 0), up_own, (ids, keep, traded), "arrange_up", 1 << 33)
    sums_a, sums_b = tie(sums_a, sums_b)
    sums_a = lax.all_to_all(sums_a, COL, 0, 0)

    args = (ids, sums_b, jnp.stack([mean_b, inv_b]), view_b, up_b, other_a)
    grad_b = vmem_call(finish_second_kernel, jax.ShapeDtypeStruct((256, 1024), f32), args, "finish_second", 1 << 20)
    grad_a, loss_value = finish_first(ids, sums_a, jnp.stack([mean_a, inv_a]), view_a, up_own, block)
    return (loss_value[0, 0], grad_a, grad_b)


def solution(mesh):
    fine = Mesh(mesh.devices.reshape((2,) * 7), NAMES)
    return jax.shard_map(
        local,
        mesh=fine,
        in_specs=(P(COL, ROW), P(ROW, COL)),
        out_specs=(P(), P(COL, ROW), P(ROW, COL)),
        check_vma=False,
    )
```

```python
import functools

import jax
import jax.numpy as jnp
from jax import lax
from jax.experimental import pallas as pl
from jax.experimental.pallas import tpu as pltpu
from jax.sharding import Mesh, PartitionSpec as P

FEAT = 16384
BATCH = 2048

off_weight = 0.0051
eps_value = 1e-05

f32 = jnp.float32
bf16 = jnp.bfloat16

NAMES = ("y1", "y0", "xh", "xl", "z1", "z0", "k")
ROW = ("y1", "y0", "xh")
COL = ("xl", "z1", "z0", "k")
SWAP = [(0, 1), (1, 0)]
AHEAD = [(i, (i + 1) % 4) for i in range(4)]
BACK = [(i, (i + 3) % 4) for i in range(4)]


TURN_A = (((0, 1, 0), (1, 0, 0), (1, 0, 1)), ((0, 1, 0, 1), (1, 1, 1, 0), (0, 1, 0, 1)))
TURN_B = ((((0, 0, 1), (0, 1, 0), (1, 0, 0)), ((0, 1, 1, 1), (1, 0, 1, 1), (1, 0, 1, 0))),) * 2


def spread(x, axes, n):
    return lax.all_to_all(jnp.broadcast_to(x[None], (n,) + x.shape), axes, 0, 0)


def bits(n):
    return [(n >> s) & 1 for s in range(6, -1, -1)]


def number(p):
    return sum(v << s for v, s in zip(p, range(6, -1, -1)))


def turned(first, second, rows):
    matrix, shift = rows
    out = []
    for m, v in zip(matrix, shift):
        out.append((sum(a * b for a, b in zip(m, first)) + sum(a * b for a, b in zip(v, second))) % 2)
    return out


def crossing_tables():
    pairs_a, wanted_a = [], [[0, 0, 0]] * 128
    pairs_b, wanted_b = [[], []], [[0] * 8 for _ in range(128)]
    for target in range(128):
        y1, y0, xh, xl, z1, z0, k = bits(target)
        g = turned((y1, y0, xh), (xl, z1, z0, k), TURN_A)
        source = number((xl, z1, z0, k, g[0], g[1], g[2]))
        pairs_a.append((source, target))
        wanted_a[source] = [y0, xh, y1]
        for step in range(2):
            g = turned((xl, z1, z0), (y1, y0, xh, k), TURN_B[step])
            source = number((g[0], g[1], g[2], y1, y0, xh, k ^ step))
            pairs_b[step].append((source, target))
            wanted_b[source][4 * step : 4 * step + 4] = [xl, z1, z0, k]
    return pairs_a, wanted_a, pairs_b, wanted_b


def finish_stats(sums, count, view):
    mean = sums[0] / count
    inv = lax.rsqrt(sums[1] / count - mean * mean + eps_value)
    return ((view - mean) * inv, mean, inv)


def stats(view):
    return jnp.stack([jnp.sum(view, axis=0), jnp.sum(view * view, axis=0)])


def dot(x, y, dims):
    return lax.dot_general(x, y, (dims, ((), ())), preferred_element_type=f32)


def pick(x, index):
    return lax.dynamic_index_in_dim(x, index, 0, keepdims=False)


def both(which, mine, other, axis):
    return jnp.concatenate([jnp.where(which == 0, mine, other), jnp.where(which == 0, other, mine)], axis=axis)


def tie(*xs):
    return lax.optimization_barrier(xs)


def ring_near(own, ring):
    return [lax.ppermute(own, ring, AHEAD), lax.ppermute(own, ring, BACK)]


def trade(blocks, axis):
    return [lax.ppermute(x, axis, SWAP) for x in blocks]


OFFSETS = (0, 3, 1, 2)


def places(ids):
    return [((ids[0] + offset) & 3, ids[1] ^ flip) for flip in range(2) for offset in OFFSETS]


def gram_kernel(first, ids, *refs):
    if first:
        out, send, held, sems = refs[8:]
    else:
        mine, give, *sends, held, sems = refs[8:]
    copies = []
    for i, ref in enumerate(refs[:8]):
        slot = held.at[i // 4, pl.ds(256 * (i % 4), 256), :]
        copies.append(pltpu.make_async_copy(ref, slot, sems.at[i]))
        copies[-1].start()
    copies[0].wait()
    own = held[0, 0:256, :].T
    for flip in range(2):
        for index in range(4 * flip, 4 * flip + 4):
            if index:
                copies[index].wait()
        prod = dot(held[flip], own, ((1,), (0,))).astype(bf16)
        for index in range(4 * flip, 4 * flip + 4):
            p, k = places(ids)[index]
            high, low = p >> 1, p & 1
            for s in range(2):
                at = 256 * (index % 4) + 128 * s
                part = prod[at : at + 128]
                if first:
                    rows = pl.ds(pl.multiple_of(128 * k, 128), 128)
                    for half in range(2):
                        out[2 * (2 * s + high) + low, half, rows, :] = part[:, 128 * half : 128 * (half + 1)]
                    wanted = (high == ids[2]) & (low == ids[3]) & (s == ids[4])

                    @pl.when(wanted)
                    def _():
                        send[k] = held[flip, at : at + 128, :]

                else:

                    @pl.when(ids[10] == s)
                    def _():
                        mine[2 * p + k] = part

                    @pl.when(ids[10] != s)
                    def _():
                        give[2 * p + k] = part

                    for step in range(2):
                        place = [ids[2 + 4 * step + j] for j in range(4)]
                        wanted = (high == place[0]) & (low == place[1]) & (k == place[2]) & (s == place[3])

                        @pl.when(wanted)
                        def _():
                            sends[step][...] = held[flip, at : at + 128, :]


def call(kernel, out_shape, extra, name, space=pltpu.VMEM, scratch=(), flops=2 * 256 * 2048 * 1024):
    vmem = pl.BlockSpec(memory_space=pltpu.VMEM)
    return pl.pallas_call(
        kernel,
        out_shape=out_shape,
        in_specs=[pl.BlockSpec(memory_space=pltpu.SMEM)] + [vmem] * extra + [pl.BlockSpec(memory_space=space)] * 8,
        out_specs=[vmem] * len(out_shape),
        scratch_shapes=list(scratch),
        compiler_params=pltpu.CompilerParams(vmem_limit_bytes=14 * 1024 * 1024),
        cost_estimate=pl.CostEstimate(flops=flops, bytes_accessed=flops >> 8, transcendentals=0),
        name=name,
    )


def gram_part(first, ids, blocks):
    if first:
        shapes = [(8, 2, 256, 128), (2, 128, 1024)]
    else:
        shapes = [(8, 128, 256), (8, 128, 256), (128, 1024), (128, 1024)]
    out = [jax.ShapeDtypeStruct(shape, bf16) for shape in shapes]
    scratch = [pltpu.VMEM((2, 1024, 1024), bf16), pltpu.SemaphoreType.DMA((8,))]
    flops = 2 * 256 * 2048 * 1024 if first else 1 << 20
    return call(functools.partial(gram_kernel, first), out, 0, "gram_part", pl.ANY, scratch, flops)(ids, *blocks)


def blend_kernel(mine, traded, received, out, held_mine, held_traded, held, sems):
    pairs = ((received, held), (mine, held_mine), (traded, held_traded))
    copies = [pltpu.make_async_copy(ref, slot, sems.at[i]) for i, (ref, slot) in enumerate(pairs)]
    for copy in copies:
        copy.start()
    copies[0].wait()
    piece = held[0].astype(f32)
    for i in range(1, 16):
        piece = piece + held[i].astype(f32)
    piece = piece.astype(bf16)
    for copy in copies[1:]:
        copy.wait()
    for i in range(8):
        out[i, 0:128] = (held_mine[i].astype(f32) + held_traded[i].astype(f32)).astype(bf16)
        out[i, 128:256, 0:128] = piece[0:128]
        out[i, 128:256, 128:256] = piece[128:256]


def blend(mine, traded, received):
    return pl.pallas_call(
        blend_kernel,
        out_shape=jax.ShapeDtypeStruct((8, 256, 256), bf16),
        in_specs=[pl.BlockSpec(memory_space=pl.ANY)] * 3,
        out_specs=pl.BlockSpec(memory_space=pltpu.VMEM),
        scratch_shapes=[pltpu.VMEM(x.shape, bf16) for x in (mine, traded, received)] + [pltpu.SemaphoreType.DMA((3,))],
        compiler_params=pltpu.CompilerParams(vmem_limit_bytes=14 * 1024 * 1024),
        cost_estimate=pl.CostEstimate(flops=1 << 20, bytes_accessed=4 << 20, transcendentals=0),
        name="blend",
    )(mine, traded, received)


def apply(part, blocks, ids):
    out = None
    for ref, (p, k) in zip(blocks, places(ids)):
        left = jnp.concatenate([part(p >> 1, p & 1, k, s) for s in range(2)], axis=1)
        prod = dot(left, ref[...], ((1,), (0,)))
        out = prod if out is None else out + prod
    return out * (2.0 * off_weight / BATCH)


def image_sum(x):
    return jnp.sum(x, axis=0, keepdims=True)


def split(x):
    high = x.astype(bf16).astype(f32)
    return [high, x - high]


def second_kernel(ids, mixed, traded, partner, *refs):
    blocks, up, out = refs[:8], refs[8], refs[9]

    def part(high, low, k, s):
        index = 4 * high + 2 * low + k
        rows = jnp.where(ids[10] == s, mixed[index, 128:256, :], traded[index])
        return jnp.concatenate([rows[:, 0:128], rows[:, 128:256]], axis=0)

    piece = mixed[0, 0:128].astype(f32)
    for i in range(1, 8):
        piece = piece + mixed[i, 0:128].astype(f32)
    piece = piece.astype(bf16)
    for i in range(16):
        out[i, 0:128] = piece
    value = apply(part, blocks, ids)
    up[...] = value
    norm = blocks[0][...].astype(f32)
    sums = [image_sum(value), partner[0:1], image_sum(norm), jnp.zeros((1, 1024), f32)]
    sums += split(image_sum(value * norm)) + split(partner[1:2])
    row = lax.broadcasted_iota(jnp.int32, (8, 1024), 0)
    rows = jnp.zeros((8, 1024), f32)
    for i in range(8):
        rows = jnp.where(row == i, sums[i], rows)
    rows = jnp.concatenate([rows[:, 256 * i : 256 * (i + 1)] for i in range(4)], axis=0).astype(bf16)
    for i in range(16):
        out[i, 128:160] = rows


def second_view(ids, mixed, traded, partner, blocks):
    out = [jax.ShapeDtypeStruct((256, 1024), f32), jax.ShapeDtypeStruct((16, 160, 256), bf16)]
    return call(second_kernel, out, 3, "second_view")(ids, mixed, traded, partner, *blocks)


def first_kernel(ids, last, *refs):
    blocks, (keep, give, out, second_sums) = refs[:8], refs[8:]

    def part(high, low, k, s):
        at = pl.ds(pl.multiple_of(k * 128, 128), 128)
        index = 4 * (2 * s + high) + 2 * low
        return jnp.concatenate([last[index, 0:128, at], last[index + 1, 0:128, at]], axis=0)

    value = apply(part, blocks, ids)
    side = ids[5]
    keep[...] = jnp.where(side == 0, value[0:128], value[128:256])
    give[...] = jnp.where(side == 0, value[128:256], value[0:128]).astype(bf16)
    sums = [image_sum(value), image_sum(value * blocks[0][...].astype(f32))]
    terms = None
    for i in range(8):
        term = last[2 * i + side, 128:160].astype(f32)
        terms = term if terms is None else terms + term
    second_sums[...] = terms
    row = lax.broadcasted_iota(jnp.int32, (32, 256), 0) % 8
    loss = image_sum(jnp.where((row == 4) | (row == 5), terms, 0.0)) / (2.0 * BATCH)
    products = []
    for j in range(4):
        products.append(terms[8 * j + 6 : 8 * j + 7] + terms[8 * j + 7 : 8 * j + 8])
        corr = products[-1] / BATCH
        miss = 1.0 - corr
        loss = loss + miss * miss - off_weight * corr * corr
    sums.append(jnp.concatenate([loss, jnp.zeros((1, 768), f32)], axis=1))
    sums.append(jnp.concatenate([terms[8 * j + 2 : 8 * j + 3] for j in range(4)], axis=1))
    sums.append(jnp.concatenate(products, axis=1))
    for i in range(16):
        for j in range(5):
            out[i, j : j + 1, :] = sums[j]


def first_view(ids, last, blocks):
    out = [
        jax.ShapeDtypeStruct((128, 1024), f32),
        jax.ShapeDtypeStruct((128, 1024), bf16),
        jax.ShapeDtypeStruct((16, 5, 1024), f32),
        jax.ShapeDtypeStruct((32, 256), f32),
    ]
    return call(first_kernel, out, 1, "first_view", flops=1 << 20)(ids, last, *blocks)


def finish(up, up_norm, partner, partner_norm, count):
    corr = partner_norm / count
    diag = -2.0 * (1.0 - corr) - 2.0 * off_weight * corr
    return diag, (up + diag * partner) / count, (up_norm + diag * partner_norm) / count


def vmem_call(kernel, out_shape, args, name, flops):
    vmem = pl.BlockSpec(memory_space=pltpu.VMEM)
    smem = pl.BlockSpec(memory_space=pltpu.SMEM)
    return pl.pallas_call(
        kernel,
        out_shape=out_shape,
        in_specs=[smem] + [vmem] * (len(args) - 1),
        out_specs=jax.tree.map(lambda _: vmem, out_shape),
        compiler_params=pltpu.CompilerParams(vmem_limit_bytes=14 * 1024 * 1024),
        cost_estimate=pl.CostEstimate(flops=flops, bytes_accessed=1 << 16, transcendentals=0),
        name=name,
    )(*args)


def partner_kernel(ids, other, half, out):
    other = other[...].astype(f32)
    out[0:1, :] = image_sum(other)
    out[1:2, :] = image_sum(other * half[...].astype(f32))


def arrange_kernel(ids, same, other, keep, traded, block, up):
    for half in range(2):
        columns = slice(1024 * half, 1024 * (half + 1))
        block[:, columns] = jnp.where(ids[1] == half, same[...], other[...])
        up[:, columns] = jnp.where(ids[0] == half, keep[...], traded[...].astype(f32))


def finish_second_kernel(ids, terms, scales, view, up, partner, grad):
    for part in range(4):
        columns = slice(256 * part, 256 * (part + 1))
        rows = [terms[8 * part + i : 8 * part + i + 1] for i in range(8)]
        diag, first, second = finish(rows[0], rows[4] + rows[5], rows[1], rows[6] + rows[7], BATCH)
        mean, inv = scales[0:1, columns], scales[1:2, columns]
        norm = (view[:, columns] - mean) * inv
        grad[:, columns] = inv * (up[:, columns] + diag * partner[:, columns].astype(f32) - first - norm * second)


def finish_kernel(ids, sums, scales, view, up, block, grad, loss):
    row = ids[2]
    loss[0, 0] = jnp.sum(sums[:, 2, :]) / FEAT
    for half in range(2):
        columns = slice(1024 * half, 1024 * (half + 1))
        total = sums[8 * half]
        for i in range(1, 8):
            total = total + sums[8 * half + i]
        partner = sums[2 * row + half]
        diag, first, second = finish(total[0:1], total[1:2], partner[3:4], partner[4:5], BATCH)
        mean, inv = scales[0:1, columns], scales[1:2, columns]
        norm = (view[:, columns] - mean) * inv
        grad[:, columns] = inv * (up[:, columns] + diag * block[:, columns].astype(f32) - first - norm * second)


def finish_first(ids, *args):
    vmem = pl.BlockSpec(memory_space=pltpu.VMEM)
    smem = pl.BlockSpec(memory_space=pltpu.SMEM)
    return pl.pallas_call(
        finish_kernel,
        out_shape=[jax.ShapeDtypeStruct((128, 2048), f32), jax.ShapeDtypeStruct((1, 1), f32)],
        in_specs=[smem] + [vmem] * len(args),
        out_specs=[vmem, smem],
        compiler_params=pltpu.CompilerParams(vmem_limit_bytes=14 * 1024 * 1024),
        cost_estimate=pl.CostEstimate(flops=1 << 20, bytes_accessed=1 << 16, transcendentals=0),
        name="finish_first",
    )(ids, *args)


def row_sum(x):
    x = x + sum(lax.ppermute(x, ("y1", "y0"), [(i, (i + step) % 4) for i in range(4)]) for step in (1, 2, 3))
    return x + lax.ppermute(x, "xh", SWAP)


def local(view_a, view_b):
    count = BATCH
    core = lax.axis_index("k")
    xl = lax.axis_index("xl")
    device = lax.axis_index(ROW + COL)
    pairs_a, wanted_a, pairs_b, wanted_b = crossing_tables()
    ids_a = jnp.concatenate([jnp.stack([lax.axis_index(("z1", "z0")), core]), jnp.array(wanted_a)[device], xl[None]])
    ids_b = jnp.concatenate([jnp.stack([lax.axis_index(("y1", "y0")), lax.axis_index("xh")]), jnp.array(wanted_b)[device], core[None]])

    stats_a, late_b = tie(stats(view_a), view_b)
    norm_a, mean_a, inv_a = finish_stats(jnp.sum(spread(stats_a, COL, 16), axis=0), count, view_a)
    norm_b, mean_b, inv_b = finish_stats(row_sum(stats(late_b)), count, view_b)
    half_a = norm_a.astype(bf16)
    half_b = norm_b.astype(bf16)

    zs, ys = ("z1", "z0"), ("y1", "y0")
    parts_a = jnp.transpose(half_a.reshape(128, 2, 1024), (1, 0, 2))
    own_a = both(xl, pick(parts_a, xl), lax.ppermute(pick(parts_a, 1 - xl), "xl", SWAP), 0)
    near_b = ring_near(half_b, ys)
    own_a, late_half_b = tie(own_a, half_b)
    near_a = ring_near(own_a, zs)
    other_own_a = trade([own_a], "k")
    other_own_b = trade([late_half_b], "xh")
    *near_a, near_b[0], near_b[1], other_own_b[0] = tie(*near_a, *near_b, *other_own_b)
    far_pairs = [(2 * i + k, 2 * ((i + (3 if k else 1)) % 4) + k) for i in range(4) for k in range(2)]
    far_a = lax.ppermute(jnp.where(core == 0, near_a[0], near_a[1]), zs + ("k",), far_pairs)
    other_near_a = trade(near_a, "k")
    other_near_b = ring_near(other_own_b[0], ys)
    far_b = lax.ppermute(near_b[0], ys, AHEAD)
    other_far_a, *other_near_b = tie(*trade([far_a], "k"), *other_near_b)
    other_far_b = lax.ppermute(other_near_b[1], ys, BACK)
    blocks_a = [own_a, *near_a, far_a, *other_own_a, *other_near_a, other_far_a]

    part_a, send_a = gram_part(True, ids_a, blocks_a)
    send_a, far_b, other_far_b = tie(send_a, far_b, other_far_b)
    blocks_b = [half_b, *near_b, far_b, *other_own_b, *other_near_b, other_far_b]
    other_a = lax.ppermute(send_a.reshape(256, 1024), ROW + COL, pairs_a)
    piece_a = lax.all_to_all(part_a.reshape(16, 256, 128), ("y1", "y0", "xh", "xl"), 0, 0)
    mine_b, give_b, *send_b = gram_part(False, ids_b, blocks_b)
    mixed = blend(mine_b, lax.ppermute(give_b, "k", SWAP), piece_a)
    ids = jnp.stack([xl, core, lax.axis_index(ROW)])
    partner = vmem_call(partner_kernel, jax.ShapeDtypeStruct((2, 1024), f32), (ids, other_a, half_b), "partner", 1 << 34)
    early = lax.ppermute(send_b[0], ROW + COL, pairs_b[0])
    mixed, partner, early = tie(mixed, partner, early)
    mixed = lax.all_to_all(mixed, ("xl", "z1", "z0"), 0, 0)

    traded = lax.ppermute(mixed[:, 128:], "k", SWAP)
    up_b, last = second_view(ids_b, mixed, traded, partner, blocks_b)
    last = lax.all_to_all(last, ("y1", "y0", "xh", "xl"), 0, 0)
    last, late = tie(last, send_b[1])
    late = lax.ppermute(late, ROW + COL, pairs_b[1])

    keep, give, sums_a, sums_b = first_view(ids_a, last, blocks_a)
    traded = lax.ppermute(give, "xl", SWAP)
    out = [jax.ShapeDtypeStruct((128, 2048), bf16), jax.ShapeDtypeStruct((128, 2048), f32)]
    block, up_own = vmem_call(arrange_kernel, out, (ids, early, late, keep, traded), "arrange", 1 << 34)
    sums_a, sums_b = tie(sums_a, sums_b)
    sums_a = lax.all_to_all(sums_a, COL, 0, 0)

    args = (ids, sums_b, jnp.stack([mean_b, inv_b]), view_b, up_b, other_a)
    grad_b = vmem_call(finish_second_kernel, jax.ShapeDtypeStruct((256, 1024), f32), args, "finish_second", 1 << 20)
    grad_a, loss_value = finish_first(ids, sums_a, jnp.stack([mean_a, inv_a]), view_a, up_own, block)
    return (loss_value[0, 0], grad_a, grad_b)


def solution(mesh):
    fine = Mesh(mesh.devices.reshape((2,) * 7), NAMES)
    return jax.shard_map(
        local,
        mesh=fine,
        in_specs=(P(COL, ROW), P(ROW, COL)),
        out_specs=(P(), P(COL, ROW), P(ROW, COL)),
        check_vma=False,
    )
```

```python
import functools

import jax
import jax.numpy as jnp
from jax import lax
from jax.experimental import pallas as pl
from jax.experimental.pallas import tpu as pltpu
from jax.sharding import Mesh, PartitionSpec as P

FEAT = 16384
BATCH = 2048

off_weight = 0.0051
eps_value = 1e-05

f32 = jnp.float32
bf16 = jnp.bfloat16

NAMES = ("y1", "y0", "xh", "xl", "z1", "z0", "k")
ROW = ("y1", "y0", "xh")
COL = ("xl", "z1", "z0", "k")
SWAP = [(0, 1), (1, 0)]
AHEAD = [(i, (i + 1) % 4) for i in range(4)]
BACK = [(i, (i + 3) % 4) for i in range(4)]


TURN_A = (((0, 1, 0), (1, 0, 0), (1, 0, 1)), ((0, 1, 0, 1), (1, 1, 1, 0), (0, 1, 0, 1)))
TURN_B = ((((0, 0, 1), (0, 1, 0), (1, 0, 0)), ((0, 1, 1, 1), (1, 0, 1, 1), (1, 0, 1, 0))),) * 2


def spread(x, axes, n):
    return lax.all_to_all(jnp.broadcast_to(x[None], (n,) + x.shape), axes, 0, 0)


def bits(n):
    return [(n >> s) & 1 for s in range(6, -1, -1)]


def number(p):
    return sum(v << s for v, s in zip(p, range(6, -1, -1)))


def turned(first, second, rows):
    matrix, shift = rows
    out = []
    for m, v in zip(matrix, shift):
        out.append((sum(a * b for a, b in zip(m, first)) + sum(a * b for a, b in zip(v, second))) % 2)
    return out


def crossing_tables():
    pairs_a, wanted_a = [], [[0, 0, 0]] * 128
    pairs_b, wanted_b = [[], []], [[0] * 8 for _ in range(128)]
    for target in range(128):
        y1, y0, xh, xl, z1, z0, k = bits(target)
        g = turned((y1, y0, xh), (xl, z1, z0, k), TURN_A)
        source = number((xl, z1, z0, k, g[0], g[1], g[2]))
        pairs_a.append((source, target))
        wanted_a[source] = [y0, xh, y1]
        for step in range(2):
            g = turned((xl, z1, z0), (y1, y0, xh, k), TURN_B[step])
            source = number((g[0], g[1], g[2], y1, y0, xh, k ^ step))
            pairs_b[step].append((source, target))
            wanted_b[source][4 * step : 4 * step + 4] = [xl, z1, z0, k]
    return pairs_a, wanted_a, pairs_b, wanted_b


def finish_stats(sums, count, view):
    mean = sums[0] / count
    inv = lax.rsqrt(sums[1] / count - mean * mean + eps_value)
    return ((view - mean) * inv, mean, inv)


def stats(view):
    return jnp.stack([jnp.sum(view, axis=0), jnp.sum(view * view, axis=0)])


def dot(x, y, dims):
    return lax.dot_general(x, y, (dims, ((), ())), preferred_element_type=f32)


def pick(x, index):
    return lax.dynamic_index_in_dim(x, index, 0, keepdims=False)


def both(which, mine, other, axis):
    return jnp.concatenate([jnp.where(which == 0, mine, other), jnp.where(which == 0, other, mine)], axis=axis)


def tie(*xs):
    return lax.optimization_barrier(xs)


def ring_near(own, ring):
    return [lax.ppermute(own, ring, AHEAD), lax.ppermute(own, ring, BACK)]


def trade(blocks, axis):
    return [lax.ppermute(x, axis, SWAP) for x in blocks]


OFFSETS = (0, 3, 1, 2)


def places(ids):
    return [((ids[0] + offset) & 3, ids[1] ^ flip) for flip in range(2) for offset in OFFSETS]


def gram_kernel(first, ids, *refs):
    if first:
        out, send, held, sems = refs[8:]
    else:
        mine, give, *sends, held, sems = refs[8:]
    copies = []
    for i, ref in enumerate(refs[:8]):
        slot = held.at[i // 4, pl.ds(256 * (i % 4), 256), :]
        copies.append(pltpu.make_async_copy(ref, slot, sems.at[i]))
        copies[-1].start()
    copies[0].wait()
    own = held[0, 0:256, :].T
    for flip in range(2):
        for index in range(4 * flip, 4 * flip + 4):
            if index:
                copies[index].wait()
        prod = dot(held[flip], own, ((1,), (0,))).astype(bf16)
        for index in range(4 * flip, 4 * flip + 4):
            p, k = places(ids)[index]
            high, low = p >> 1, p & 1
            for s in range(2):
                at = 256 * (index % 4) + 128 * s
                part = prod[at : at + 128]
                if first:
                    rows = pl.ds(pl.multiple_of(128 * k, 128), 128)
                    for half in range(2):
                        out[2 * (2 * s + high) + low, half, rows, :] = part[:, 128 * half : 128 * (half + 1)]
                    wanted = (high == ids[2]) & (low == ids[3]) & (s == ids[4])

                    @pl.when(wanted)
                    def _():
                        send[k] = held[flip, at : at + 128, :]

                else:

                    @pl.when(ids[10] == s)
                    def _():
                        mine[2 * p + k] = part

                    @pl.when(ids[10] != s)
                    def _():
                        give[2 * p + k] = part

                    for step in range(2):
                        place = [ids[2 + 4 * step + j] for j in range(4)]
                        wanted = (high == place[0]) & (low == place[1]) & (k == place[2]) & (s == place[3])

                        @pl.when(wanted)
                        def _():
                            sends[step][...] = held[flip, at : at + 128, :]


def call(kernel, out_shape, extra, name, space=pltpu.VMEM, scratch=(), flops=2 * 256 * 2048 * 1024):
    vmem = pl.BlockSpec(memory_space=pltpu.VMEM)
    return pl.pallas_call(
        kernel,
        out_shape=out_shape,
        in_specs=[pl.BlockSpec(memory_space=pltpu.SMEM)] + [vmem] * extra + [pl.BlockSpec(memory_space=space)] * 8,
        out_specs=[vmem] * len(out_shape),
        scratch_shapes=list(scratch),
        compiler_params=pltpu.CompilerParams(vmem_limit_bytes=14 * 1024 * 1024),
        cost_estimate=pl.CostEstimate(flops=flops, bytes_accessed=flops >> 8, transcendentals=0),
        name=name,
    )


def gram_part(first, ids, blocks):
    if first:
        shapes = [(8, 2, 256, 128), (2, 128, 1024)]
    else:
        shapes = [(8, 128, 256), (8, 128, 256), (128, 1024), (128, 1024)]
    out = [jax.ShapeDtypeStruct(shape, bf16) for shape in shapes]
    scratch = [pltpu.VMEM((2, 1024, 1024), bf16), pltpu.SemaphoreType.DMA((8,))]
    flops = 2 * 256 * 2048 * 1024 if first else 1 << 20
    return call(functools.partial(gram_kernel, first), out, 0, "gram_part", pl.ANY, scratch, flops)(ids, *blocks)


def blend_kernel(mine, traded, received, out, held_mine, held_traded, held, sems):
    pairs = ((received, held), (mine, held_mine), (traded, held_traded))
    copies = [pltpu.make_async_copy(ref, slot, sems.at[i]) for i, (ref, slot) in enumerate(pairs)]
    for copy in copies:
        copy.start()
    copies[0].wait()
    piece = held[0].astype(f32)
    for i in range(1, 16):
        piece = piece + held[i].astype(f32)
    piece = piece.astype(bf16)
    for copy in copies[1:]:
        copy.wait()
    for i in range(8):
        out[i, 0:128] = (held_mine[i].astype(f32) + held_traded[i].astype(f32)).astype(bf16)
        out[i, 128:256, 0:128] = piece[0:128]
        out[i, 128:256, 128:256] = piece[128:256]


def blend(mine, traded, received):
    return pl.pallas_call(
        blend_kernel,
        out_shape=jax.ShapeDtypeStruct((8, 256, 256), bf16),
        in_specs=[pl.BlockSpec(memory_space=pl.ANY)] * 3,
        out_specs=pl.BlockSpec(memory_space=pltpu.VMEM),
        scratch_shapes=[pltpu.VMEM(x.shape, bf16) for x in (mine, traded, received)] + [pltpu.SemaphoreType.DMA((3,))],
        compiler_params=pltpu.CompilerParams(vmem_limit_bytes=14 * 1024 * 1024),
        cost_estimate=pl.CostEstimate(flops=1 << 20, bytes_accessed=4 << 20, transcendentals=0),
        name="blend",
    )(mine, traded, received)


def apply(part, blocks, ids):
    out = None
    for ref, (p, k) in zip(blocks, places(ids)):
        left = jnp.concatenate([part(p >> 1, p & 1, k, s) for s in range(2)], axis=1)
        prod = dot(left, ref[...], ((1,), (0,)))
        out = prod if out is None else out + prod
    return out * (2.0 * off_weight / BATCH)


def image_sum(x):
    return jnp.sum(x, axis=0, keepdims=True)


def split(x):
    high = x.astype(bf16).astype(f32)
    return [high, x - high]


def second_kernel(ids, mixed, traded, partner, *refs):
    blocks, up, out = refs[:8], refs[8], refs[9]

    def part(high, low, k, s):
        index = 4 * high + 2 * low + k
        rows = jnp.where(ids[10] == s, mixed[index, 128:256, :], traded[index])
        return jnp.concatenate([rows[:, 0:128], rows[:, 128:256]], axis=0)

    piece = mixed[0, 0:128].astype(f32)
    for i in range(1, 8):
        piece = piece + mixed[i, 0:128].astype(f32)
    piece = piece.astype(bf16)
    for i in range(16):
        out[i, 0:128] = piece
    value = apply(part, blocks, ids)
    up[...] = value
    norm = blocks[0][...].astype(f32)
    sums = [image_sum(value), partner[0:1], image_sum(norm), jnp.zeros((1, 1024), f32)]
    sums += split(image_sum(value * norm)) + split(partner[1:2])
    row = lax.broadcasted_iota(jnp.int32, (8, 1024), 0)
    rows = jnp.zeros((8, 1024), f32)
    for i in range(8):
        rows = jnp.where(row == i, sums[i], rows)
    rows = jnp.concatenate([rows[:, 256 * i : 256 * (i + 1)] for i in range(4)], axis=0).astype(bf16)
    for i in range(16):
        out[i, 128:160] = rows


def second_view(ids, mixed, traded, partner, blocks):
    out = [jax.ShapeDtypeStruct((256, 1024), f32), jax.ShapeDtypeStruct((16, 160, 256), bf16)]
    return call(second_kernel, out, 3, "second_view")(ids, mixed, traded, partner, *blocks)


def first_kernel(ids, last, *refs):
    blocks, (keep, give, out, second_sums) = refs[:8], refs[8:]

    def part(high, low, k, s):
        at = pl.ds(pl.multiple_of(k * 128, 128), 128)
        index = 4 * (2 * s + high) + 2 * low
        return jnp.concatenate([last[index, 0:128, at], last[index + 1, 0:128, at]], axis=0)

    value = apply(part, blocks, ids)
    side = ids[5]
    keep[...] = jnp.where(side == 0, value[0:128], value[128:256])
    give[...] = jnp.where(side == 0, value[128:256], value[0:128]).astype(bf16)
    sums = [image_sum(value), image_sum(value * blocks[0][...].astype(f32))]
    terms = None
    for i in range(8):
        term = last[2 * i + side, 128:160].astype(f32)
        terms = term if terms is None else terms + term
    second_sums[...] = terms
    row = lax.broadcasted_iota(jnp.int32, (32, 256), 0) % 8
    loss = image_sum(jnp.where((row == 4) | (row == 5), terms, 0.0)) / (2.0 * BATCH)
    products = []
    for j in range(4):
        products.append(terms[8 * j + 6 : 8 * j + 7] + terms[8 * j + 7 : 8 * j + 8])
        corr = products[-1] / BATCH
        miss = 1.0 - corr
        loss = loss + miss * miss - off_weight * corr * corr
    sums.append(jnp.concatenate([loss, jnp.zeros((1, 768), f32)], axis=1))
    pair = [jnp.concatenate([terms[8 * j + 2 : 8 * j + 3] for j in range(4)], axis=1), jnp.concatenate(products, axis=1)]
    for half in range(2):
        sums += [jnp.where(ids[1] == half, x, 0.0) for x in pair]
    sums.append(jnp.zeros((1, 1024), f32))
    for j in range(8):
        out[j : j + 1, :] = sums[j]


def first_view(ids, last, blocks):
    out = [
        jax.ShapeDtypeStruct((128, 1024), f32),
        jax.ShapeDtypeStruct((128, 1024), bf16),
        jax.ShapeDtypeStruct((8, 1024), f32),
        jax.ShapeDtypeStruct((32, 256), f32),
    ]
    return call(first_kernel, out, 1, "first_view", flops=1 << 20)(ids, last, *blocks)


def finish(up, up_norm, partner, partner_norm, count):
    corr = partner_norm / count
    diag = -2.0 * (1.0 - corr) - 2.0 * off_weight * corr
    return diag, (up + diag * partner) / count, (up_norm + diag * partner_norm) / count


def vmem_call(kernel, out_shape, args, name, flops):
    vmem = pl.BlockSpec(memory_space=pltpu.VMEM)
    smem = pl.BlockSpec(memory_space=pltpu.SMEM)
    return pl.pallas_call(
        kernel,
        out_shape=out_shape,
        in_specs=[smem] + [vmem] * (len(args) - 1),
        out_specs=jax.tree.map(lambda _: vmem, out_shape),
        compiler_params=pltpu.CompilerParams(vmem_limit_bytes=14 * 1024 * 1024),
        cost_estimate=pl.CostEstimate(flops=flops, bytes_accessed=1 << 16, transcendentals=0),
        name=name,
    )(*args)


def partner_kernel(ids, other, half, out):
    other = other[...].astype(f32)
    out[0:1, :] = image_sum(other)
    out[1:2, :] = image_sum(other * half[...].astype(f32))


def arrange_kernel(which, ids, same, other, out):
    for half in range(2):
        picked = jnp.where(ids[which] == half, same[...].astype(out.dtype), other[...].astype(out.dtype))
        out[:, 1024 * half : 1024 * (half + 1)] = picked


def finish_second_kernel(ids, terms, scales, view, up, partner, grad):
    for part in range(4):
        columns = slice(256 * part, 256 * (part + 1))
        rows = [terms[8 * part + i : 8 * part + i + 1] for i in range(8)]
        diag, first, second = finish(rows[0], rows[4] + rows[5], rows[1], rows[6] + rows[7], BATCH)
        mean, inv = scales[0:1, columns], scales[1:2, columns]
        norm = (view[:, columns] - mean) * inv
        grad[:, columns] = inv * (up[:, columns] + diag * partner[:, columns].astype(f32) - first - norm * second)


def finish_kernel(ids, sums, scales, view, up, block, grad, loss):
    row = ids[2]
    loss[0, 0] = jnp.sum(sums[:, 2, :]) / FEAT
    partner = sums[row]
    for half in range(2):
        columns = slice(1024 * half, 1024 * (half + 1))
        total = sums[4 * half] + sums[4 * half + 1] + sums[4 * half + 2] + sums[4 * half + 3]
        rows = [partner[3 + 2 * half : 4 + 2 * half], partner[4 + 2 * half : 5 + 2 * half]]
        diag, first, second = finish(total[0:1], total[1:2], *rows, BATCH)
        mean, inv = scales[0:1, columns], scales[1:2, columns]
        norm = (view[:, columns] - mean) * inv
        grad[:, columns] = inv * (up[:, columns] + diag * block[:, columns].astype(f32) - first - norm * second)


def finish_first(ids, *args):
    vmem = pl.BlockSpec(memory_space=pltpu.VMEM)
    smem = pl.BlockSpec(memory_space=pltpu.SMEM)
    return pl.pallas_call(
        finish_kernel,
        out_shape=[jax.ShapeDtypeStruct((128, 2048), f32), jax.ShapeDtypeStruct((1, 1), f32)],
        in_specs=[smem] + [vmem] * len(args),
        out_specs=[vmem, smem],
        compiler_params=pltpu.CompilerParams(vmem_limit_bytes=14 * 1024 * 1024),
        cost_estimate=pl.CostEstimate(flops=1 << 20, bytes_accessed=1 << 16, transcendentals=0),
        name="finish_first",
    )(ids, *args)


def row_sum(x):
    x = x + sum(lax.ppermute(x, ("y1", "y0"), [(i, (i + step) % 4) for i in range(4)]) for step in (1, 2, 3))
    return x + lax.ppermute(x, "xh", SWAP)


def local(view_a, view_b):
    count = BATCH
    core = lax.axis_index("k")
    xl = lax.axis_index("xl")
    device = lax.axis_index(ROW + COL)
    pairs_a, wanted_a, pairs_b, wanted_b = crossing_tables()
    ids_a = jnp.concatenate([jnp.stack([lax.axis_index(("z1", "z0")), core]), jnp.array(wanted_a)[device], xl[None]])
    ids_b = jnp.concatenate([jnp.stack([lax.axis_index(("y1", "y0")), lax.axis_index("xh")]), jnp.array(wanted_b)[device], core[None]])

    stats_a, late_b = tie(stats(view_a), view_b)
    norm_a, mean_a, inv_a = finish_stats(jnp.sum(spread(stats_a, COL, 16), axis=0), count, view_a)
    norm_b, mean_b, inv_b = finish_stats(row_sum(stats(late_b)), count, view_b)
    half_a = norm_a.astype(bf16)
    half_b = norm_b.astype(bf16)

    zs, ys = ("z1", "z0"), ("y1", "y0")
    parts_a = jnp.transpose(half_a.reshape(128, 2, 1024), (1, 0, 2))
    own_a = both(xl, pick(parts_a, xl), lax.ppermute(pick(parts_a, 1 - xl), "xl", SWAP), 0)
    near_b = ring_near(half_b, ys)
    own_a, late_half_b = tie(own_a, half_b)
    near_a = ring_near(own_a, zs)
    other_own_a = trade([own_a], "k")
    other_own_b = trade([late_half_b], "xh")
    *near_a, near_b[0], near_b[1], other_own_b[0] = tie(*near_a, *near_b, *other_own_b)
    far_pairs = [(2 * i + k, 2 * ((i + (3 if k else 1)) % 4) + k) for i in range(4) for k in range(2)]
    far_a = lax.ppermute(jnp.where(core == 0, near_a[0], near_a[1]), zs + ("k",), far_pairs)
    other_near_a = trade(near_a, "k")
    other_near_b = ring_near(other_own_b[0], ys)
    far_b = lax.ppermute(near_b[0], ys, AHEAD)
    other_far_a, *other_near_b = tie(*trade([far_a], "k"), *other_near_b)
    other_far_b = lax.ppermute(other_near_b[1], ys, BACK)
    blocks_a = [own_a, *near_a, far_a, *other_own_a, *other_near_a, other_far_a]

    part_a, send_a = gram_part(True, ids_a, blocks_a)
    send_a, far_b, other_far_b = tie(send_a, far_b, other_far_b)
    blocks_b = [half_b, *near_b, far_b, *other_own_b, *other_near_b, other_far_b]
    other_a = lax.ppermute(send_a.reshape(256, 1024), ROW + COL, pairs_a)
    piece_a = lax.all_to_all(part_a.reshape(16, 256, 128), ("y1", "y0", "xh", "xl"), 0, 0)
    mine_b, give_b, *send_b = gram_part(False, ids_b, blocks_b)
    mixed = blend(mine_b, lax.ppermute(give_b, "k", SWAP), piece_a)
    ids = jnp.stack([xl, core, lax.axis_index(ROW)])
    partner = vmem_call(partner_kernel, jax.ShapeDtypeStruct((2, 1024), f32), (ids, other_a, half_b), "partner", 1 << 34)
    early = lax.ppermute(send_b[0], ROW + COL, pairs_b[0])
    mixed, partner, early = tie(mixed, partner, early)
    mixed = lax.all_to_all(mixed, ("xl", "z1", "z0"), 0, 0)

    traded = lax.ppermute(mixed[:, 128:], "k", SWAP)
    up_b, last = second_view(ids_b, mixed, traded, partner, blocks_b)
    last = lax.all_to_all(last, ("y1", "y0", "xh", "xl"), 0, 0)
    last, late = tie(last, send_b[1])
    late = lax.ppermute(late, ROW + COL, pairs_b[1])

    keep, give, sums_a, sums_b = first_view(ids_a, last, blocks_a)
    traded = lax.ppermute(give, "xl", SWAP)
    block = jax.ShapeDtypeStruct((128, 2048), bf16)
    block = vmem_call(functools.partial(arrange_kernel, 1), block, (ids, early, late), "arrange_block", 1 << 34)
    keep, block = tie(keep, block)
    up_own = jax.ShapeDtypeStruct((128, 2048), f32)
    up_own = vmem_call(functools.partial(arrange_kernel, 0), up_own, (ids, keep, traded), "arrange_up", 1 << 33)
    sums_a, sums_b = tie(sums_a, sums_b)
    sums_a = spread(sums_a + lax.ppermute(sums_a, "k", SWAP), ("xl", "z1", "z0"), 8)

    args = (ids, sums_b, jnp.stack([mean_b, inv_b]), view_b, up_b, other_a)
    grad_b = vmem_call(finish_second_kernel, jax.ShapeDtypeStruct((256, 1024), f32), args, "finish_second", 1 << 20)
    grad_a, loss_value = finish_first(ids, sums_a, jnp.stack([mean_a, inv_a]), view_a, up_own, block)
    return (loss_value[0, 0], grad_a, grad_b)


def solution(mesh):
    fine = Mesh(mesh.devices.reshape((2,) * 7), NAMES)
    return jax.shard_map(
        local,
        mesh=fine,
        in_specs=(P(COL, ROW), P(ROW, COL)),
        out_specs=(P(), P(COL, ROW), P(ROW, COL)),
        check_vma=False,
    )
```

```python
import functools

import jax
import jax.numpy as jnp
from jax import lax
from jax.experimental import pallas as pl
from jax.experimental.pallas import tpu as pltpu
from jax.sharding import Mesh, PartitionSpec as P

FEAT = 16384
BATCH = 2048

off_weight = 0.0051
eps_value = 1e-05

f32 = jnp.float32
bf16 = jnp.bfloat16

NAMES = ("y1", "y0", "xh", "xl", "z1", "z0", "k")
ROW = ("y1", "y0", "xh")
COL = ("xl", "z1", "z0", "k")
SWAP = [(0, 1), (1, 0)]
AHEAD = [(i, (i + 1) % 4) for i in range(4)]
BACK = [(i, (i + 3) % 4) for i in range(4)]


TURN_A = (((0, 1, 0), (1, 0, 0), (1, 0, 1)), ((0, 1, 0, 1), (1, 1, 1, 0), (0, 1, 0, 1)))
TURN_B = ((((0, 0, 1), (0, 1, 0), (1, 0, 0)), ((0, 1, 1, 1), (1, 0, 1, 1), (1, 0, 1, 0))),) * 2


def spread(x, axes, n):
    return lax.all_to_all(jnp.broadcast_to(x[None], (n,) + x.shape), axes, 0, 0)


def bits(n):
    return [(n >> s) & 1 for s in range(6, -1, -1)]


def number(p):
    return sum(v << s for v, s in zip(p, range(6, -1, -1)))


def turned(first, second, rows):
    matrix, shift = rows
    out = []
    for m, v in zip(matrix, shift):
        out.append((sum(a * b for a, b in zip(m, first)) + sum(a * b for a, b in zip(v, second))) % 2)
    return out


def crossing_tables():
    pairs_a, wanted_a = [], [[0, 0, 0]] * 128
    pairs_b, wanted_b = [[], []], [[0] * 8 for _ in range(128)]
    for target in range(128):
        y1, y0, xh, xl, z1, z0, k = bits(target)
        g = turned((y1, y0, xh), (xl, z1, z0, k), TURN_A)
        source = number((xl, z1, z0, k, g[0], g[1], g[2]))
        pairs_a.append((source, target))
        wanted_a[source] = [y0, xh, y1]
        for step in range(2):
            g = turned((xl, z1, z0), (y1, y0, xh, k), TURN_B[step])
            source = number((g[0], g[1], g[2], y1, y0, xh, k ^ step))
            pairs_b[step].append((source, target))
            wanted_b[source][4 * step : 4 * step + 4] = [xl, z1, z0, k]
    return pairs_a, wanted_a, pairs_b, wanted_b


def finish_stats(sums, count, view):
    mean = sums[0] / count
    inv = lax.rsqrt(sums[1] / count - mean * mean + eps_value)
    return ((view - mean) * inv, mean, inv)


def stats(view):
    return jnp.stack([jnp.sum(view, axis=0), jnp.sum(view * view, axis=0)])


def dot(x, y, dims):
    return lax.dot_general(x, y, (dims, ((), ())), preferred_element_type=f32)


def pick(x, index):
    return lax.dynamic_index_in_dim(x, index, 0, keepdims=False)


def both(which, mine, other, axis):
    return jnp.concatenate([jnp.where(which == 0, mine, other), jnp.where(which == 0, other, mine)], axis=axis)


def tie(*xs):
    return lax.optimization_barrier(xs)


def ring_near(own, ring):
    return [lax.ppermute(own, ring, AHEAD), lax.ppermute(own, ring, BACK)]


def trade(blocks, axis):
    return [lax.ppermute(x, axis, SWAP) for x in blocks]


OFFSETS = (0, 3, 1, 2)


def places(ids):
    return [((ids[0] + offset) & 3, ids[1] ^ flip) for flip in range(2) for offset in OFFSETS]


def gram_kernel(first, ids, *refs):
    if first:
        out, send, held, sems = refs[8:]
    else:
        mine, give, *sends, held, sems = refs[8:]
    copies = []
    for i, ref in enumerate(refs[:8]):
        slot = held.at[i // 4, pl.ds(256 * (i % 4), 256), :]
        copies.append(pltpu.make_async_copy(ref, slot, sems.at[i]))
        copies[-1].start()
    copies[0].wait()
    own = held[0, 0:256, :].T
    for flip in range(2):
        for index in range(4 * flip, 4 * flip + 4):
            if index:
                copies[index].wait()
        prod = dot(held[flip], own, ((1,), (0,))).astype(bf16)
        for index in range(4 * flip, 4 * flip + 4):
            p, k = places(ids)[index]
            high, low = p >> 1, p & 1
            for s in range(2):
                at = 256 * (index % 4) + 128 * s
                part = prod[at : at + 128]
                if first:
                    rows = pl.ds(pl.multiple_of(128 * k, 128), 128)
                    for half in range(2):
                        out[2 * (2 * s + high) + low, half, rows, :] = part[:, 128 * half : 128 * (half + 1)]
                    wanted = (high == ids[2]) & (low == ids[3]) & (s == ids[4])

                    @pl.when(wanted)
                    def _():
                        send[k] = held[flip, at : at + 128, :]

                else:

                    @pl.when(ids[10] == s)
                    def _():
                        mine[2 * p + k] = part

                    @pl.when(ids[10] != s)
                    def _():
                        give[2 * p + k] = part

                    for step in range(2):
                        place = [ids[2 + 4 * step + j] for j in range(4)]
                        wanted = (high == place[0]) & (low == place[1]) & (k == place[2]) & (s == place[3])

                        @pl.when(wanted)
                        def _():
                            sends[step][...] = held[flip, at : at + 128, :]


def call(kernel, out_shape, extra, name, space=pltpu.VMEM, scratch=(), flops=2 * 256 * 2048 * 1024):
    vmem = pl.BlockSpec(memory_space=pltpu.VMEM)
    return pl.pallas_call(
        kernel,
        out_shape=out_shape,
        in_specs=[pl.BlockSpec(memory_space=pltpu.SMEM)] + [vmem] * extra + [pl.BlockSpec(memory_space=space)] * 8,
        out_specs=[vmem] * len(out_shape),
        scratch_shapes=list(scratch),
        compiler_params=pltpu.CompilerParams(vmem_limit_bytes=14 * 1024 * 1024),
        cost_estimate=pl.CostEstimate(flops=flops, bytes_accessed=flops >> 8, transcendentals=0),
        name=name,
    )


def gram_part(first, ids, blocks):
    if first:
        shapes = [(8, 2, 256, 128), (2, 128, 1024)]
    else:
        shapes = [(8, 128, 256), (8, 128, 256), (128, 1024), (128, 1024)]
    out = [jax.ShapeDtypeStruct(shape, bf16) for shape in shapes]
    scratch = [pltpu.VMEM((2, 1024, 1024), bf16), pltpu.SemaphoreType.DMA((8,))]
    flops = 2 * 256 * 2048 * 1024 if first else 1 << 20
    return call(functools.partial(gram_kernel, first), out, 0, "gram_part", pl.ANY, scratch, flops)(ids, *blocks)


def blend_kernel(mine, traded, received, out, held_mine, held_traded, held, sems):
    pairs = ((received, held), (mine, held_mine), (traded, held_traded))
    copies = [pltpu.make_async_copy(ref, slot, sems.at[i]) for i, (ref, slot) in enumerate(pairs)]
    for copy in copies:
        copy.start()
    copies[0].wait()
    piece = held[0].astype(f32)
    for i in range(1, 16):
        piece = piece + held[i].astype(f32)
    piece = piece.astype(bf16)
    for copy in copies[1:]:
        copy.wait()
    for i in range(8):
        out[i, 0:128] = (held_mine[i].astype(f32) + held_traded[i].astype(f32)).astype(bf16)
        out[i, 128:256, 0:128] = piece[0:128]
        out[i, 128:256, 128:256] = piece[128:256]


def blend(mine, traded, received):
    return pl.pallas_call(
        blend_kernel,
        out_shape=jax.ShapeDtypeStruct((8, 256, 256), bf16),
        in_specs=[pl.BlockSpec(memory_space=pl.ANY)] * 3,
        out_specs=pl.BlockSpec(memory_space=pltpu.VMEM),
        scratch_shapes=[pltpu.VMEM(x.shape, bf16) for x in (mine, traded, received)] + [pltpu.SemaphoreType.DMA((3,))],
        compiler_params=pltpu.CompilerParams(vmem_limit_bytes=14 * 1024 * 1024),
        cost_estimate=pl.CostEstimate(flops=1 << 20, bytes_accessed=4 << 20, transcendentals=0),
        name="blend",
    )(mine, traded, received)


def apply(part, blocks, ids):
    out = None
    for ref, (p, k) in zip(blocks, places(ids)):
        left = jnp.concatenate([part(p >> 1, p & 1, k, s) for s in range(2)], axis=1)
        prod = dot(left, ref[...], ((1,), (0,)))
        out = prod if out is None else out + prod
    return out * (2.0 * off_weight / BATCH)


def image_sum(x):
    return jnp.sum(x, axis=0, keepdims=True)


def split(x):
    high = x.astype(bf16).astype(f32)
    return [high, x - high]


def second_kernel(ids, mixed, traded, partner, *refs):
    blocks, up, out = refs[:8], refs[8], refs[9]

    def part(high, low, k, s):
        index = 4 * high + 2 * low + k
        rows = jnp.where(ids[10] == s, mixed[index, 128:256, :], traded[index])
        return jnp.concatenate([rows[:, 0:128], rows[:, 128:256]], axis=0)

    piece = mixed[0, 0:128].astype(f32)
    for i in range(1, 8):
        piece = piece + mixed[i, 0:128].astype(f32)
    piece = piece.astype(bf16)
    for i in range(16):
        out[i, 0:128] = piece
    value = apply(part, blocks, ids)
    up[...] = value
    norm = blocks[0][...].astype(f32)
    sums = [image_sum(value), partner[0:1], image_sum(norm), jnp.zeros((1, 1024), f32)]
    sums += split(image_sum(value * norm)) + split(partner[1:2])
    row = lax.broadcasted_iota(jnp.int32, (8, 1024), 0)
    rows = jnp.zeros((8, 1024), f32)
    for i in range(8):
        rows = jnp.where(row == i, sums[i], rows)
    rows = jnp.concatenate([rows[:, 256 * i : 256 * (i + 1)] for i in range(4)], axis=0).astype(bf16)
    for i in range(16):
        out[i, 128:160] = rows


def second_view(ids, mixed, traded, partner, blocks):
    out = [jax.ShapeDtypeStruct((256, 1024), f32), jax.ShapeDtypeStruct((16, 160, 256), bf16)]
    return call(second_kernel, out, 3, "second_view")(ids, mixed, traded, partner, *blocks)


def first_kernel(ids, last, *refs):
    blocks, (keep, give, out, second_sums) = refs[:8], refs[8:]

    def part(high, low, k, s):
        at = pl.ds(pl.multiple_of(k * 128, 128), 128)
        index = 4 * (2 * s + high) + 2 * low
        return jnp.concatenate([last[index, 0:128, at], last[index + 1, 0:128, at]], axis=0)

    value = apply(part, blocks, ids)
    side = ids[5]
    keep[...] = jnp.where(side == 0, value[0:128], value[128:256])
    give[...] = jnp.where(side == 0, value[128:256], value[0:128]).astype(bf16)
    sums = [image_sum(value), image_sum(value * blocks[0][...].astype(f32))]
    terms = None
    for i in range(8):
        term = last[2 * i + side, 128:160].astype(f32)
        terms = term if terms is None else terms + term
    second_sums[...] = terms
    row = lax.broadcasted_iota(jnp.int32, (32, 256), 0) % 8
    loss = image_sum(jnp.where((row == 4) | (row == 5), terms, 0.0)) / (2.0 * BATCH)
    products = []
    for j in range(4):
        products.append(terms[8 * j + 6 : 8 * j + 7] + terms[8 * j + 7 : 8 * j + 8])
        corr = products[-1] / BATCH
        miss = 1.0 - corr
        loss = loss + miss * miss - off_weight * corr * corr
    sums.append(jnp.concatenate([loss, jnp.zeros((1, 768), f32)], axis=1))
    pair = [jnp.concatenate([terms[8 * j + 2 : 8 * j + 3] for j in range(4)], axis=1), jnp.concatenate(products, axis=1)]
    for half in range(2):
        sums += [jnp.where(ids[1] == half, x, 0.0) for x in pair]
    sums.append(jnp.zeros((1, 1024), f32))
    for j in range(8):
        out[j : j + 1, :] = sums[j]


def first_view(ids, last, blocks):
    out = [
        jax.ShapeDtypeStruct((128, 1024), f32),
        jax.ShapeDtypeStruct((128, 1024), bf16),
        jax.ShapeDtypeStruct((8, 1024), f32),
        jax.ShapeDtypeStruct((32, 256), f32),
    ]
    return call(first_kernel, out, 1, "first_view", flops=1 << 20)(ids, last, *blocks)


def finish(up, up_norm, partner, partner_norm, count):
    corr = partner_norm / count
    diag = -2.0 * (1.0 - corr) - 2.0 * off_weight * corr
    return diag, (up + diag * partner) / count, (up_norm + diag * partner_norm) / count


def vmem_call(kernel, out_shape, args, name, flops):
    vmem = pl.BlockSpec(memory_space=pltpu.VMEM)
    smem = pl.BlockSpec(memory_space=pltpu.SMEM)
    return pl.pallas_call(
        kernel,
        out_shape=out_shape,
        in_specs=[smem] + [vmem] * (len(args) - 1),
        out_specs=jax.tree.map(lambda _: vmem, out_shape),
        compiler_params=pltpu.CompilerParams(vmem_limit_bytes=14 * 1024 * 1024),
        cost_estimate=pl.CostEstimate(flops=flops, bytes_accessed=1 << 16, transcendentals=0),
        name=name,
    )(*args)


def partner_kernel(ids, other, half, out):
    other = other[...].astype(f32)
    out[0:1, :] = image_sum(other)
    out[1:2, :] = image_sum(other * half[...].astype(f32))


def arrange_kernel(which, ids, same, other, out):
    for half in range(2):
        picked = jnp.where(ids[which] == half, same[...].astype(out.dtype), other[...].astype(out.dtype))
        out[:, 1024 * half : 1024 * (half + 1)] = picked


def finish_second_kernel(ids, terms, scales, view, up, partner, grad):
    for part in range(4):
        columns = slice(256 * part, 256 * (part + 1))
        rows = [terms[8 * part + i : 8 * part + i + 1] for i in range(8)]
        diag, first, second = finish(rows[0], rows[4] + rows[5], rows[1], rows[6] + rows[7], BATCH)
        mean, inv = scales[0:1, columns], scales[1:2, columns]
        norm = (view[:, columns] - mean) * inv
        grad[:, columns] = inv * (up[:, columns] + diag * partner[:, columns].astype(f32) - first - norm * second)


def finish_kernel(ids, sums, scales, view, up, block, grad, loss):
    row = ids[2]
    loss[0, 0] = jnp.sum(sums[:, 2, :]) / FEAT
    partner = sums[row]
    for half in range(2):
        columns = slice(1024 * half, 1024 * (half + 1))
        total = sums[4 * half] + sums[4 * half + 1] + sums[4 * half + 2] + sums[4 * half + 3]
        rows = [partner[3 + 2 * half : 4 + 2 * half], partner[4 + 2 * half : 5 + 2 * half]]
        diag, first, second = finish(total[0:1], total[1:2], *rows, BATCH)
        mean, inv = scales[0:1, columns], scales[1:2, columns]
        norm = (view[:, columns] - mean) * inv
        grad[:, columns] = inv * (up[:, columns] + diag * block[:, columns].astype(f32) - first - norm * second)


def finish_first(ids, *args):
    vmem = pl.BlockSpec(memory_space=pltpu.VMEM)
    smem = pl.BlockSpec(memory_space=pltpu.SMEM)
    return pl.pallas_call(
        finish_kernel,
        out_shape=[jax.ShapeDtypeStruct((128, 2048), f32), jax.ShapeDtypeStruct((1, 1), f32)],
        in_specs=[smem] + [vmem] * len(args),
        out_specs=[vmem, smem],
        compiler_params=pltpu.CompilerParams(vmem_limit_bytes=14 * 1024 * 1024),
        cost_estimate=pl.CostEstimate(flops=1 << 20, bytes_accessed=1 << 16, transcendentals=0),
        name="finish_first",
    )(ids, *args)


def row_sum(x):
    x = x + sum(lax.ppermute(x, ("y1", "y0"), [(i, (i + step) % 4) for i in range(4)]) for step in (1, 2, 3))
    return x + lax.ppermute(x, "xh", SWAP)


def local(view_a, view_b):
    count = BATCH
    core = lax.axis_index("k")
    xl = lax.axis_index("xl")
    device = lax.axis_index(ROW + COL)
    pairs_a, wanted_a, pairs_b, wanted_b = crossing_tables()
    ids_a = jnp.concatenate([jnp.stack([lax.axis_index(("z1", "z0")), core]), jnp.array(wanted_a)[device], xl[None]])
    ids_b = jnp.concatenate([jnp.stack([lax.axis_index(("y1", "y0")), lax.axis_index("xh")]), jnp.array(wanted_b)[device], core[None]])

    stats_a, late_b = tie(stats(view_a), view_b)
    norm_a, mean_a, inv_a = finish_stats(jnp.sum(spread(stats_a, COL, 16), axis=0), count, view_a)
    norm_b, mean_b, inv_b = finish_stats(row_sum(stats(late_b)), count, view_b)
    half_a = norm_a.astype(bf16)
    half_b = norm_b.astype(bf16)

    zs, ys = ("z1", "z0"), ("y1", "y0")
    parts_a = jnp.transpose(half_a.reshape(128, 2, 1024), (1, 0, 2))
    own_a = both(xl, pick(parts_a, xl), lax.ppermute(pick(parts_a, 1 - xl), "xl", SWAP), 0)
    near_b = ring_near(half_b, ys)
    other_own_b = trade([half_b], "xh")
    other_near_b = ring_near(other_own_b[0], ys)
    near_a = ring_near(own_a, zs)
    other_own_a = trade([own_a], "k")
    near_a[0], near_a[1], *near_b = tie(*near_a, *near_b, *other_near_b)
    near_b, other_near_b = near_b[:2], near_b[2:]
    far_pairs = [(2 * i + k, 2 * ((i + (3 if k else 1)) % 4) + k) for i in range(4) for k in range(2)]
    far_a = lax.ppermute(jnp.where(core == 0, near_a[0], near_a[1]), zs + ("k",), far_pairs)
    other_near_a = trade(near_a, "k")
    far_b = lax.ppermute(near_b[0], ys, AHEAD)
    other_far_b = lax.ppermute(other_near_b[1], ys, BACK)
    other_far_a, far_b, other_far_b = tie(*trade([far_a], "k"), far_b, other_far_b)
    blocks_a = [own_a, *near_a, far_a, *other_own_a, *other_near_a, other_far_a]

    part_a, send_a = gram_part(True, ids_a, blocks_a)
    send_a, far_b, other_far_b = tie(send_a, far_b, other_far_b)
    blocks_b = [half_b, *near_b, far_b, *other_own_b, *other_near_b, other_far_b]
    other_a = lax.ppermute(send_a.reshape(256, 1024), ROW + COL, pairs_a)
    piece_a = lax.all_to_all(part_a.reshape(16, 256, 128), ("y1", "y0", "xh", "xl"), 0, 0)
    mine_b, give_b, *send_b = gram_part(False, ids_b, blocks_b)
    mixed = blend(mine_b, lax.ppermute(give_b, "k", SWAP), piece_a)
    ids = jnp.stack([xl, core, lax.axis_index(ROW)])
    partner = vmem_call(partner_kernel, jax.ShapeDtypeStruct((2, 1024), f32), (ids, other_a, half_b), "partner", 1 << 34)
    early = lax.ppermute(send_b[0], ROW + COL, pairs_b[0])
    mixed, partner, early = tie(mixed, partner, early)
    mixed = lax.all_to_all(mixed, ("xl", "z1", "z0"), 0, 0)

    traded = lax.ppermute(mixed[:, 128:], "k", SWAP)
    up_b, last = second_view(ids_b, mixed, traded, partner, blocks_b)
    last = lax.all_to_all(last, ("y1", "y0", "xh", "xl"), 0, 0)
    last, late = tie(last, send_b[1])
    late = lax.ppermute(late, ROW + COL, pairs_b[1])

    keep, give, sums_a, sums_b = first_view(ids_a, last, blocks_a)
    traded = lax.ppermute(give, "xl", SWAP)
    block = jax.ShapeDtypeStruct((128, 2048), bf16)
    block = vmem_call(functools.partial(arrange_kernel, 1), block, (ids, early, late), "arrange_block", 1 << 34)
    keep, block = tie(keep, block)
    up_own = jax.ShapeDtypeStruct((128, 2048), f32)
    up_own = vmem_call(functools.partial(arrange_kernel, 0), up_own, (ids, keep, traded), "arrange_up", 1 << 33)
    sums_a, sums_b = tie(sums_a + lax.ppermute(sums_a, "k", SWAP), sums_b)
    sums_a = spread(sums_a, ("xl", "z1", "z0"), 8)

    args = (ids, sums_b, jnp.stack([mean_b, inv_b]), view_b, up_b, other_a)
    grad_b = vmem_call(finish_second_kernel, jax.ShapeDtypeStruct((256, 1024), f32), args, "finish_second", 1 << 20)
    grad_a, loss_value = finish_first(ids, sums_a, jnp.stack([mean_a, inv_a]), view_a, up_own, block)
    return (loss_value[0, 0], grad_a, grad_b)


def solution(mesh):
    fine = Mesh(mesh.devices.reshape((2,) * 7), NAMES)
    return jax.shard_map(
        local,
        mesh=fine,
        in_specs=(P(COL, ROW), P(ROW, COL)),
        out_specs=(P(), P(COL, ROW), P(ROW, COL)),
        check_vma=False,
    )
```

```python
import functools

import jax
import jax.numpy as jnp
from jax import lax
from jax.experimental import pallas as pl
from jax.experimental.pallas import tpu as pltpu
from jax.sharding import Mesh, PartitionSpec as P

FEAT = 16384
BATCH = 2048

off_weight = 0.0051
eps_value = 1e-05

f32 = jnp.float32
bf16 = jnp.bfloat16

NAMES = ("y1", "y0", "xh", "xl", "z1", "z0", "k")
ROW = ("y1", "y0", "xh")
COL = ("xl", "z1", "z0", "k")
SWAP = [(0, 1), (1, 0)]
AHEAD = [(i, (i + 1) % 4) for i in range(4)]
BACK = [(i, (i + 3) % 4) for i in range(4)]


TURN_A = (((0, 1, 0), (1, 0, 0), (1, 0, 1)), ((0, 1, 0, 1), (1, 1, 1, 0), (0, 1, 0, 1)))
TURN_B = ((((0, 0, 1), (0, 1, 0), (1, 0, 0)), ((0, 1, 1, 1), (1, 0, 1, 1), (1, 0, 1, 0))),) * 2


def spread(x, axes, n):
    return lax.all_to_all(jnp.broadcast_to(x[None], (n,) + x.shape), axes, 0, 0)


def bits(n):
    return [(n >> s) & 1 for s in range(6, -1, -1)]


def number(p):
    return sum(v << s for v, s in zip(p, range(6, -1, -1)))


def turned(first, second, rows):
    matrix, shift = rows
    out = []
    for m, v in zip(matrix, shift):
        out.append((sum(a * b for a, b in zip(m, first)) + sum(a * b for a, b in zip(v, second))) % 2)
    return out


def crossing_tables():
    pairs_a, wanted_a = [], [[0, 0, 0]] * 128
    pairs_b, wanted_b = [[], []], [[0] * 8 for _ in range(128)]
    for target in range(128):
        y1, y0, xh, xl, z1, z0, k = bits(target)
        g = turned((y1, y0, xh), (xl, z1, z0, k), TURN_A)
        source = number((xl, z1, z0, k, g[0], g[1], g[2]))
        pairs_a.append((source, target))
        wanted_a[source] = [y0, xh, y1]
        for step in range(2):
            g = turned((xl, z1, z0), (y1, y0, xh, k), TURN_B[step])
            source = number((g[0], g[1], g[2], y1, y0, xh, k ^ step))
            pairs_b[step].append((source, target))
            wanted_b[source][4 * step : 4 * step + 4] = [xl, z1, z0, k]
    return pairs_a, wanted_a, pairs_b, wanted_b


def finish_stats(sums, count, view):
    mean = sums[0] / count
    inv = lax.rsqrt(sums[1] / count - mean * mean + eps_value)
    return ((view - mean) * inv, mean, inv)


def stats(view):
    return jnp.stack([jnp.sum(view, axis=0), jnp.sum(view * view, axis=0)])


def dot(x, y, dims):
    return lax.dot_general(x, y, (dims, ((), ())), preferred_element_type=f32)


def pick(x, index):
    return lax.dynamic_index_in_dim(x, index, 0, keepdims=False)


def both(which, mine, other, axis):
    return jnp.concatenate([jnp.where(which == 0, mine, other), jnp.where(which == 0, other, mine)], axis=axis)


def tie(*xs):
    return lax.optimization_barrier(xs)


def ring_near(own, ring):
    return [lax.ppermute(own, ring, AHEAD), lax.ppermute(own, ring, BACK)]


def trade(blocks, axis):
    return [lax.ppermute(x, axis, SWAP) for x in blocks]


OFFSETS = (0, 3, 1, 2)


def places(ids):
    return [((ids[0] + offset) & 3, ids[1] ^ flip) for flip in range(2) for offset in OFFSETS]


def gram_kernel(first, ids, *refs):
    if first:
        out, send, held, sems = refs[8:]
    else:
        mine, give, *sends, held, sems = refs[8:]
    copies = []
    for i, ref in enumerate(refs[:8]):
        slot = held.at[i // 4, pl.ds(256 * (i % 4), 256), :]
        copies.append(pltpu.make_async_copy(ref, slot, sems.at[i]))
        copies[-1].start()
    copies[0].wait()
    own = held[0, 0:256, :].T
    for flip in range(2):
        for index in range(4 * flip, 4 * flip + 4):
            if index:
                copies[index].wait()
        prod = dot(held[flip], own, ((1,), (0,))).astype(bf16)
        for index in range(4 * flip, 4 * flip + 4):
            p, k = places(ids)[index]
            high, low = p >> 1, p & 1
            for s in range(2):
                at = 256 * (index % 4) + 128 * s
                part = prod[at : at + 128]
                if first:
                    rows = pl.ds(pl.multiple_of(128 * k, 128), 128)
                    for half in range(2):
                        out[2 * (2 * s + high) + low, half, rows, :] = part[:, 128 * half : 128 * (half + 1)]
                    wanted = (high == ids[2]) & (low == ids[3]) & (s == ids[4])

                    @pl.when(wanted)
                    def _():
                        send[k] = held[flip, at : at + 128, :]

                else:

                    @pl.when(ids[10] == s)
                    def _():
                        mine[2 * p + k] = part

                    @pl.when(ids[10] != s)
                    def _():
                        give[2 * p + k] = part

                    for step in range(2):
                        place = [ids[2 + 4 * step + j] for j in range(4)]
                        wanted = (high == place[0]) & (low == place[1]) & (k == place[2]) & (s == place[3])

                        @pl.when(wanted)
                        def _():
                            sends[step][...] = held[flip, at : at + 128, :]


def call(kernel, out_shape, extra, name, space=pltpu.VMEM, scratch=(), flops=2 * 256 * 2048 * 1024):
    vmem = pl.BlockSpec(memory_space=pltpu.VMEM)
    return pl.pallas_call(
        kernel,
        out_shape=out_shape,
        in_specs=[pl.BlockSpec(memory_space=pltpu.SMEM)] + [vmem] * extra + [pl.BlockSpec(memory_space=space)] * 8,
        out_specs=[vmem] * len(out_shape),
        scratch_shapes=list(scratch),
        compiler_params=pltpu.CompilerParams(vmem_limit_bytes=14 * 1024 * 1024),
        cost_estimate=pl.CostEstimate(flops=flops, bytes_accessed=flops >> 8, transcendentals=0),
        name=name,
    )


def gram_part(first, ids, blocks):
    if first:
        shapes = [(8, 2, 256, 128), (2, 128, 1024)]
    else:
        shapes = [(8, 128, 256), (8, 128, 256), (128, 1024), (128, 1024)]
    out = [jax.ShapeDtypeStruct(shape, bf16) for shape in shapes]
    scratch = [pltpu.VMEM((2, 1024, 1024), bf16), pltpu.SemaphoreType.DMA((8,))]
    flops = 2 * 256 * 2048 * 1024 if first else 1 << 20
    return call(functools.partial(gram_kernel, first), out, 0, "gram_part", pl.ANY, scratch, flops)(ids, *blocks)


def blend_kernel(mine, traded, received, out, held_mine, held_traded, held, sems):
    pairs = ((received, held), (mine, held_mine), (traded, held_traded))
    copies = [pltpu.make_async_copy(ref, slot, sems.at[i]) for i, (ref, slot) in enumerate(pairs)]
    for copy in copies:
        copy.start()
    copies[0].wait()
    piece = held[0].astype(f32)
    for i in range(1, 16):
        piece = piece + held[i].astype(f32)
    piece = piece.astype(bf16)
    for copy in copies[1:]:
        copy.wait()
    for i in range(8):
        out[i, 0:128] = (held_mine[i].astype(f32) + held_traded[i].astype(f32)).astype(bf16)
        out[i, 128:256, 0:128] = piece[0:128]
        out[i, 128:256, 128:256] = piece[128:256]


def blend(mine, traded, received):
    return pl.pallas_call(
        blend_kernel,
        out_shape=jax.ShapeDtypeStruct((8, 256, 256), bf16),
        in_specs=[pl.BlockSpec(memory_space=pl.ANY)] * 3,
        out_specs=pl.BlockSpec(memory_space=pltpu.VMEM),
        scratch_shapes=[pltpu.VMEM(x.shape, bf16) for x in (mine, traded, received)] + [pltpu.SemaphoreType.DMA((3,))],
        compiler_params=pltpu.CompilerParams(vmem_limit_bytes=14 * 1024 * 1024),
        cost_estimate=pl.CostEstimate(flops=1 << 20, bytes_accessed=4 << 20, transcendentals=0),
        name="blend",
    )(mine, traded, received)


def apply(part, blocks, ids):
    out = None
    for ref, (p, k) in zip(blocks, places(ids)):
        left = jnp.concatenate([part(p >> 1, p & 1, k, s) for s in range(2)], axis=1)
        prod = dot(left, ref[...], ((1,), (0,)))
        out = prod if out is None else out + prod
    return out * (2.0 * off_weight / BATCH)


def image_sum(x):
    return jnp.sum(x, axis=0, keepdims=True)


def split(x):
    high = x.astype(bf16).astype(f32)
    return [high, x - high]


def second_kernel(ids, mixed, traded, partner, *refs):
    blocks, up, out = refs[:8], refs[8], refs[9]

    def part(high, low, k, s):
        index = 4 * high + 2 * low + k
        rows = jnp.where(ids[10] == s, mixed[index, 128:256, :], traded[index])
        return jnp.concatenate([rows[:, 0:128], rows[:, 128:256]], axis=0)

    piece = mixed[0, 0:128].astype(f32)
    for i in range(1, 8):
        piece = piece + mixed[i, 0:128].astype(f32)
    piece = piece.astype(bf16)
    for i in range(16):
        out[i, 0:128] = piece
    value = apply(part, blocks, ids)
    up[...] = value
    norm = blocks[0][...].astype(f32)
    sums = [image_sum(value), partner[0:1], image_sum(norm), jnp.zeros((1, 1024), f32)]
    sums += split(image_sum(value * norm)) + split(partner[1:2])
    row = lax.broadcasted_iota(jnp.int32, (8, 1024), 0)
    rows = jnp.zeros((8, 1024), f32)
    for i in range(8):
        rows = jnp.where(row == i, sums[i], rows)
    rows = jnp.concatenate([rows[:, 256 * i : 256 * (i + 1)] for i in range(4)], axis=0).astype(bf16)
    for i in range(16):
        out[i, 128:160] = rows


def second_view(ids, mixed, traded, partner, blocks):
    out = [jax.ShapeDtypeStruct((256, 1024), f32), jax.ShapeDtypeStruct((16, 160, 256), bf16)]
    return call(second_kernel, out, 3, "second_view")(ids, mixed, traded, partner, *blocks)


def first_kernel(ids, last, *refs):
    blocks, (keep, give, out, second_sums) = refs[:8], refs[8:]

    def part(high, low, k, s):
        at = pl.ds(pl.multiple_of(k * 128, 128), 128)
        index = 4 * (2 * s + high) + 2 * low
        return jnp.concatenate([last[index, 0:128, at], last[index + 1, 0:128, at]], axis=0)

    value = apply(part, blocks, ids)
    side = ids[5]
    keep[...] = jnp.where(side == 0, value[0:128], value[128:256])
    give[...] = jnp.where(side == 0, value[128:256], value[0:128]).astype(bf16)
    sums = [image_sum(value), image_sum(value * blocks[0][...].astype(f32))]
    terms = None
    for i in range(8):
        term = last[2 * i + side, 128:160].astype(f32)
        terms = term if terms is None else terms + term
    second_sums[...] = terms
    row = lax.broadcasted_iota(jnp.int32, (32, 256), 0) % 8
    loss = image_sum(jnp.where((row == 4) | (row == 5), terms, 0.0)) / (2.0 * BATCH)
    products = []
    for j in range(4):
        products.append(terms[8 * j + 6 : 8 * j + 7] + terms[8 * j + 7 : 8 * j + 8])
        corr = products[-1] / BATCH
        miss = 1.0 - corr
        loss = loss + miss * miss - off_weight * corr * corr
    sums.append(jnp.concatenate([loss, jnp.zeros((1, 768), f32)], axis=1))
    pair = [jnp.concatenate([terms[8 * j + 2 : 8 * j + 3] for j in range(4)], axis=1), jnp.concatenate(products, axis=1)]
    for half in range(2):
        sums += [jnp.where(ids[1] == half, x, 0.0) for x in pair]
    sums.append(jnp.zeros((1, 1024), f32))
    for j in range(8):
        out[j : j + 1, :] = sums[j]


def first_view(ids, last, blocks):
    out = [
        jax.ShapeDtypeStruct((128, 1024), f32),
        jax.ShapeDtypeStruct((128, 1024), bf16),
        jax.ShapeDtypeStruct((8, 1024), f32),
        jax.ShapeDtypeStruct((32, 256), f32),
    ]
    return call(first_kernel, out, 1, "first_view", flops=1 << 20)(ids, last, *blocks)


def finish(up, up_norm, partner, partner_norm, count):
    corr = partner_norm / count
    diag = -2.0 * (1.0 - corr) - 2.0 * off_weight * corr
    return diag, (up + diag * partner) / count, (up_norm + diag * partner_norm) / count


def vmem_call(kernel, out_shape, args, name, flops):
    vmem = pl.BlockSpec(memory_space=pltpu.VMEM)
    smem = pl.BlockSpec(memory_space=pltpu.SMEM)
    return pl.pallas_call(
        kernel,
        out_shape=out_shape,
        in_specs=[smem] + [vmem] * (len(args) - 1),
        out_specs=jax.tree.map(lambda _: vmem, out_shape),
        compiler_params=pltpu.CompilerParams(vmem_limit_bytes=14 * 1024 * 1024),
        cost_estimate=pl.CostEstimate(flops=flops, bytes_accessed=1 << 16, transcendentals=0),
        name=name,
    )(*args)


def partner_kernel(ids, other, half, out):
    other = other[...].astype(f32)
    out[0:1, :] = image_sum(other)
    out[1:2, :] = image_sum(other * half[...].astype(f32))


def arrange_kernel(ids, same, other, block):
    for half in range(2):
        block[:, 1024 * half : 1024 * (half + 1)] = jnp.where(ids[1] == half, same[...], other[...])


def finish_second_kernel(ids, terms, scales, view, up, partner, grad):
    for part in range(4):
        columns = slice(256 * part, 256 * (part + 1))
        rows = [terms[8 * part + i : 8 * part + i + 1] for i in range(8)]
        diag, first, second = finish(rows[0], rows[4] + rows[5], rows[1], rows[6] + rows[7], BATCH)
        mean, inv = scales[0:1, columns], scales[1:2, columns]
        norm = (view[:, columns] - mean) * inv
        grad[:, columns] = inv * (up[:, columns] + diag * partner[:, columns].astype(f32) - first - norm * second)


def finish_kernel(ids, sums, scales, view, keep, traded, block, grad, loss):
    row = ids[2]
    loss[0, 0] = jnp.sum(sums[:, 2, :]) / FEAT
    partner = sums[row]
    for half in range(2):
        columns = slice(1024 * half, 1024 * (half + 1))
        total = sums[4 * half] + sums[4 * half + 1] + sums[4 * half + 2] + sums[4 * half + 3]
        rows = [partner[3 + 2 * half : 4 + 2 * half], partner[4 + 2 * half : 5 + 2 * half]]
        diag, first, second = finish(total[0:1], total[1:2], *rows, BATCH)
        mean, inv = scales[0:1, columns], scales[1:2, columns]
        norm = (view[:, columns] - mean) * inv
        up = jnp.where(ids[0] == half, keep[...], traded[...].astype(f32))
        grad[:, columns] = inv * (up + diag * block[:, columns].astype(f32) - first - norm * second)


def finish_first(ids, *args):
    vmem = pl.BlockSpec(memory_space=pltpu.VMEM)
    smem = pl.BlockSpec(memory_space=pltpu.SMEM)
    return pl.pallas_call(
        finish_kernel,
        out_shape=[jax.ShapeDtypeStruct((128, 2048), f32), jax.ShapeDtypeStruct((1, 1), f32)],
        in_specs=[smem] + [vmem] * len(args),
        out_specs=[vmem, smem],
        compiler_params=pltpu.CompilerParams(vmem_limit_bytes=14 * 1024 * 1024),
        cost_estimate=pl.CostEstimate(flops=1 << 20, bytes_accessed=1 << 16, transcendentals=0),
        name="finish_first",
    )(ids, *args)


def row_sum(x):
    x = x + sum(lax.ppermute(x, ("y1", "y0"), [(i, (i + step) % 4) for i in range(4)]) for step in (1, 2, 3))
    return x + lax.ppermute(x, "xh", SWAP)


def local(view_a, view_b):
    count = BATCH
    core = lax.axis_index("k")
    xl = lax.axis_index("xl")
    device = lax.axis_index(ROW + COL)
    pairs_a, wanted_a, pairs_b, wanted_b = crossing_tables()
    ids_a = jnp.concatenate([jnp.stack([lax.axis_index(("z1", "z0")), core]), jnp.array(wanted_a)[device], xl[None]])
    ids_b = jnp.concatenate([jnp.stack([lax.axis_index(("y1", "y0")), lax.axis_index("xh")]), jnp.array(wanted_b)[device], core[None]])

    stats_a, late_b = tie(stats(view_a), view_b)
    norm_a, mean_a, inv_a = finish_stats(jnp.sum(spread(stats_a, COL, 16), axis=0), count, view_a)
    norm_b, mean_b, inv_b = finish_stats(row_sum(stats(late_b)), count, view_b)
    half_a = norm_a.astype(bf16)
    half_b = norm_b.astype(bf16)

    zs, ys = ("z1", "z0"), ("y1", "y0")
    parts_a = jnp.transpose(half_a.reshape(128, 2, 1024), (1, 0, 2))
    own_a = both(xl, pick(parts_a, xl), lax.ppermute(pick(parts_a, 1 - xl), "xl", SWAP), 0)
    near_b = ring_near(half_b, ys)
    own_a, late_half_b = tie(own_a, half_b)
    near_a = ring_near(own_a, zs)
    other_own_a = trade([own_a], "k")
    other_own_b = trade([late_half_b], "xh")
    *near_a, near_b[0], near_b[1], other_own_b[0] = tie(*near_a, *near_b, *other_own_b)
    far_pairs = [(2 * i + k, 2 * ((i + (3 if k else 1)) % 4) + k) for i in range(4) for k in range(2)]
    far_a = lax.ppermute(jnp.where(core == 0, near_a[0], near_a[1]), zs + ("k",), far_pairs)
    other_near_a = trade(near_a, "k")
    other_near_b = ring_near(other_own_b[0], ys)
    far_b = lax.ppermute(near_b[0], ys, AHEAD)
    other_far_a, *other_near_b = tie(*trade([far_a], "k"), *other_near_b)
    other_far_b = lax.ppermute(other_near_b[1], ys, BACK)
    blocks_a = [own_a, *near_a, far_a, *other_own_a, *other_near_a, other_far_a]

    part_a, send_a = gram_part(True, ids_a, blocks_a)
    send_a, far_b, other_far_b = tie(send_a, far_b, other_far_b)
    blocks_b = [half_b, *near_b, far_b, *other_own_b, *other_near_b, other_far_b]
    other_a = lax.ppermute(send_a.reshape(256, 1024), ROW + COL, pairs_a)
    piece_a = lax.all_to_all(part_a.reshape(16, 256, 128), ("y1", "y0", "xh", "xl"), 0, 0)
    mine_b, give_b, *send_b = gram_part(False, ids_b, blocks_b)
    mixed = blend(mine_b, lax.ppermute(give_b, "k", SWAP), piece_a)
    ids = jnp.stack([xl, core, lax.axis_index(ROW)])
    partner = vmem_call(partner_kernel, jax.ShapeDtypeStruct((2, 1024), f32), (ids, other_a, half_b), "partner", 1 << 34)
    early = lax.ppermute(send_b[0], ROW + COL, pairs_b[0])
    mixed, partner, early = tie(mixed, partner, early)
    mixed = lax.all_to_all(mixed, ("xl", "z1", "z0"), 0, 0)

    traded = lax.ppermute(mixed[:, 128:], "k", SWAP)
    up_b, last = second_view(ids_b, mixed, traded, partner, blocks_b)
    last = lax.all_to_all(last, ("y1", "y0", "xh", "xl"), 0, 0)
    last, late = tie(last, send_b[1])
    late = lax.ppermute(late, ROW + COL, pairs_b[1])

    keep, give, sums_a, sums_b = first_view(ids_a, last, blocks_a)
    traded = lax.ppermute(give, "xl", SWAP)
    block = jax.ShapeDtypeStruct((128, 2048), bf16)
    block = vmem_call(arrange_kernel, block, (ids, early, late), "arrange_block", 1 << 34)
    sums_a, sums_b = tie(sums_a, sums_b)
    sums_a = spread(sums_a + lax.ppermute(sums_a, "k", SWAP), ("xl", "z1", "z0"), 8)

    args = (ids, sums_b, jnp.stack([mean_b, inv_b]), view_b, up_b, other_a)
    grad_b = vmem_call(finish_second_kernel, jax.ShapeDtypeStruct((256, 1024), f32), args, "finish_second", 1 << 20)
    grad_a, loss_value = finish_first(ids, sums_a, jnp.stack([mean_a, inv_a]), view_a, keep, traded, block)
    return (loss_value[0, 0], grad_a, grad_b)


def solution(mesh):
    fine = Mesh(mesh.devices.reshape((2,) * 7), NAMES)
    return jax.shard_map(
        local,
        mesh=fine,
        in_specs=(P(COL, ROW), P(ROW, COL)),
        out_specs=(P(), P(COL, ROW), P(ROW, COL)),
        check_vma=False,
    )
```

```python
import functools

import jax
import jax.numpy as jnp
from jax import lax
from jax.experimental import pallas as pl
from jax.experimental.pallas import tpu as pltpu
from jax.sharding import Mesh, PartitionSpec as P

FEAT = 16384
BATCH = 2048

off_weight = 0.0051
eps_value = 1e-05

f32 = jnp.float32
bf16 = jnp.bfloat16

NAMES = ("y1", "y0", "xh", "xl", "z1", "z0", "k")
ROW = ("y1", "y0", "xh")
COL = ("xl", "z1", "z0", "k")
SWAP = [(0, 1), (1, 0)]
AHEAD = [(i, (i + 1) % 4) for i in range(4)]
BACK = [(i, (i + 3) % 4) for i in range(4)]


TURN_A = (((0, 1, 0), (1, 0, 0), (1, 0, 1)), ((0, 1, 0, 1), (1, 1, 1, 0), (0, 1, 0, 1)))
TURN_B = ((((0, 0, 1), (0, 1, 0), (1, 0, 0)), ((0, 1, 1, 1), (1, 0, 1, 1), (1, 0, 1, 0))),) * 2


def spread(x, axes, n):
    return lax.all_to_all(jnp.broadcast_to(x[None], (n,) + x.shape), axes, 0, 0)


def bits(n):
    return [(n >> s) & 1 for s in range(6, -1, -1)]


def number(p):
    return sum(v << s for v, s in zip(p, range(6, -1, -1)))


def turned(first, second, rows):
    matrix, shift = rows
    out = []
    for m, v in zip(matrix, shift):
        out.append((sum(a * b for a, b in zip(m, first)) + sum(a * b for a, b in zip(v, second))) % 2)
    return out


def crossing_tables():
    pairs_a, wanted_a = [], [[0, 0, 0]] * 128
    pairs_b, wanted_b = [[], []], [[0] * 8 for _ in range(128)]
    for target in range(128):
        y1, y0, xh, xl, z1, z0, k = bits(target)
        g = turned((y1, y0, xh), (xl, z1, z0, k), TURN_A)
        source = number((xl, z1, z0, k, g[0], g[1], g[2]))
        pairs_a.append((source, target))
        wanted_a[source] = [y0, xh, y1]
        for step in range(2):
            g = turned((xl, z1, z0), (y1, y0, xh, k), TURN_B[step])
            source = number((g[0], g[1], g[2], y1, y0, xh, k ^ step))
            pairs_b[step].append((source, target))
            wanted_b[source][4 * step : 4 * step + 4] = [xl, z1, z0, k]
    return pairs_a, wanted_a, pairs_b, wanted_b


def finish_stats(sums, count, view):
    mean = sums[0] / count
    inv = lax.rsqrt(sums[1] / count - mean * mean + eps_value)
    return ((view - mean) * inv, mean, inv)


def stats(view):
    return jnp.stack([jnp.sum(view, axis=0), jnp.sum(view * view, axis=0)])


def dot(x, y, dims):
    return lax.dot_general(x, y, (dims, ((), ())), preferred_element_type=f32)


def pick(x, index):
    return lax.dynamic_index_in_dim(x, index, 0, keepdims=False)


def both(which, mine, other, axis):
    return jnp.concatenate([jnp.where(which == 0, mine, other), jnp.where(which == 0, other, mine)], axis=axis)


def tie(*xs):
    return lax.optimization_barrier(xs)


def ring_near(own, ring):
    return [lax.ppermute(own, ring, AHEAD), lax.ppermute(own, ring, BACK)]


def trade(blocks, axis):
    return [lax.ppermute(x, axis, SWAP) for x in blocks]


OFFSETS = (0, 3, 1, 2)


def places(ids):
    return [((ids[0] + offset) & 3, ids[1] ^ flip) for flip in range(2) for offset in OFFSETS]


def gram_kernel(first, ids, *refs):
    if first:
        out, send, held, sems = refs[8:]
    else:
        mine, give, *sends, held, sems = refs[8:]
    copies = []
    for i, ref in enumerate(refs[:8]):
        slot = held.at[i // 4, pl.ds(256 * (i % 4), 256), :]
        copies.append(pltpu.make_async_copy(ref, slot, sems.at[i]))
        copies[-1].start()
    copies[0].wait()
    own = held[0, 0:256, :].T
    for flip in range(2):
        for index in range(4 * flip, 4 * flip + 4):
            if index:
                copies[index].wait()
        prod = dot(held[flip], own, ((1,), (0,))).astype(bf16)
        for index in range(4 * flip, 4 * flip + 4):
            p, k = places(ids)[index]
            high, low = p >> 1, p & 1
            for s in range(2):
                at = 256 * (index % 4) + 128 * s
                part = prod[at : at + 128]
                if first:
                    rows = pl.ds(pl.multiple_of(128 * k, 128), 128)
                    for half in range(2):
                        out[2 * (2 * s + high) + low, half, rows, :] = part[:, 128 * half : 128 * (half + 1)]
                    wanted = (high == ids[2]) & (low == ids[3]) & (s == ids[4])

                    @pl.when(wanted)
                    def _():
                        send[k] = held[flip, at : at + 128, :]

                else:

                    @pl.when(ids[10] == s)
                    def _():
                        mine[2 * p + k] = part

                    @pl.when(ids[10] != s)
                    def _():
                        give[2 * p + k] = part

                    for step in range(2):
                        place = [ids[2 + 4 * step + j] for j in range(4)]
                        wanted = (high == place[0]) & (low == place[1]) & (k == place[2]) & (s == place[3])

                        @pl.when(wanted)
                        def _():
                            sends[step][...] = held[flip, at : at + 128, :]


def call(kernel, out_shape, extra, name, space=pltpu.VMEM, scratch=(), flops=2 * 256 * 2048 * 1024):
    vmem = pl.BlockSpec(memory_space=pltpu.VMEM)
    return pl.pallas_call(
        kernel,
        out_shape=out_shape,
        in_specs=[pl.BlockSpec(memory_space=pltpu.SMEM)] + [vmem] * extra + [pl.BlockSpec(memory_space=space)] * 8,
        out_specs=[vmem] * len(out_shape),
        scratch_shapes=list(scratch),
        compiler_params=pltpu.CompilerParams(vmem_limit_bytes=14 * 1024 * 1024),
        cost_estimate=pl.CostEstimate(flops=flops, bytes_accessed=flops >> 8, transcendentals=0),
        name=name,
    )


def gram_part(first, ids, blocks):
    if first:
        shapes = [(8, 2, 256, 128), (2, 128, 1024)]
    else:
        shapes = [(8, 128, 256), (8, 128, 256), (128, 1024), (128, 1024)]
    out = [jax.ShapeDtypeStruct(shape, bf16) for shape in shapes]
    scratch = [pltpu.VMEM((2, 1024, 1024), bf16), pltpu.SemaphoreType.DMA((8,))]
    flops = 2 * 256 * 2048 * 1024 if first else 1 << 20
    return call(functools.partial(gram_kernel, first), out, 0, "gram_part", pl.ANY, scratch, flops)(ids, *blocks)


def blend_kernel(mine, traded, received, out, held_mine, held_traded, held, sems):
    pairs = ((received, held), (mine, held_mine), (traded, held_traded))
    copies = [pltpu.make_async_copy(ref, slot, sems.at[i]) for i, (ref, slot) in enumerate(pairs)]
    for copy in copies:
        copy.start()
    copies[0].wait()
    piece = held[0].astype(f32)
    for i in range(1, 16):
        piece = piece + held[i].astype(f32)
    piece = piece.astype(bf16)
    for copy in copies[1:]:
        copy.wait()
    for i in range(8):
        out[i, 0:128] = (held_mine[i].astype(f32) + held_traded[i].astype(f32)).astype(bf16)
        out[i, 128:256, 0:128] = piece[0:128]
        out[i, 128:256, 128:256] = piece[128:256]


def blend(mine, traded, received):
    return pl.pallas_call(
        blend_kernel,
        out_shape=jax.ShapeDtypeStruct((8, 256, 256), bf16),
        in_specs=[pl.BlockSpec(memory_space=pl.ANY)] * 3,
        out_specs=pl.BlockSpec(memory_space=pltpu.VMEM),
        scratch_shapes=[pltpu.VMEM(x.shape, bf16) for x in (mine, traded, received)] + [pltpu.SemaphoreType.DMA((3,))],
        compiler_params=pltpu.CompilerParams(vmem_limit_bytes=14 * 1024 * 1024),
        cost_estimate=pl.CostEstimate(flops=1 << 20, bytes_accessed=4 << 20, transcendentals=0),
        name="blend",
    )(mine, traded, received)


def apply(part, blocks, ids):
    out = None
    for ref, (p, k) in zip(blocks, places(ids)):
        left = jnp.concatenate([part(p >> 1, p & 1, k, s) for s in range(2)], axis=1)
        prod = dot(left, ref[...], ((1,), (0,)))
        out = prod if out is None else out + prod
    return out * (2.0 * off_weight / BATCH)


def image_sum(x):
    return jnp.sum(x, axis=0, keepdims=True)


def split(x):
    high = x.astype(bf16).astype(f32)
    return [high, x - high]


def second_kernel(ids, mixed, traded, partner, *refs):
    blocks, up, out = refs[:8], refs[8], refs[9]

    def part(high, low, k, s):
        index = 4 * high + 2 * low + k
        rows = jnp.where(ids[10] == s, mixed[index, 128:256, :], traded[index])
        return jnp.concatenate([rows[:, 0:128], rows[:, 128:256]], axis=0)

    piece = mixed[0, 0:128].astype(f32)
    for i in range(1, 8):
        piece = piece + mixed[i, 0:128].astype(f32)
    piece = piece.astype(bf16)
    for i in range(16):
        out[i, 0:128] = piece
    value = apply(part, blocks, ids)
    up[...] = value
    norm = blocks[0][...].astype(f32)
    sums = [image_sum(value), partner[0:1], image_sum(norm), jnp.zeros((1, 1024), f32)]
    sums += split(image_sum(value * norm)) + split(partner[1:2])
    row = lax.broadcasted_iota(jnp.int32, (8, 1024), 0)
    rows = jnp.zeros((8, 1024), f32)
    for i in range(8):
        rows = jnp.where(row == i, sums[i], rows)
    rows = jnp.concatenate([rows[:, 256 * i : 256 * (i + 1)] for i in range(4)], axis=0).astype(bf16)
    for i in range(16):
        out[i, 128:160] = rows


def second_view(ids, mixed, traded, partner, blocks):
    out = [jax.ShapeDtypeStruct((256, 1024), f32), jax.ShapeDtypeStruct((16, 160, 256), bf16)]
    return call(second_kernel, out, 3, "second_view")(ids, mixed, traded, partner, *blocks)


def first_kernel(ids, last, *refs):
    blocks, (keep, give, out, second_sums) = refs[:8], refs[8:]

    def part(high, low, k, s):
        at = pl.ds(pl.multiple_of(k * 128, 128), 128)
        index = 4 * (2 * s + high) + 2 * low
        return jnp.concatenate([last[index, 0:128, at], last[index + 1, 0:128, at]], axis=0)

    value = apply(part, blocks, ids)
    side = ids[5]
    keep[...] = jnp.where(side == 0, value[0:128], value[128:256])
    give[...] = jnp.where(side == 0, value[128:256], value[0:128]).astype(bf16)
    sums = [image_sum(value), image_sum(value * blocks[0][...].astype(f32))]
    terms = None
    for i in range(8):
        term = last[2 * i + side, 128:160].astype(f32)
        terms = term if terms is None else terms + term
    second_sums[...] = terms
    row = lax.broadcasted_iota(jnp.int32, (32, 256), 0) % 8
    loss = image_sum(jnp.where((row == 4) | (row == 5), terms, 0.0)) / (2.0 * BATCH)
    products = []
    for j in range(4):
        products.append(terms[8 * j + 6 : 8 * j + 7] + terms[8 * j + 7 : 8 * j + 8])
        corr = products[-1] / BATCH
        miss = 1.0 - corr
        loss = loss + miss * miss - off_weight * corr * corr
    sums.append(jnp.concatenate([loss, jnp.zeros((1, 768), f32)], axis=1))
    pair = [jnp.concatenate([terms[8 * j + 2 : 8 * j + 3] for j in range(4)], axis=1), jnp.concatenate(products, axis=1)]
    for half in range(2):
        sums += [jnp.where(ids[1] == half, x, 0.0) for x in pair]
    sums.append(jnp.zeros((1, 1024), f32))
    for j in range(8):
        out[j : j + 1, :] = sums[j]


def first_view(ids, last, blocks):
    out = [
        jax.ShapeDtypeStruct((128, 1024), f32),
        jax.ShapeDtypeStruct((128, 1024), bf16),
        jax.ShapeDtypeStruct((8, 1024), f32),
        jax.ShapeDtypeStruct((32, 256), f32),
    ]
    return call(first_kernel, out, 1, "first_view", flops=1 << 20)(ids, last, *blocks)


def finish(up, up_norm, partner, partner_norm, count):
    corr = partner_norm / count
    diag = -2.0 * (1.0 - corr) - 2.0 * off_weight * corr
    return diag, (up + diag * partner) / count, (up_norm + diag * partner_norm) / count


def vmem_call(kernel, out_shape, args, name, flops):
    vmem = pl.BlockSpec(memory_space=pltpu.VMEM)
    smem = pl.BlockSpec(memory_space=pltpu.SMEM)
    return pl.pallas_call(
        kernel,
        out_shape=out_shape,
        in_specs=[smem] + [vmem] * (len(args) - 1),
        out_specs=jax.tree.map(lambda _: vmem, out_shape),
        compiler_params=pltpu.CompilerParams(vmem_limit_bytes=14 * 1024 * 1024),
        cost_estimate=pl.CostEstimate(flops=flops, bytes_accessed=1 << 16, transcendentals=0),
        name=name,
    )(*args)


def partner_kernel(ids, other, half, out):
    other = other[...].astype(f32)
    out[0:1, :] = image_sum(other)
    out[1:2, :] = image_sum(other * half[...].astype(f32))


def arrange_kernel(which, ids, same, other, out):
    for half in range(2):
        picked = jnp.where(ids[which] == half, same[...].astype(out.dtype), other[...].astype(out.dtype))
        out[:, 1024 * half : 1024 * (half + 1)] = picked


def finish_second_kernel(ids, terms, scales, view, up, partner, grad):
    for part in range(4):
        columns = slice(256 * part, 256 * (part + 1))
        rows = [terms[8 * part + i : 8 * part + i + 1] for i in range(8)]
        diag, first, second = finish(rows[0], rows[4] + rows[5], rows[1], rows[6] + rows[7], BATCH)
        mean, inv = scales[0:1, columns], scales[1:2, columns]
        norm = (view[:, columns] - mean) * inv
        grad[:, columns] = inv * (up[:, columns] + diag * partner[:, columns].astype(f32) - first - norm * second)


def finish_kernel(ids, sums, scales, view, up, block, grad, loss):
    row = ids[2]
    loss[0, 0] = jnp.sum(sums[:, 2, :]) / FEAT
    partner = sums[row]
    for half in range(2):
        columns = slice(1024 * half, 1024 * (half + 1))
        total = sums[4 * half] + sums[4 * half + 1] + sums[4 * half + 2] + sums[4 * half + 3]
        rows = [partner[3 + 2 * half : 4 + 2 * half], partner[4 + 2 * half : 5 + 2 * half]]
        diag, first, second = finish(total[0:1], total[1:2], *rows, BATCH)
        mean, inv = scales[0:1, columns], scales[1:2, columns]
        norm = (view[:, columns] - mean) * inv
        grad[:, columns] = inv * (up[:, columns] + diag * block[:, columns].astype(f32) - first - norm * second)


def finish_first(ids, *args):
    vmem = pl.BlockSpec(memory_space=pltpu.VMEM)
    smem = pl.BlockSpec(memory_space=pltpu.SMEM)
    return pl.pallas_call(
        finish_kernel,
        out_shape=[jax.ShapeDtypeStruct((128, 2048), f32), jax.ShapeDtypeStruct((1, 1), f32)],
        in_specs=[smem] + [vmem] * len(args),
        out_specs=[vmem, smem],
        compiler_params=pltpu.CompilerParams(vmem_limit_bytes=14 * 1024 * 1024),
        cost_estimate=pl.CostEstimate(flops=1 << 20, bytes_accessed=1 << 16, transcendentals=0),
        name="finish_first",
    )(ids, *args)


def row_sum(x):
    x = x + sum(lax.ppermute(x, ("y1", "y0"), [(i, (i + step) % 4) for i in range(4)]) for step in (1, 2, 3))
    return x + lax.ppermute(x, "xh", SWAP)


def local(view_a, view_b):
    count = BATCH
    core = lax.axis_index("k")
    xl = lax.axis_index("xl")
    device = lax.axis_index(ROW + COL)
    pairs_a, wanted_a, pairs_b, wanted_b = crossing_tables()
    ids_a = jnp.concatenate([jnp.stack([lax.axis_index(("z1", "z0")), core]), jnp.array(wanted_a)[device], xl[None]])
    ids_b = jnp.concatenate([jnp.stack([lax.axis_index(("y1", "y0")), lax.axis_index("xh")]), jnp.array(wanted_b)[device], core[None]])

    stats_a, late_b = tie(stats(view_a), view_b)
    norm_a, mean_a, inv_a = finish_stats(jnp.sum(spread(stats_a, COL, 16), axis=0), count, view_a)
    norm_b, mean_b, inv_b = finish_stats(row_sum(stats(late_b)), count, view_b)
    half_a = norm_a.astype(bf16)
    half_b = norm_b.astype(bf16)

    zs, ys = ("z1", "z0"), ("y1", "y0")
    parts_a = jnp.transpose(half_a.reshape(128, 2, 1024), (1, 0, 2))
    own_a = both(xl, pick(parts_a, xl), lax.ppermute(pick(parts_a, 1 - xl), "xl", SWAP), 0)
    near_b = ring_near(half_b, ys)
    own_a, late_half_b = tie(own_a, half_b)
    near_a = ring_near(own_a, zs)
    other_own_a = trade([own_a], "k")
    other_own_b = trade([late_half_b], "xh")
    *near_a, near_b[0], near_b[1], other_own_b[0] = tie(*near_a, *near_b, *other_own_b)
    far_pairs = [(2 * i + k, 2 * ((i + (3 if k else 1)) % 4) + k) for i in range(4) for k in range(2)]
    far_a = lax.ppermute(jnp.where(core == 0, near_a[0], near_a[1]), zs + ("k",), far_pairs)
    other_near_a = trade(near_a, "k")
    other_near_b = ring_near(other_own_b[0], ys)
    far_b = lax.ppermute(near_b[0], ys, AHEAD)
    other_far_a, *other_near_b = tie(*trade([far_a], "k"), *other_near_b)
    other_far_b = lax.ppermute(other_near_b[1], ys, BACK)
    blocks_a = [own_a, *near_a, far_a, *other_own_a, *other_near_a, other_far_a]

    part_a, send_a = gram_part(True, ids_a, blocks_a)
    send_a, far_b, other_far_b = tie(send_a, far_b, other_far_b)
    blocks_b = [half_b, *near_b, far_b, *other_own_b, *other_near_b, other_far_b]
    other_a = lax.ppermute(send_a.reshape(256, 1024), ROW + COL, pairs_a)
    piece_a = lax.all_to_all(part_a.reshape(16, 256, 128), ("y1", "y0", "xh", "xl"), 0, 0)
    mine_b, give_b, *send_b = gram_part(False, ids_b, blocks_b)
    mixed = blend(mine_b, lax.ppermute(give_b, "k", SWAP), piece_a)
    ids = jnp.stack([xl, core, lax.axis_index(ROW)])
    partner = vmem_call(partner_kernel, jax.ShapeDtypeStruct((2, 1024), f32), (ids, other_a, half_b), "partner", 1 << 34)
    early = lax.ppermute(send_b[0], ROW + COL, pairs_b[0])
    mixed, partner, early = tie(mixed, partner, early)
    mixed = lax.all_to_all(mixed, ("xl", "z1", "z0"), 0, 0)

    traded = lax.ppermute(mixed[:, 128:], "k", SWAP)
    up_b, last = second_view(ids_b, mixed, traded, partner, blocks_b)
    last = lax.all_to_all(last, ("y1", "y0", "xh", "xl"), 0, 0)
    last, late = tie(last, send_b[1])
    late = lax.ppermute(late, ROW + COL, pairs_b[1])

    keep, give, sums_a, sums_b = first_view(ids_a, last, blocks_a)
    traded = lax.ppermute(give, "xl", SWAP)
    block = jax.ShapeDtypeStruct((128, 2048), bf16)
    block = vmem_call(functools.partial(arrange_kernel, 1), block, (ids, early, late), "arrange_block", 1 << 34)
    keep, block = tie(keep, block)
    up_own = jax.ShapeDtypeStruct((128, 2048), f32)
    up_own = vmem_call(functools.partial(arrange_kernel, 0), up_own, (ids, keep, traded), "arrange_up", 1 << 33)
    sums_a, sums_b = tie(sums_a + lax.ppermute(sums_a, "k", SWAP), sums_b)
    sums_a = spread(sums_a, ("xl", "z1", "z0"), 8)

    args = (ids, sums_b, jnp.stack([mean_b, inv_b]), view_b, up_b, other_a)
    grad_b = vmem_call(finish_second_kernel, jax.ShapeDtypeStruct((256, 1024), f32), args, "finish_second", 1 << 20)
    grad_a, loss_value = finish_first(ids, sums_a, jnp.stack([mean_a, inv_a]), view_a, up_own, block)
    return (loss_value[0, 0], grad_a, grad_b)


def solution(mesh):
    fine = Mesh(mesh.devices.reshape((2,) * 7), NAMES)
    return jax.shard_map(
        local,
        mesh=fine,
        in_specs=(P(COL, ROW), P(ROW, COL)),
        out_specs=(P(), P(COL, ROW), P(ROW, COL)),
        check_vma=False,
    )
```
